128 devices in a mesh: segment: 8 (over y, core), band: 16 (over x, z).
Axes of the slice: x: 4, y: 4, z: 4, core: 2. Of those that a mesh axis runs over, the one named last changes fastest.
Arguments:
- tokens: bfloat16 [8, 128, 128, 1536], P('segment', 'band'), may hold values from -6 to 6
- in_gain: float32 [8, 1536], P('segment'), may hold values from 0.1 to 1.9
- w_xbc: bfloat16 [8, 1536, 1664], P('segment'), may hold values from -0.15625 to 0.15625
- w_gate: bfloat16 [8, 1536, 1536], P('segment'), may hold values from -0.15625 to 0.15625
- w_dt: bfloat16 [8, 1536, 24], P('segment'), may hold values from -0.078125 to 0.078125
- dt_bias: float32 [8, 24], P('segment'), may hold values from -1 to 1
- decay_rate: float32 [8, 24], P('segment'), may hold values from 6.1035156e-06 to 0.1, as said below
- conv_w: float32 [8, 9, 1664], P('segment'), may hold values from -2 to 2
- conv_bias: float32 [8, 1664], P('segment'), may hold values from -0.5 to 0.5
- skip: float32 [8, 24], P('segment'), may hold values from 0.5 to 1.5
- out_gain: float32 [8, 1536], P('segment'), may hold values from 0.1 to 1.9
- w_out: bfloat16 [8, 1536, 1536], P('segment'), may hold values from -0.15625 to 0.15625
Outputs:
- handed: bfloat16 [8, 128, 128, 1536], P('segment', 'band')
The draws below stay inside these ranges and needn't reach their ends.
Inputs may be any that keep to these rules, and one draw needn't show every extreme that they name: `decay_rate`: positive rates per head, differing between heads and sections.
All inputs are finite; a program needn't handle non-finite values.
Results may differ from the reference program's by a relative error of at most 0.015.
Values may be sent and summed in bfloat16 or wider, within the bound.
No kernel may reach another device: no remote copies, remote signals or barrier semaphores. Data moves between devices by JAX's collectives and lax.ppermute only.
A program may use at most 192 MiB of HBM per device.

```python
import math
import jax
import jax.numpy as jnp
from jax import lax

D = 1536
HEADS = 24
BLOCK = 128
INNER = 1536
XBC = 1664
GRID = 128
N_SEGMENT = 8


def draw_decay_rate(key, part):
    key = jax.random.fold_in(key, 11)
    key_pick, key_slow, key_fast = jax.random.split(key, 3)
    share = 0.5
    picked = jax.random.uniform(key_pick, (N_SEGMENT, HEADS), jnp.float32) < share
    slow = jnp.exp(jax.random.uniform(key_slow, (N_SEGMENT, HEADS), jnp.float32, math.log(0.1), math.log(1.0))) / (GRID * GRID)
    quick = jnp.exp(jax.random.uniform(key_fast, (N_SEGMENT, HEADS), jnp.float32, math.log(0.02), math.log(0.1)))
    return jnp.where(picked, quick, slow).astype(jnp.float32)


def block_scale(stream_key, dims, cuts, low, top_value):
    loudness = 1.0
    for dim, blocks in cuts:
        heights = jax.random.uniform(jax.random.fold_in(jax.random.fold_in(stream_key, 6), dim), (blocks,), jnp.float32, low / len(cuts), top_value / len(cuts))
        loudness = loudness * jnp.repeat(jnp.exp(heights), dims[dim] // blocks).reshape((-1,) + (1,) * (len(dims) - 1 - dim))
    return loudness


def bell_draw(stream_key, dims, scale, most, shards=(), dtype=jnp.bfloat16):
    values = jax.random.normal(stream_key, dims, jnp.float32) * scale
    if len(shards) > 0:
        values = block_scale(stream_key, dims, shards, -0.22, 0.18) * values
    return jnp.clip(values, min=-most, max=most).astype(dtype)


def setup_inputs(seed: int = 0) -> dict:
    arg_keys = jax.random.split(jax.random.key(seed), 13)
    return {
        "tokens": bell_draw(arg_keys[0], (N_SEGMENT, GRID, GRID, D), 1.0, 6.0, ((0, 8), (1, 16))),
        "in_gain": jnp.clip(1.0 + 0.18 * jax.random.normal(arg_keys[1], (N_SEGMENT, D), jnp.float32), 0.1, 1.9),
        "w_xbc": bell_draw(arg_keys[2], (N_SEGMENT, D, XBC), D ** -0.5, 0.15625, ((0, 8),)),
        "w_gate": bell_draw(arg_keys[3], (N_SEGMENT, D, INNER), D ** -0.5, 0.15625, ((0, 8),)),
        "w_dt": bell_draw(arg_keys[4], (N_SEGMENT, D, HEADS), (4 * D) ** -0.5, 0.078125, ((0, 8),)),
        "dt_bias": jnp.clip(jax.random.uniform(arg_keys[5], (N_SEGMENT, HEADS), jnp.float32, -1.0, 1.0) * block_scale(arg_keys[5], (N_SEGMENT, HEADS), ((0, 8),), -0.4, 0.0), -1.0, 1.0),
        "decay_rate": draw_decay_rate(jax.random.fold_in(arg_keys[12], 71), 0),
        "conv_w": bell_draw(arg_keys[7], (N_SEGMENT, 9, XBC), 9 ** -0.5, 2.0, ((0, 8),), jnp.float32),
        "conv_bias": jnp.clip(jax.random.uniform(arg_keys[8], (N_SEGMENT, XBC), jnp.float32, -0.5, 0.5) * block_scale(arg_keys[8], (N_SEGMENT, XBC), ((0, 8),), -0.4, 0.0), -0.5, 0.5),
        "skip": jnp.clip(0.5 + 1.0 * jax.random.uniform(arg_keys[9], (N_SEGMENT, HEADS), jnp.float32) ** block_scale(arg_keys[9], (N_SEGMENT, HEADS), ((0, 8),), -0.2, 0.2), 0.5, 1.5),
        "out_gain": jnp.clip(1.0 + 0.18 * jax.random.normal(arg_keys[10], (N_SEGMENT, INNER), jnp.float32), 0.1, 1.9),
        "w_out": bell_draw(arg_keys[11], (N_SEGMENT, INNER, D), INNER ** -0.5, 0.15625, ((0, 8),)),
    }


EPSILON = 1e-05

def block_step(state, pieces):
    x_block, b_block, c_block, log_block, dt_block = pieces
    cumul = jnp.cumsum(log_block, axis=0)
    cumul_t = cumul.T
    positions = jnp.arange(log_block.shape[0])
    causal = positions[:, None] >= positions[None, :]
    spread = cumul_t[:, :, None] - cumul_t[:, None, :]
    decay = jnp.exp(jnp.where(causal[None], spread, -jnp.inf))
    intersection = jnp.dot(c_block, b_block.T, preferred_element_type=jnp.float32)
    mixing = (intersection[None] * decay * dt_block.T[:, None, :]).astype(jnp.bfloat16)
    inner_part = jnp.einsum('hij,jhp->ihp', mixing.astype(jnp.float32), x_block.astype(jnp.float32))
    carried = jnp.exp(cumul)[:, :, None] * jnp.einsum('in,hpn->ihp', c_block.astype(jnp.float32), state, precision=lax.Precision.HIGHEST)
    tail = jnp.exp(cumul[-1][None, :] - cumul) * dt_block
    scaled = tail[:, :, None] * x_block.astype(jnp.float32)
    contrib = jnp.einsum('jhp,jn->hpn', scaled, b_block.astype(jnp.float32), precision=lax.Precision.HIGHEST)
    new_state = jnp.exp(cumul[-1])[:, None, None] * state + contrib
    return (new_state, inner_part + carried)

def section(tokens_one, in_gain, w_xbc, w_gate, w_dt, dt_bias, decay_rate, conv_w, conv_bias, skip, out_gain, w_out):
    grid_rows, grid_cols, width_d = tokens_one.shape
    length = grid_rows * grid_cols
    upcast = tokens_one.astype(jnp.float32)
    normed = (upcast * lax.rsqrt(lax.optimization_barrier(jnp.mean(upcast * upcast, -1, keepdims=True)) + EPSILON) * in_gain).astype(jnp.bfloat16)
    flat = normed.reshape(length, width_d)
    conv_input = jnp.dot(flat, w_xbc, preferred_element_type=jnp.float32).astype(jnp.bfloat16).reshape(grid_rows, grid_cols, -1)
    gate = jnp.dot(flat, w_gate, preferred_element_type=jnp.float32).astype(jnp.bfloat16)
    step_size = jax.nn.softplus(jnp.dot(flat, w_dt, preferred_element_type=jnp.float32) + dt_bias)
    padded = jnp.pad(conv_input, ((1, 1), (1, 1), (0, 0)))
    summed = jnp.zeros(conv_input.shape, jnp.float32)
    for tap_row in range(3):
        for tap_col in range(3):
            window = padded[tap_row:tap_row + grid_rows, tap_col:tap_col + grid_cols].astype(jnp.float32)
            summed = summed + window * conv_w[tap_row * 3 + tap_col]
    conv_output = jax.nn.silu(summed + conv_bias).astype(jnp.bfloat16).reshape(length, -1)
    inner = w_gate.shape[1]
    heads = dt_bias.shape[0]
    headdim = inner // heads
    state_n = (conv_output.shape[1] - inner) // 2
    blocks = length // BLOCK
    x_all = conv_output[:, :inner].reshape(blocks, BLOCK, heads, headdim)
    b_all = conv_output[:, inner:inner + state_n].reshape(blocks, BLOCK, state_n)
    c_all = conv_output[:, inner + state_n:].reshape(blocks, BLOCK, state_n)
    log_all = (-step_size * decay_rate).reshape(blocks, BLOCK, heads)
    dt_all = step_size.reshape(blocks, BLOCK, heads)
    start = jnp.zeros((heads, headdim, state_n), jnp.float32)
    _, outputs = lax.scan(block_step, start, (x_all, b_all, c_all, log_all, dt_all))
    x_flat = x_all.reshape(length, heads, headdim).astype(jnp.float32)
    scanned = outputs.reshape(length, heads, headdim) + skip[None, :, None] * x_flat
    gated = scanned.reshape(length, inner) * jax.nn.silu(gate.astype(jnp.float32))
    hidden = (gated * lax.rsqrt(lax.optimization_barrier(jnp.mean(gated * gated, -1, keepdims=True)) + EPSILON) * out_gain).astype(jnp.bfloat16)
    result = upcast.reshape(length, width_d) + jnp.dot(hidden, w_out, preferred_element_type=jnp.float32)
    return result.astype(jnp.bfloat16).reshape(grid_rows, grid_cols, width_d)

def reference(tokens, in_gain, w_xbc, w_gate, w_dt, dt_bias, decay_rate, conv_w, conv_bias, skip, out_gain, w_out):
    results = []
    for segment_index in range(N_SEGMENT):
        results.append(section(tokens[segment_index], in_gain[segment_index], w_xbc[segment_index], w_gate[segment_index], w_dt[segment_index], dt_bias[segment_index], decay_rate[segment_index], conv_w[segment_index], conv_bias[segment_index], skip[segment_index], out_gain[segment_index], w_out[segment_index]))
    handed = [jnp.swapaxes(results[(segment_index - 1) % N_SEGMENT], 0, 1) for segment_index in range(N_SEGMENT)]
    return jnp.stack(handed)
```

```python
import functools

import jax
import jax.numpy as jnp
from jax import lax
from jax.experimental import pallas as pl
from jax.experimental.pallas import tpu as pltpu
from jax.sharding import PartitionSpec as P

EPSILON = 1e-05
ROWS = 8
LINE = 128
LENGTH = ROWS * LINE
HEADS = 24
WIDTH = 64
STATE = 64
INNER = HEADS * WIDTH
D = 1536
HALF = D // 2
GROUP = 384
GROUP_HEADS = GROUP // WIDTH
BANDS = 16
F32 = jnp.float32
BF16 = jnp.bfloat16
VMEM = 56 * 1024 * 1024


def params(limit=VMEM):
    return pltpu.CompilerParams(
        dimension_semantics=("arbitrary",), vmem_limit_bytes=limit
    )


def whole(*shape):
    return pl.BlockSpec(shape, lambda i: (0,) * len(shape))


def dot(a, b):
    return jnp.dot(a, b, preferred_element_type=F32)


def rms(values, gain):
    return values * lax.rsqrt(jnp.mean(values * values, -1, keepdims=True) + EPSILON) * gain


def silu(v):
    return v / (1.0 + jnp.exp(-v))


def head_spread(channels, first):
    head = lax.broadcasted_iota(jnp.int32, (HEADS, channels), 0)
    channel = lax.broadcasted_iota(jnp.int32, (HEADS, channels), 1)
    return jnp.where(head - first == channel // WIDTH, 1.0, 0.0).astype(BF16)


def to_channels(values, spread):
    high = values.astype(BF16)
    low = (values - high.astype(F32)).astype(BF16)
    return dot(high, spread) + dot(low, spread)


def project_kernel(
    tok, gain, w_x, w_bc, w_dt, dt_bias, rate, normed, xc, bc, cum, dt, band_tail, band_decay, total
):
    @pl.when(pl.program_id(0) == 0)
    def _():
        for r in range(ROWS):
            part = pl.ds(r * LINE, LINE)
            normed[part, :] = rms(tok[part, :].astype(F32), gain[...]).astype(BF16)
        bc[...] = dot(normed[...], w_bc[...]).astype(BF16)
        raw = dot(normed[...], w_dt[...]) + dt_bias[...]
        step = jnp.maximum(raw, 0.0) + jnp.log1p(jnp.exp(-jnp.abs(raw)))
        dt[...] = step
        log_decay = -rate[...] * step
        i = lax.broadcasted_iota(jnp.int32, (LINE, LINE), 0)
        j = lax.broadcasted_iota(jnp.int32, (LINE, LINE), 1)
        lower = jnp.where(i >= j, 1.0, 0.0).astype(F32)
        lines = [
            jnp.dot(
                lower,
                log_decay[r * LINE : (r + 1) * LINE],
                precision=lax.Precision.HIGHEST,
                preferred_element_type=F32,
            )
            for r in range(ROWS)
        ]
        ends = [line[LINE - 1 : LINE] for line in lines]
        before = [jnp.zeros_like(ends[0])]
        after = [jnp.zeros_like(ends[0])]
        for r in range(ROWS - 1):
            before.append(before[-1] + ends[r])
            after.append(after[-1] + ends[ROWS - 1 - r])
        for r in range(ROWS):
            part = pl.ds(r * LINE, LINE)
            cum[part, :] = lines[r]
            band_decay[part, :] = jnp.exp(lines[r] + before[r])
            band_tail[part, :] = step[r * LINE : (r + 1) * LINE] * jnp.exp(
                (ends[r] - lines[r]) + after[ROWS - 1 - r]
            )
        total[...] = before[-1] + ends[-1]

    for m in range(4):
        part = pl.ds(m * 256, 256)
        xc[part, :] = dot(normed[part, :], w_x[...]).astype(BF16)


def project(tok, gain, w_xbc, w_dt, dt_bias, rate):
    per_head = jax.ShapeDtypeStruct((LENGTH, HEADS), F32)
    return pl.pallas_call(
        project_kernel,
        grid=(6,),
        in_specs=[
            whole(LENGTH, D),
            whole(1, D),
            pl.BlockSpec((D, 256), lambda i: (0, i)),
            pl.BlockSpec((D, 128), lambda i: (0, INNER // 128)),
            whole(D, HEADS),
            whole(1, HEADS),
            whole(1, HEADS),
        ],
        out_specs=[
            whole(LENGTH, D),
            pl.BlockSpec((LENGTH, 256), lambda i: (0, i)),
            whole(LENGTH, 128),
            whole(LENGTH, HEADS),
            whole(LENGTH, HEADS),
            whole(LENGTH, HEADS),
            whole(LENGTH, HEADS),
            whole(1, HEADS),
        ],
        out_shape=[
            jax.ShapeDtypeStruct((LENGTH, D), BF16),
            jax.ShapeDtypeStruct((LENGTH, INNER), BF16),
            jax.ShapeDtypeStruct((LENGTH, 128), BF16),
            per_head,
            per_head,
            per_head,
            per_head,
            jax.ShapeDtypeStruct((1, HEADS), F32),
        ],
        compiler_params=params(),
        cost_estimate=pl.CostEstimate(
            flops=2 * LENGTH * D * 1688, bytes_accessed=16 << 20, transcendentals=LENGTH * 128
        ),
        name="project",
    )(tok, gain, w_xbc, w_xbc, w_dt, dt_bias, rate)


def gate_kernel(normed, w, out):
    for m in range(4):
        part = pl.ds(m * 256, 256)
        out[part, :] = silu(dot(normed[part, :], w[...])).astype(BF16)


def gate_of(normed, w_gate):
    return pl.pallas_call(
        gate_kernel,
        grid=(6,),
        in_specs=[whole(LENGTH, D), pl.BlockSpec((D, 256), lambda i: (0, i))],
        out_specs=pl.BlockSpec((LENGTH, 256), lambda i: (0, i)),
        out_shape=jax.ShapeDtypeStruct((LENGTH, INNER), BF16),
        compiler_params=params(),
        cost_estimate=pl.CostEstimate(
            flops=2 * LENGTH * D * INNER, bytes_accessed=11 << 20, transcendentals=LENGTH * INNER
        ),
        name="gate",
    )(normed, w_gate)


def convolved(above, own, below, taps, bias, out):
    channels = taps.shape[1]
    column = lax.broadcasted_iota(jnp.int32, (LINE, channels), 0)

    def line(r):
        if r < 0:
            return above.astype(F32)
        if r >= ROWS:
            return below.astype(F32)
        return own[pl.ds(r * LINE, LINE), :].astype(F32)

    for r in range(ROWS):
        lines = [line(r - 1), line(r), line(r + 1)]
        west, here, east = (
            sum(lines[i] * taps[3 * i + j : 3 * i + j + 1] for i in range(3)) for j in range(3)
        )
        west = jnp.where(column == 0, 0.0, pltpu.roll(west, 1, 0))
        east = jnp.where(column == LINE - 1, 0.0, pltpu.roll(east, LINE - 1, 0))
        out[pl.ds(r * LINE, LINE), :] = silu(west + here + east + bias).astype(BF16)


def conv_kernel(
    top,
    bottom,
    gain,
    w_x,
    w_bc,
    xc,
    bc,
    taps_x,
    taps_bc,
    bias_x,
    bias_bc,
    band_tail,
    total,
    x,
    bcs,
    pieces,
    edge,
    b_t,
):
    g = pl.program_id(0)

    @pl.when(g == 0)
    def _():
        edge[pl.ds(0, LINE), :] = rms(top[...].astype(F32), gain[...]).astype(BF16)
        edge[pl.ds(LINE, LINE), :] = rms(bottom[...].astype(F32), gain[...]).astype(BF16)
        side = dot(edge[...], w_bc[...]).astype(BF16)
        convolved(side[:LINE], bc, side[LINE:], taps_bc[...], bias_bc[...], bcs)
        for r in range(ROWS):
            part = pl.ds(r * LINE, LINE)
            b_t[:, part] = bcs[part, :].astype(F32).T.astype(BF16)

    side = dot(edge[...], w_x[...]).astype(BF16)
    convolved(side[:LINE], xc, side[LINE:], taps_x[...], bias_x[...], x)
    spread = head_spread(GROUP, g * GROUP_HEADS)
    state = jnp.zeros((STATE, GROUP), F32)
    for r in range(ROWS):
        part = pl.ds(r * LINE, LINE)
        weighted = x[part, :].astype(F32) * to_channels(band_tail[part, :], spread)
        state = state + dot(b_t[pl.ds(0, STATE), part], weighted.astype(BF16))
    head = lax.broadcasted_iota(jnp.int32, (HEADS, 128), 0)
    lane = lax.broadcasted_iota(jnp.int32, (HEADS, 128), 1)
    pick = jnp.where(head == lane + g * GROUP_HEADS, 1.0, 0.0).astype(BF16)
    first = total[...].astype(BF16)
    rest = total[...] - first.astype(F32)
    second = rest.astype(BF16)
    third = (rest - second.astype(F32)).astype(BF16)
    terms = jnp.concatenate(
        [dot(jnp.broadcast_to(t, (8, HEADS)), pick)[:1] for t in (first, second, third)]
        + [jnp.zeros((13, 128), F32)],
        axis=0,
    ).astype(BF16)
    for a in range(4):
        pieces[a, 0, :, pl.ds(0, GROUP)] = state[16 * a : 16 * a + 16].astype(BF16)
        pieces[a, 0, :, pl.ds(GROUP, 128)] = terms


def convolve(top, bottom, gain, w_xbc, xc, bc, conv_w, conv_bias, band_tail, total):
    return pl.pallas_call(
        conv_kernel,
        grid=(4,),
        in_specs=[
            whole(LINE, D),
            whole(LINE, D),
            whole(1, D),
            pl.BlockSpec((D, GROUP), lambda i: (0, i)),
            pl.BlockSpec((D, 128), lambda i: (0, INNER // 128)),
            pl.BlockSpec((LENGTH, GROUP), lambda i: (0, i)),
            whole(LENGTH, 128),
            pl.BlockSpec((9, GROUP), lambda i: (0, i)),
            pl.BlockSpec((9, 128), lambda i: (0, INNER // 128)),
            pl.BlockSpec((1, GROUP), lambda i: (0, i)),
            pl.BlockSpec((1, 128), lambda i: (0, INNER // 128)),
            whole(LENGTH, HEADS),
            whole(1, HEADS),
        ],
        out_specs=[
            pl.BlockSpec((LENGTH, GROUP), lambda i: (0, i)),
            whole(LENGTH, 128),
            pl.BlockSpec((4, 1, 16, GROUP + 128), lambda i: (0, i, 0, 0)),
        ],
        out_shape=[
            jax.ShapeDtypeStruct((LENGTH, INNER), BF16),
            jax.ShapeDtypeStruct((LENGTH, 128), BF16),
            jax.ShapeDtypeStruct((4, 4, 16, GROUP + 128), BF16),
        ],
        scratch_shapes=[pltpu.VMEM((2 * LINE, D), BF16), pltpu.VMEM((128, LENGTH), BF16)],
        compiler_params=params(),
        cost_estimate=pl.CostEstimate(
            flops=2 * 256 * D * 1664 + 40 * LENGTH * 1664,
            bytes_accessed=14 << 20,
            transcendentals=LENGTH * 1664,
        ),
        name="convolve",
    )(top, bottom, gain, w_xbc, w_xbc, xc, bc, conv_w, conv_w, conv_bias, conv_bias, band_tail, total)


def scan_kernel(x, bcs, cum, dt, gate, skip, out, spread, state):
    @pl.when(pl.program_id(0) == 0)
    def _():
        spread[...] = head_spread(INNER, 0)
        state[...] = jnp.zeros_like(state)

    sums = cum[...]
    sums_t = sums.T
    end = sums[LINE - 1 : LINE]
    both = bcs[...]
    lane = lax.broadcasted_iota(jnp.int32, (LINE, LINE), 1)
    row = lax.broadcasted_iota(jnp.int32, (LINE, LINE), 0)
    both_f = both.astype(F32)
    both_t = both_f.T.astype(BF16)
    c_only = jnp.where(lane < STATE, pltpu.roll(both_f, STATE, 1), 0.0).astype(BF16)
    weights = jnp.where(row >= lane, dot(c_only, both_t), 0.0)
    values = jnp.concatenate(
        [
            jnp.exp(sums),
            dt[...],
            dt[...] * jnp.exp(end - sums),
            jnp.broadcast_to(jnp.exp(end), (8, HEADS)),
            jnp.broadcast_to(skip[...], (8, HEADS)),
        ],
        axis=0,
    )
    high = values.astype(BF16)
    low = (values - high.astype(F32)).astype(BF16)
    for p in range(HEADS // 2):
        part = pl.ds(p * 128, 128)
        wide = dot(high, spread[:, part]) + dot(low, spread[:, part])
        carry, step, tail = wide[:LINE], wide[LINE : 2 * LINE], wide[2 * LINE : 3 * LINE]
        past, direct = wide[3 * LINE : 3 * LINE + 1], wide[3 * LINE + 8 : 3 * LINE + 9]
        values_x = x[:, part].astype(F32)
        stepped = values_x * step
        mixing = [
            (jnp.exp(jnp.minimum(sums[:, h : h + 1] - sums_t[h : h + 1], 0.0)) * weights).astype(BF16)
            for h in (2 * p, 2 * p + 1)
        ]
        columns = jnp.concatenate(
            [jnp.where(lane < WIDTH, stepped, 0.0), jnp.where(lane < WIDTH, 0.0, stepped)], axis=0
        ).astype(BF16)
        inner = dot(jnp.concatenate(mixing, axis=1), columns)
        carried = carry * dot(both, state[:, part].astype(BF16))
        y = inner + carried + direct * values_x
        out[:, part] = (y * gate[:, part].astype(F32)).astype(BF16)
        state[pl.ds(STATE, STATE), part] = past * state[pl.ds(STATE, STATE), part] + dot(
            both_t[:STATE], (values_x * tail).astype(BF16)
        )


def scan(x, bcs, cum, dt, gate, skip):
    line = lambda n: pl.BlockSpec((LINE, n), lambda i: (i, 0))
    return pl.pallas_call(
        scan_kernel,
        grid=(ROWS,),
        in_specs=[line(INNER), line(128), line(HEADS), line(HEADS), line(INNER), whole(1, HEADS)],
        out_specs=line(INNER),
        out_shape=jax.ShapeDtypeStruct((LENGTH, INNER), BF16),
        scratch_shapes=[pltpu.VMEM((HEADS, INNER), BF16), pltpu.VMEM((2 * STATE, INNER), F32)],
        compiler_params=params(),
        cost_estimate=pl.CostEstimate(
            flops=4 << 30, bytes_accessed=10 << 20, transcendentals=LENGTH * LINE * HEADS
        ),
        name="scan",
    )(x, bcs, cum, dt, gate, skip)


def relay_kernel(arrived, out):
    logs = jnp.concatenate(
        [
            jnp.sum(arrived[j, :, pl.ds(GROUP, 128)].astype(F32), axis=0, keepdims=True)
            for j in range(BANDS)
        ],
        axis=0,
    )
    decay = jnp.exp(logs)
    lane = lax.broadcasted_iota(jnp.int32, (128, GROUP), 0)
    channel = lax.broadcasted_iota(jnp.int32, (128, GROUP), 1)
    wide = to_channels(decay, jnp.where(lane == channel // WIDTH, 1.0, 0.0).astype(BF16))
    state = jnp.zeros((16, GROUP), F32)
    for j in range(BANDS):
        out[j] = state.astype(BF16)
        state = wide[j : j + 1] * state + arrived[j, :, pl.ds(0, GROUP)].astype(F32)


def relay(arrived):
    return pl.pallas_call(
        relay_kernel,
        out_shape=jax.ShapeDtypeStruct((BANDS, 16, GROUP), BF16),
        compiler_params=pltpu.CompilerParams(vmem_limit_bytes=16 << 20),
        name="relay",
    )(arrived)


def columns_out(values, tokens, turned, out):
    values = values + tokens
    for k in range(HALF // 128):
        part = slice(k * 128, (k + 1) * 128)
        for r in range(ROWS):
            turned[k, pl.ds(r, 32, stride=ROWS), :] = values[r * 32 : (r + 1) * 32, part]
        out[:, part] = turned[k].astype(BF16)


def finish_kernel(local, gate, bcs, band_decay, entering, gain, tok, w, hidden, out, spread, state, turned):
    @pl.when(pl.program_id(0) == 0)
    def _():
        spread[...] = head_spread(INNER, 0)
        state[pl.ds(0, STATE), :] = jnp.zeros((STATE, INNER), BF16)
        for a in range(4):
            for g in range(4):
                state[pl.ds(STATE + 16 * a, 16), pl.ds(g * GROUP, GROUP)] = entering[4 * a + g]

    both = bcs[...].reshape(256, 128)
    decay = band_decay[...].reshape(256, HEADS)
    carried = dot(both, state[...]) * to_channels(decay, spread[...])
    gated = local[...].reshape(256, INNER).astype(F32) + carried * gate[...].reshape(256, INNER).astype(F32)
    normed = rms(gated, gain[...]).astype(BF16)
    hidden[...] = normed.reshape(ROWS, 32, INNER)
    columns_out(dot(normed, w[...]), tok[...].reshape(256, HALF).astype(F32), turned, out)


def finish(local, gate, bcs, band_decay, entering, gain, tok, w_out):
    cells = lambda n: pl.BlockSpec((ROWS, 32, n), lambda i: (0, i, 0))
    return pl.pallas_call(
        finish_kernel,
        grid=(LINE // 32,),
        in_specs=[
            cells(INNER),
            cells(INNER),
            cells(128),
            cells(HEADS),
            whole(BANDS, 16, GROUP),
            whole(1, INNER),
            cells(HALF),
            whole(INNER, HALF),
        ],
        out_specs=[cells(INNER), pl.BlockSpec((256, HALF), lambda i: (i, 0))],
        out_shape=[
            jax.ShapeDtypeStruct((ROWS, LINE, INNER), BF16),
            jax.ShapeDtypeStruct((LENGTH, HALF), BF16),
        ],
        scratch_shapes=[
            pltpu.VMEM((HEADS, INNER), BF16),
            pltpu.VMEM((2 * STATE, INNER), BF16),
            pltpu.VMEM((HALF // 128, 256, 128), F32),
        ],
        compiler_params=params(),
        cost_estimate=pl.CostEstimate(
            flops=2 * LENGTH * D * HALF, bytes_accessed=16 << 20, transcendentals=LENGTH
        ),
        name="finish",
    )(local, gate, bcs, band_decay, entering, gain, tok, w_out)


def rest_kernel(hidden, tok, w, out, turned):
    columns_out(
        dot(hidden[...].reshape(256, INNER), w[...]),
        tok[...].reshape(256, HALF).astype(F32),
        turned,
        out,
    )


def rest(hidden, tok, w_out):
    return pl.pallas_call(
        rest_kernel,
        grid=(LINE // 32,),
        in_specs=[
            pl.BlockSpec((ROWS, 32, INNER), lambda i: (0, i, 0)),
            pl.BlockSpec((ROWS, 32, HALF), lambda i: (0, i, 1)),
            pl.BlockSpec((INNER, HALF), lambda i: (0, 1)),
        ],
        out_specs=pl.BlockSpec((256, HALF), lambda i: (i, 0)),
        out_shape=jax.ShapeDtypeStruct((LENGTH, HALF), BF16),
        scratch_shapes=[pltpu.VMEM((HALF // 128, 256, 128), F32)],
        compiler_params=params(),
        cost_estimate=pl.CostEstimate(
            flops=2 * LENGTH * D * HALF, bytes_accessed=8 << 20, transcendentals=0
        ),
        name="rest",
    )(hidden, tok, w_out)


def shards(
    tokens,
    in_gain,
    w_xbc,
    w_gate,
    w_dt,
    dt_bias,
    decay_rate,
    conv_w,
    conv_bias,
    skip,
    out_gain,
    w_out,
):
    bands = lax.axis_size("band")
    segments = lax.axis_size("segment")
    cells = tokens[0]
    tok = cells.reshape(LENGTH, D)
    top = lax.ppermute(cells[ROWS - 1], "band", [(i, i + 1) for i in range(bands - 1)])
    bottom = lax.ppermute(cells[0], "band", [(i + 1, i) for i in range(bands - 1)])

    normed, xc, bc, cum, dt, band_tail, band_decay, total = project(
        tok, in_gain, w_xbc[0], w_dt[0], dt_bias, decay_rate
    )
    gate = gate_of(normed, w_gate[0])
    x, bcs, pieces = convolve(
        top, bottom, in_gain, w_xbc[0], xc, bc, conv_w[0], conv_bias, band_tail, total
    )
    swap = functools.partial(
        lax.all_to_all, axis_name="band", split_axis=0, concat_axis=0, tiled=True
    )
    onward = functools.partial(
        lax.ppermute, axis_name="segment", perm=[(i, (i + 1) % segments) for i in range(segments)]
    )
    arrived = swap(pieces.reshape(BANDS, 16, GROUP + 128))
    local = scan(x, bcs, cum, dt, gate, skip)
    entering = swap(relay(arrived))

    grid = lambda a: a.reshape(ROWS, LINE, a.shape[-1])
    hidden, first = finish(
        grid(local), grid(gate), grid(bcs), grid(band_decay), entering, out_gain, cells, w_out[0]
    )
    first = onward(first.reshape(BANDS, LENGTH // BANDS, HALF))
    second = swap(rest(hidden, cells, w_out[0]).reshape(BANDS, LENGTH // BANDS, HALF))
    first = swap(first)
    second = onward(second)
    both = jnp.concatenate([first, second], axis=-1)
    handed = both.reshape(BANDS, LINE // BANDS, ROWS, D).swapaxes(0, 1)
    return handed.reshape(1, LINE // BANDS, BANDS * ROWS, D)


def solution(mesh):
    in_specs = (
        P("segment", "band", None, None),
        P("segment", None),
        P("segment", None, None),
        P("segment", None, None),
        P("segment", None, None),
        P("segment", None),
        P("segment", None),
        P("segment", None, None),
        P("segment", None),
        P("segment", None),
        P("segment", None),
        P("segment", None, None),
    )
    out_specs = P("segment", "band", None, None)
    return jax.shard_map(shards, mesh=mesh, in_specs=in_specs, out_specs=out_specs, check_vma=False)
```

```python
import functools

import jax
import jax.numpy as jnp
from jax import lax
from jax.experimental import pallas as pl
from jax.experimental.pallas import tpu as pltpu
from jax.sharding import PartitionSpec as P

EPSILON = 1e-05
ROWS = 8
LINE = 128
LENGTH = ROWS * LINE
HEADS = 24
WIDTH = 64
STATE = 64
INNER = HEADS * WIDTH
D = 1536
HALF = D // 2
GROUP = 384
GROUP_HEADS = GROUP // WIDTH
BANDS = 16
F32 = jnp.float32
BF16 = jnp.bfloat16
MIB = 1 << 20
LOG2E = 1.4426950408889634


def params(mib):
    return pltpu.CompilerParams(
        dimension_semantics=("arbitrary",), vmem_limit_bytes=mib * MIB
    )


def whole(*shape):
    return pl.BlockSpec(shape, lambda i: (0,) * len(shape), pipeline_mode=pl.Buffered(1))


def dot(a, b):
    return jnp.dot(a, b, preferred_element_type=F32)


def rms(values, gain):
    return values * lax.rsqrt(jnp.mean(values * values, -1, keepdims=True) + EPSILON) * gain


def silu(v):
    half = 0.5 * v
    return half + half * jnp.tanh(half)


def head_spread(channels, first):
    head = lax.broadcasted_iota(jnp.int32, (2 * HEADS, channels), 0)
    head = jnp.where(head < HEADS, head, head - HEADS)
    channel = lax.broadcasted_iota(jnp.int32, (2 * HEADS, channels), 1)
    return jnp.where(head - first == channel // WIDTH, 1.0, 0.0).astype(BF16)


def two_terms(values_t):
    high = values_t.astype(BF16).astype(F32)
    return jnp.concatenate([high, values_t - high], axis=0).T.astype(BF16)


def project_kernel(
    tok, gain, w_x, w_g, w_bc, w_dt, dt_bias, rate, xc, gate, bc, cum, dt, band_tail, band_decay, total, normed
):
    step = pl.program_id(0)

    @pl.when(step == 0)
    def _():
        for r in range(ROWS):
            part = pl.ds(r * LINE, LINE)
            normed[part, :] = rms(tok[part, :].astype(F32), gain[...]).astype(BF16)
        bc[...] = dot(normed[...], w_bc[...]).astype(BF16)
        raw = (
            lax.dot_general(
                w_dt[...], normed[...], (((1,), (1,)), ((), ())), preferred_element_type=F32
            )
            + dt_bias[...]
        )
        steps = jnp.maximum(raw, 0.0) + jnp.log1p(jnp.exp(-jnp.abs(raw)))
        dt[...] = steps
        log_decay = -rate[...] * steps
        i = lax.broadcasted_iota(jnp.int32, (LINE, LINE), 0)
        j = lax.broadcasted_iota(jnp.int32, (LINE, LINE), 1)
        sums = jnp.dot(
            jnp.concatenate([log_decay[:, r * LINE : (r + 1) * LINE] for r in range(ROWS)], axis=0),
            jnp.where(i <= j, 1.0, 0.0).astype(F32),
            precision=lax.Precision.HIGHEST,
            preferred_element_type=F32,
        )
        lines = [sums[r * HEADS : (r + 1) * HEADS] for r in range(ROWS)]
        ends = [line[:, LINE - 1 :] for line in lines]
        before = [jnp.zeros_like(ends[0])]
        after = [jnp.zeros_like(ends[0])]
        for r in range(ROWS - 1):
            before.append(before[-1] + ends[r])
            after.append(after[-1] + ends[ROWS - 1 - r])
        for r in range(ROWS):
            part = slice(r * LINE, (r + 1) * LINE)
            cum[:, part] = lines[r]
            band_decay[:, part] = jnp.exp(lines[r] + before[r])
            band_tail[:, part] = steps[:, part] * jnp.exp((ends[r] - lines[r]) + after[ROWS - 1 - r])
        total[...] = jnp.broadcast_to(before[-1] + ends[-1], (HEADS, LINE)).T[:1]

    @pl.when(step < 3)
    def _():
        for m in range(2):
            part = pl.ds(m * 512, 512)
            xc[part, :] = dot(normed[part, :], w_x[...]).astype(BF16)

    @pl.when(step >= 3)
    def _():
        for m in range(2):
            part = pl.ds(m * 512, 512)
            gate[part, :] = silu(dot(normed[part, :], w_g[...])).astype(BF16)


def project(tok, gain, w_xbc, w_gate, w_dt_t, dt_bias_t, rate_t):
    per_head = jax.ShapeDtypeStruct((HEADS, LENGTH), F32)
    first = lambda i: (0, jnp.minimum(i, 2))
    second = lambda i: (0, jnp.maximum(i - 3, 0))
    return pl.pallas_call(
        project_kernel,
        grid=(6,),
        in_specs=[
            whole(LENGTH, D),
            whole(1, D),
            pl.BlockSpec((D, 512), first),
            pl.BlockSpec((D, 512), second),
            pl.BlockSpec((D, 128), lambda i: (0, INNER // 128), pipeline_mode=pl.Buffered(1)),
            whole(HEADS, D),
            whole(HEADS, 1),
            whole(HEADS, 1),
        ],
        out_specs=[
            pl.BlockSpec((LENGTH, 512), first),
            pl.BlockSpec((LENGTH, 512), second),
            whole(LENGTH, 128),
            whole(HEADS, LENGTH),
            whole(HEADS, LENGTH),
            whole(HEADS, LENGTH),
            whole(HEADS, LENGTH),
            whole(1, HEADS),
        ],
        out_shape=[
            jax.ShapeDtypeStruct((LENGTH, INNER), BF16),
            jax.ShapeDtypeStruct((LENGTH, INNER), BF16),
            jax.ShapeDtypeStruct((LENGTH, 128), BF16),
            per_head,
            per_head,
            per_head,
            per_head,
            jax.ShapeDtypeStruct((1, HEADS), F32),
        ],
        scratch_shapes=[pltpu.VMEM((LENGTH, D), BF16)],
        compiler_params=params(32),
        cost_estimate=pl.CostEstimate(
            flops=2 * LENGTH * D * 3224, bytes_accessed=20 << 20, transcendentals=LENGTH * INNER
        ),
        name="project",
    )(tok, gain, w_xbc, w_gate, w_xbc, w_dt_t, dt_bias_t, rate_t)


def convolved(above, own, below, taps, bias, out):
    channels = bias.shape[1]
    column = lax.broadcasted_iota(jnp.int32, (LINE, channels), 0)

    def line(r):
        if r < 0:
            return above.astype(F32)
        if r >= ROWS:
            return below.astype(F32)
        return own[pl.ds(r * LINE, LINE), :].astype(F32)

    for r in range(ROWS):
        lines = [line(r - 1), line(r), line(r + 1)]
        west, here, east = (
            lines[0] * taps[j] + lines[1] * taps[3 + j] + lines[2] * taps[6 + j] for j in range(3)
        )
        west = jnp.where(column == 0, 0.0, pltpu.roll(west, 1, 0))
        east = jnp.where(column == LINE - 1, 0.0, pltpu.roll(east, LINE - 1, 0))
        out[pl.ds(r * LINE, LINE), :] = silu(west + here + east + bias).astype(BF16)


def conv_kernel(
    top,
    bottom,
    gain,
    w_x,
    w_bc,
    xc,
    bc,
    taps_x,
    taps_bc,
    bias_x,
    bias_bc,
    band_tail,
    total,
    x,
    bcs,
    pieces,
    edge,
    b_t,
    tails,
):
    g = pl.program_id(0)

    @pl.when(g == 0)
    def _():
        edge[pl.ds(0, LINE), :] = rms(top[...].astype(F32), gain[...]).astype(BF16)
        edge[pl.ds(LINE, LINE), :] = rms(bottom[...].astype(F32), gain[...]).astype(BF16)
        side = dot(edge[...], w_bc[...]).astype(BF16)
        convolved(side[:LINE], bc, side[LINE:], [taps_bc[k] for k in range(9)], bias_bc[...], bcs)
        for r in range(ROWS):
            part = pl.ds(r * LINE, LINE)
            b_t[:, part] = bcs[part, :].astype(F32).T.astype(BF16)
            tails[part, :] = two_terms(band_tail[:, part])

    side = dot(edge[...], w_x[...]).astype(BF16)
    convolved(side[:LINE], xc, side[LINE:], [taps_x[k] for k in range(9)], bias_x[...], x)
    spread = head_spread(GROUP, g * GROUP_HEADS)
    state = jnp.zeros((STATE, GROUP), F32)
    for r in range(ROWS // 2):
        part = pl.ds(r * 2 * LINE, 2 * LINE)
        weighted = x[part, :].astype(F32) * dot(tails[part, :], spread)
        state = state + dot(b_t[pl.ds(0, STATE), part], weighted.astype(BF16))
    head = lax.broadcasted_iota(jnp.int32, (HEADS, 128), 0)
    lane = lax.broadcasted_iota(jnp.int32, (HEADS, 128), 1)
    pick = jnp.where(head == lane + g * GROUP_HEADS, 1.0, 0.0).astype(BF16)
    first = total[...].astype(BF16)
    rest = total[...] - first.astype(F32)
    second = rest.astype(BF16)
    third = (rest - second.astype(F32)).astype(BF16)
    terms = jnp.concatenate(
        [dot(jnp.broadcast_to(t, (8, HEADS)), pick)[:1] for t in (first, second, third)]
        + [jnp.zeros((13, 128), F32)],
        axis=0,
    ).astype(BF16)
    for a in range(4):
        pieces[a, 0, :, pl.ds(0, GROUP)] = state[16 * a : 16 * a + 16].astype(BF16)
        pieces[a, 0, :, pl.ds(GROUP, 128)] = terms


def convolve(top, bottom, gain, w_xbc, xc, bc, taps, conv_bias, band_tail, total):
    return pl.pallas_call(
        conv_kernel,
        grid=(4,),
        in_specs=[
            whole(LINE, D),
            whole(LINE, D),
            whole(1, D),
            pl.BlockSpec((D, GROUP), lambda i: (0, i)),
            pl.BlockSpec((D, 128), lambda i: (0, INNER // 128), pipeline_mode=pl.Buffered(1)),
            pl.BlockSpec((LENGTH, GROUP), lambda i: (0, i)),
            whole(LENGTH, 128),
            pl.BlockSpec((9, 1, GROUP), lambda i: (0, 0, i)),
            pl.BlockSpec((9, 1, 128), lambda i: (0, 0, INNER // 128)),
            pl.BlockSpec((1, GROUP), lambda i: (0, i)),
            pl.BlockSpec((1, 128), lambda i: (0, INNER // 128)),
            whole(HEADS, LENGTH),
            whole(1, HEADS),
        ],
        out_specs=[
            pl.BlockSpec((LENGTH, GROUP), lambda i: (0, i)),
            whole(LENGTH, 128),
            pl.BlockSpec((4, 1, 16, GROUP + 128), lambda i: (0, i, 0, 0)),
        ],
        out_shape=[
            jax.ShapeDtypeStruct((LENGTH, INNER), BF16),
            jax.ShapeDtypeStruct((LENGTH, 128), BF16),
            jax.ShapeDtypeStruct((4, 4, 16, GROUP + 128), BF16),
        ],
        scratch_shapes=[
            pltpu.VMEM((2 * LINE, D), BF16),
            pltpu.VMEM((128, LENGTH), BF16),
            pltpu.VMEM((LENGTH, 2 * HEADS), BF16),
        ],
        compiler_params=params(20),
        cost_estimate=pl.CostEstimate(
            flops=2 * 256 * D * 1664 + 40 * LENGTH * 1664,
            bytes_accessed=14 << 20,
            transcendentals=LENGTH * 1664,
        ),
        name="convolve",
    )(top, bottom, gain, w_xbc, w_xbc, xc, bc, taps, taps, conv_bias, conv_bias, band_tail, total)


def scan_kernel(x, bcs, cum, dt, gate, skip, out, direct, state):
    @pl.when(pl.program_id(0) == 0)
    def _():
        direct[...] = dot(
            two_terms(jnp.broadcast_to(skip[...], (HEADS, 8))), head_spread(INNER, 0)
        )
        state[...] = jnp.zeros_like(state)

    sums_t = cum[...] * LOG2E
    step_t = dt[...]
    sums = sums_t.T
    step = step_t.T
    both = bcs[...].astype(F32)
    lane = lax.broadcasted_iota(jnp.int32, (LINE, LINE), 1)
    row = lax.broadcasted_iota(jnp.int32, (LINE, LINE), 0)
    left = lane < WIDTH
    b_t = both.T.astype(BF16)[:STATE]
    c = pltpu.roll(both, STATE, 1).astype(BF16)[:, :STATE]
    weights = jnp.where(row >= lane, dot(c, b_t), 0.0)

    def mixing(h):
        along = jnp.broadcast_to(sums[:, h : h + 1], (LINE, LINE))
        decay = jnp.exp2(jnp.minimum(along - sums_t[h : h + 1], 0.0))
        return along, (decay * (weights * step_t[h : h + 1])).astype(BF16)

    for q in range(HEADS // 4):
        quad = pl.ds(q * 256, 256)
        carried = dot(c, state[:, quad].astype(BF16))
        tails, decays = [], []
        for p in (2 * q, 2 * q + 1):
            part = pl.ds(p * 128, 128)
            values = x[:, part].astype(F32)
            (along_a, mixing_a), (along_b, mixing_b) = mixing(2 * p), mixing(2 * p + 1)
            columns = jnp.concatenate(
                [jnp.where(left, values, 0.0), jnp.where(left, 0.0, values)], axis=0
            ).astype(BF16)
            inner = dot(jnp.concatenate([mixing_a, mixing_b], axis=1), columns)
            here = jnp.where(left, along_a, along_b)
            carry = jnp.exp2(here)
            stepped = jnp.where(left, step[:, 2 * p : 2 * p + 1], step[:, 2 * p + 1 : 2 * p + 2])
            tails.append((values * stepped * jnp.exp2(here[LINE - 1 :] - here)).astype(BF16))
            decays.append(carry[LINE - 1 :])
            side = slice((p % 2) * 128, (p % 2) * 128 + 128)
            y = inner + carry * carried[:, side] + direct[0:1, part] * values
            out[:, part] = (y * gate[:, part].astype(F32)).astype(BF16)
        state[:, quad] = jnp.concatenate(decays, axis=1) * state[:, quad] + dot(
            b_t, jnp.concatenate(tails, axis=1)
        )


def scan(x, bcs, cum, dt, gate, skip_t):
    line = lambda n: pl.BlockSpec((LINE, n), lambda i: (i, 0))
    heads = pl.BlockSpec((HEADS, LINE), lambda i: (0, i))
    return pl.pallas_call(
        scan_kernel,
        grid=(ROWS,),
        in_specs=[line(INNER), line(128), heads, heads, line(INNER), whole(HEADS, 1)],
        out_specs=line(INNER),
        out_shape=jax.ShapeDtypeStruct((LENGTH, INNER), BF16),
        scratch_shapes=[pltpu.VMEM((8, INNER), F32), pltpu.VMEM((STATE, INNER), F32)],
        compiler_params=params(12),
        cost_estimate=pl.CostEstimate(
            flops=4 << 30, bytes_accessed=10 << 20, transcendentals=LENGTH * LINE * HEADS
        ),
        name="scan",
    )(x, bcs, cum, dt, gate, skip_t)


def relay_kernel(arrived, out):
    logs = jnp.concatenate(
        [
            jnp.sum(arrived[j, :, pl.ds(GROUP, 128)].astype(F32), axis=0, keepdims=True)
            for j in range(BANDS)
        ],
        axis=0,
    )
    decay = jnp.exp(logs)
    high = decay.astype(BF16)
    low = (decay - high.astype(F32)).astype(BF16)
    lane = lax.broadcasted_iota(jnp.int32, (128, GROUP), 0)
    channel = lax.broadcasted_iota(jnp.int32, (128, GROUP), 1)
    spread = jnp.where(lane == channel // WIDTH, 1.0, 0.0).astype(BF16)
    wide = dot(high, spread) + dot(low, spread)
    state = jnp.zeros((16, GROUP), F32)
    for j in range(BANDS):
        out[j] = state.astype(BF16)
        state = wide[j : j + 1] * state + arrived[j, :, pl.ds(0, GROUP)].astype(F32)


def relay(arrived):
    return pl.pallas_call(
        relay_kernel,
        out_shape=jax.ShapeDtypeStruct((BANDS, 16, GROUP), BF16),
        compiler_params=pltpu.CompilerParams(vmem_limit_bytes=4 * MIB),
        name="relay",
    )(arrived)


def columns_out(values, tokens, turned, out):
    values = values + tokens
    for k in range(HALF // 128):
        part = slice(k * 128, (k + 1) * 128)
        for r in range(ROWS):
            turned[k, pl.ds(r, 32, stride=ROWS), :] = values[r * 32 : (r + 1) * 32, part]
        out[:, part] = turned[k].astype(BF16)


def finish_kernel(
    local, gate, bcs, band_decay, entering, gain, tok, w, hidden, out, spread, state, decays, turned
):
    step = pl.program_id(0)

    @pl.when(step == 0)
    def _():
        spread[...] = head_spread(INNER, 0)
        state[pl.ds(0, STATE), :] = jnp.zeros((STATE, INNER), BF16)
        for a in range(4):
            for g in range(4):
                state[pl.ds(STATE + 16 * a, 16), pl.ds(g * GROUP, GROUP)] = entering[4 * a + g]
        for r in range(ROWS):
            decays[r] = two_terms(band_decay[:, r * LINE : (r + 1) * LINE])

    both = bcs[...].reshape(256, 128)
    here = pl.ds(pl.multiple_of(step * 32, 32), 32)
    decay = dot(decays[:, here, :].reshape(256, 2 * HEADS), spread[...])
    gated = local[...].reshape(256, INNER).astype(F32) + (
        dot(both, state[...]) * decay * gate[...].reshape(256, INNER).astype(F32)
    )
    normed = rms(gated, gain[...]).astype(BF16)
    hidden[...] = normed.reshape(ROWS, 32, INNER)
    columns_out(dot(normed, w[...]), tok[...].reshape(256, HALF).astype(F32), turned, out)


def finish(local, gate, bcs, band_decay, entering, gain, tok, w_out):
    cells = lambda n: pl.BlockSpec((ROWS, 32, n), lambda i: (0, i, 0))
    return pl.pallas_call(
        finish_kernel,
        grid=(LINE // 32,),
        in_specs=[
            cells(INNER),
            cells(INNER),
            cells(128),
            whole(HEADS, LENGTH),
            whole(BANDS, 16, GROUP),
            whole(1, INNER),
            cells(HALF),
            whole(INNER, HALF),
        ],
        out_specs=[cells(INNER), pl.BlockSpec((256, HALF), lambda i: (i, 0))],
        out_shape=[
            jax.ShapeDtypeStruct((ROWS, LINE, INNER), BF16),
            jax.ShapeDtypeStruct((LENGTH, HALF), BF16),
        ],
        scratch_shapes=[
            pltpu.VMEM((2 * HEADS, INNER), BF16),
            pltpu.VMEM((2 * STATE, INNER), BF16),
            pltpu.VMEM((ROWS, LINE, 2 * HEADS), BF16),
            pltpu.VMEM((HALF // 128, 256, 128), F32),
        ],
        compiler_params=params(24),
        cost_estimate=pl.CostEstimate(
            flops=2 * LENGTH * D * HALF, bytes_accessed=16 << 20, transcendentals=LENGTH
        ),
        name="finish",
    )(local, gate, bcs, band_decay, entering, gain, tok, w_out)


def rest_kernel(hidden, tok, w, out, turned):
    columns_out(
        dot(hidden[...].reshape(256, INNER), w[...]),
        tok[...].reshape(256, HALF).astype(F32),
        turned,
        out,
    )


def rest(hidden, tok, w_out):
    return pl.pallas_call(
        rest_kernel,
        grid=(LINE // 32,),
        in_specs=[
            pl.BlockSpec((ROWS, 32, INNER), lambda i: (0, i, 0)),
            pl.BlockSpec((ROWS, 32, HALF), lambda i: (0, i, 1)),
            pl.BlockSpec((INNER, HALF), lambda i: (0, 1), pipeline_mode=pl.Buffered(1)),
        ],
        out_specs=pl.BlockSpec((256, HALF), lambda i: (i, 0)),
        out_shape=jax.ShapeDtypeStruct((LENGTH, HALF), BF16),
        scratch_shapes=[pltpu.VMEM((HALF // 128, 256, 128), F32)],
        compiler_params=params(12),
        cost_estimate=pl.CostEstimate(flops=1 << 20, bytes_accessed=1 << 20, transcendentals=0),
        name="rest",
    )(hidden, tok, w_out)


def shards(
    tokens,
    in_gain,
    w_xbc,
    w_gate,
    w_dt,
    dt_bias,
    decay_rate,
    conv_w,
    conv_bias,
    skip,
    out_gain,
    w_out,
):
    bands = lax.axis_size("band")
    segments = lax.axis_size("segment")
    cells = tokens[0]
    tok = cells.reshape(LENGTH, D)
    top = lax.ppermute(cells[ROWS - 1], "band", [(i, i + 1) for i in range(bands - 1)])
    bottom = lax.ppermute(cells[0], "band", [(i + 1, i) for i in range(bands - 1)])

    xc, gate, bc, cum, dt, band_tail, band_decay, total = project(
        tok, in_gain, w_xbc[0], w_gate[0], w_dt[0].T, dt_bias.T, decay_rate.T
    )
    x, bcs, pieces = convolve(
        top, bottom, in_gain, w_xbc[0], xc, bc, conv_w.swapaxes(0, 1), conv_bias, band_tail, total
    )
    swap = functools.partial(
        lax.all_to_all, axis_name="band", split_axis=0, concat_axis=0, tiled=True
    )
    onward = functools.partial(
        lax.ppermute, axis_name="segment", perm=[(i, (i + 1) % segments) for i in range(segments)]
    )
    arrived = swap(pieces.reshape(BANDS, 16, GROUP + 128))
    local = scan(x, bcs, cum, dt, gate, skip.T)
    entering = swap(relay(arrived))

    grid = lambda a: a.reshape(ROWS, LINE, a.shape[-1])
    hidden, first = finish(
        grid(local), grid(gate), grid(bcs), band_decay, entering, out_gain, cells, w_out[0]
    )
    first = onward(first.reshape(BANDS, LENGTH // BANDS, HALF))
    second = swap(rest(hidden, cells, w_out[0]).reshape(BANDS, LENGTH // BANDS, HALF))
    first = swap(first)
    second = onward(second)
    both = jnp.concatenate([first, second], axis=-1)
    handed = both.reshape(BANDS, LINE // BANDS, ROWS, D).swapaxes(0, 1)
    return handed.reshape(1, LINE // BANDS, BANDS * ROWS, D)


def solution(mesh):
    in_specs = (
        P("segment", "band", None, None),
        P("segment", None),
        P("segment", None, None),
        P("segment", None, None),
        P("segment", None, None),
        P("segment", None),
        P("segment", None),
        P("segment", None, None),
        P("segment", None),
        P("segment", None),
        P("segment", None),
        P("segment", None, None),
    )
    out_specs = P("segment", "band", None, None)
    return jax.shard_map(shards, mesh=mesh, in_specs=in_specs, out_specs=out_specs, check_vma=False)
```

```python
import functools

import jax
import jax.numpy as jnp
from jax import lax
from jax.experimental import pallas as pl
from jax.experimental.pallas import tpu as pltpu
from jax.sharding import PartitionSpec as P

EPSILON = 1e-05
ROWS = 8
LINE = 128
LENGTH = ROWS * LINE
HEADS = 24
WIDTH = 64
STATE = 64
INNER = HEADS * WIDTH
D = 1536
HALF = D // 2
GROUP = 384
GROUP_HEADS = GROUP // WIDTH
BANDS = 16
F32 = jnp.float32
BF16 = jnp.bfloat16
MIB = 1 << 20
LOG2E = 1.4426950408889634


def params():
    return pltpu.CompilerParams(dimension_semantics=("arbitrary",), vmem_limit_bytes=60 * MIB)


def upright(row):
    return jnp.broadcast_to(row, (LINE, HEADS)).T[:, :1]


def whole(*shape):
    return pl.BlockSpec(shape, lambda i: (0,) * len(shape), pipeline_mode=pl.Buffered(1))


def dot(a, b):
    return jnp.dot(a, b, preferred_element_type=F32)


def rms(values, gain):
    return values * lax.rsqrt(jnp.mean(values * values, -1, keepdims=True) + EPSILON) * gain


def silu(v):
    half = 0.5 * v
    return half + half * jnp.tanh(half)


def head_spread(channels, first):
    head = lax.broadcasted_iota(jnp.int32, (2 * HEADS, channels), 0)
    head = jnp.where(head < HEADS, head, head - HEADS)
    channel = lax.broadcasted_iota(jnp.int32, (2 * HEADS, channels), 1)
    return jnp.where(head - first == channel // WIDTH, 1.0, 0.0).astype(BF16)


def two_terms(values_t):
    high = values_t.astype(BF16).astype(F32)
    return jnp.concatenate([high, values_t - high], axis=0).T.astype(BF16)


def place(r):
    return (r + 1) % ROWS * LINE


def fill(padded, tile, slot, line):
    padded[tile, slot, pl.ds(8, LINE), :] = line.astype(F32)


def convolved(padded, tile, slot, taps, bias):
    total = bias
    for i in range(3):
        for j in range(3):
            total = total + padded[tile, slot - 1 + i, pl.ds(7 + j, LINE), :] * taps[3 * i + j]
    return silu(total).astype(BF16)


def lanes(refs, k):
    return [ref[:, k * 128 : (k + 1) * 128] for ref in refs]


def project_kernel(
    tok,
    gain,
    w_x,
    w_g,
    w_bc,
    w_dt,
    dt_bias,
    rate,
    taps_x,
    taps_bc,
    bias_x,
    bias_bc,
    x,
    gate,
    rim,
    bcs,
    rim_bc,
    cum,
    dt,
    band_tail,
    band_decay,
    total,
    mid,
    normed,
    lines_a,
    lines_b,
    lines_bc,
    x_keep,
    b_t,
    tails,
    tok_here,
    w_g_here,
    tok_sem,
    w_g_sem,
):
    step = pl.program_id(0)

    def tokens_in(m):
        part = pl.ds(m * 256, 256)
        return pltpu.make_async_copy(tok.at[part, :], tok_here.at[part, :], tok_sem.at[m])

    def gate_in(n):
        return pltpu.make_async_copy(w_g.at[:, pl.ds(n * 512, 512)], w_g_here.at[n], w_g_sem.at[n])

    def store(m, values, padded, out, tiles):
        for n in range(m * 2, m * 2 + 2):
            line = values[(n - m * 2) * LINE : (n - m * 2 + 1) * LINE]
            for k in range(tiles):
                fill(padded, k, n, line[:, k * 128 : (k + 1) * 128])
            if n in (0, 1, 6, 7):
                out[pl.ds((n if n < 2 else n - 4) * LINE, LINE), :] = line

    def multiply_x(m, padded):
        here = normed[pl.ds(m * 256, 256), :]
        store(m, dot(here, w_x[...]).astype(BF16), padded, rim, 4)

    def multiply_gate(m, n):
        part = pl.ds(m * 256, 256)
        gate[part, :] = silu(dot(normed[part, :], w_g_here[n])).astype(BF16)

    def inside(k, padded, chunk):
        taps, bias = lanes([taps_x[n] for n in range(9)], k), bias_x[:, k * 128 : (k + 1) * 128]
        for r in range(1, ROWS - 1):
            values = convolved(padded, k, r, taps, bias)
            x[pl.ds(place(r), LINE), pl.ds(k * 128, 128)] = values
            x_keep[pl.ds((r - 1) * LINE, LINE), pl.ds(chunk * 512 + k * 128, 128)] = values

    def add_state(piece):
        part = pl.ds(piece * 256, 256)
        spread = head_spread(256, piece * 4)
        weighted = x_keep[:, part].astype(F32) * dot(tails[...], spread)
        mid[:, part] = dot(b_t[pl.ds(0, STATE), :], weighted.astype(BF16))

    @pl.when(step == 0)
    def _():
        for m in range(4):
            tokens_in(m).start()
        for padded in (lines_a, lines_b, lines_bc):
            for n in range(ROWS):
                for k in range(padded.shape[0]):
                    padded[k, n, pl.ds(0, 8), :] = jnp.zeros((8, 128), F32)
                    padded[k, n, pl.ds(LINE + 8, 8), :] = jnp.zeros((8, 128), F32)
        for m in range(4):
            tokens_in(m).wait()
            part = pl.ds(m * 256, 256)
            here = rms(tok_here[part, :].astype(F32), gain[...]).astype(BF16)
            normed[part, :] = here
            store(m, dot(here, w_bc[...]).astype(BF16), lines_bc, rim_bc, 1)
            store(m, dot(here, w_x[...]).astype(BF16), lines_a, rim, 4)
        for n in range(3):
            gate_in(n).start()

    @pl.when(step == 1)
    def _():
        taps = [taps_bc[n] for n in range(9)]
        for r in range(1, ROWS - 1):
            values = convolved(lines_bc, 0, r, taps, bias_bc[...])
            bcs[pl.ds(place(r), LINE), :] = values
            b_t[:, pl.ds((r - 1) * LINE, LINE)] = values.astype(F32).T.astype(BF16)
        raw = lax.dot_general(
            w_dt[...], normed[...], (((1,), (1,)), ((), ())), preferred_element_type=F32
        ) + upright(dt_bias[...])
        dt[...] = jnp.maximum(raw, 0.0) + jnp.log1p(jnp.exp(-jnp.abs(raw)))
        for m in range(4):
            multiply_x(m, lines_b)
            inside(m, lines_a, 0)

    @pl.when(step == 2)
    def _():
        steps = dt[...]
        log_decay = -upright(rate[...]) * steps
        i = lax.broadcasted_iota(jnp.int32, (LINE, LINE), 0)
        j = lax.broadcasted_iota(jnp.int32, (LINE, LINE), 1)
        sums = jnp.dot(
            jnp.concatenate([log_decay[:, r * LINE : (r + 1) * LINE] for r in range(ROWS)], axis=0),
            jnp.where(i <= j, 1.0, 0.0).astype(F32),
            precision=lax.Precision.HIGHEST,
            preferred_element_type=F32,
        )
        lines = [sums[r * HEADS : (r + 1) * HEADS] for r in range(ROWS)]
        ends = [line[:, LINE - 1 :] for line in lines]
        before = [jnp.zeros_like(ends[0])]
        after = [jnp.zeros_like(ends[0])]
        for r in range(ROWS - 1):
            before.append(before[-1] + ends[r])
            after.append(after[-1] + ends[ROWS - 1 - r])
        for r in range(ROWS):
            part = slice(r * LINE, (r + 1) * LINE)
            cum[:, part] = lines[r]
            band_decay[:, part] = jnp.exp(lines[r] + before[r])
            tail = steps[:, part] * jnp.exp((ends[r] - lines[r]) + after[ROWS - 1 - r])
            band_tail[:, part] = tail
            if 0 < r < ROWS - 1:
                tails[pl.ds((r - 1) * LINE, LINE), :] = two_terms(tail)
        total[...] = jnp.broadcast_to(before[-1] + ends[-1], (HEADS, LINE)).T[:1]
        for m in range(4):
            multiply_x(m, lines_a)
            inside(m, lines_b, 1)

    @pl.when(step == 3)
    def _():
        gate_in(0).wait()
        for m in range(4):
            multiply_gate(m, 0)
            inside(m, lines_a, 2)

    for late in (4, 5):

        @pl.when(step == late)
        def _():
            gate_in(late - 3).wait()
            for m in range(4):
                multiply_gate(m, late - 3)
                if m < 3:
                    add_state((late - 4) * 3 + m)


def project(tok, gain, w_xbc, w_gate, w_dt_t, dt_bias, rate, taps, conv_bias):
    per_head = jax.ShapeDtypeStruct((HEADS, LENGTH), F32)
    first = lambda i: (0, jnp.minimum(i, 2))
    second = lambda i: (0, jnp.maximum(i - 3, 0))
    behind = lambda i: jnp.clip(i - 1, 0, 2)
    last = INNER // 128
    return pl.pallas_call(
        project_kernel,
        grid=(6,),
        in_specs=[
            pl.BlockSpec(memory_space=pl.ANY),
            whole(1, D),
            pl.BlockSpec((D, 512), first),
            pl.BlockSpec(memory_space=pl.ANY),
            pl.BlockSpec((D, 128), lambda i: (0, last), pipeline_mode=pl.Buffered(1)),
            whole(HEADS, D),
            whole(1, HEADS),
            whole(1, HEADS),
            pl.BlockSpec((9, 1, 512), lambda i: (0, 0, behind(i))),
            pl.BlockSpec((9, 1, 128), lambda i: (0, 0, last)),
            pl.BlockSpec((1, 512), lambda i: (0, behind(i))),
            pl.BlockSpec((1, 128), lambda i: (0, last)),
        ],
        out_specs=[
            pl.BlockSpec((LENGTH, 512), lambda i: (0, behind(i))),
            pl.BlockSpec((LENGTH, 512), second),
            pl.BlockSpec((4 * LINE, 512), first),
            whole(LENGTH, 128),
            whole(4 * LINE, 128),
            whole(HEADS, LENGTH),
            whole(HEADS, LENGTH),
            whole(HEADS, LENGTH),
            whole(HEADS, LENGTH),
            whole(1, HEADS),
            whole(STATE, INNER),
        ],
        out_shape=[
            jax.ShapeDtypeStruct((LENGTH, INNER), BF16),
            jax.ShapeDtypeStruct((LENGTH, INNER), BF16),
            jax.ShapeDtypeStruct((4 * LINE, INNER), BF16),
            jax.ShapeDtypeStruct((LENGTH, 128), BF16),
            jax.ShapeDtypeStruct((4 * LINE, 128), BF16),
            per_head,
            per_head,
            per_head,
            per_head,
            jax.ShapeDtypeStruct((1, HEADS), F32),
            jax.ShapeDtypeStruct((STATE, INNER), F32),
        ],
        scratch_shapes=[
            pltpu.VMEM((LENGTH, D), BF16),
            pltpu.VMEM((4, ROWS, LINE + 16, 128), F32),
            pltpu.VMEM((4, ROWS, LINE + 16, 128), F32),
            pltpu.VMEM((1, ROWS, LINE + 16, 128), F32),
            pltpu.VMEM(((ROWS - 2) * LINE, INNER), BF16),
            pltpu.VMEM((128, (ROWS - 2) * LINE), BF16),
            pltpu.VMEM(((ROWS - 2) * LINE, 2 * HEADS), BF16),
            pltpu.VMEM((LENGTH, D), BF16),
            pltpu.VMEM((3, D, 512), BF16),
            pltpu.SemaphoreType.DMA((4,)),
            pltpu.SemaphoreType.DMA((3,)),
        ],
        compiler_params=params(),
        cost_estimate=pl.CostEstimate(
            flops=2 * LENGTH * D * 3224, bytes_accessed=20 << 20, transcendentals=LENGTH * INNER
        ),
        name="project",
    )(tok, gain, w_xbc, w_gate, w_xbc, w_dt_t, dt_bias, rate, taps, taps, conv_bias, conv_bias)


def edge_kernel(
    top,
    bottom,
    gain,
    w_x,
    w_bc,
    rim,
    rim_bc,
    taps_x,
    taps_bc,
    bias_x,
    bias_bc,
    band_tail,
    total,
    mid,
    x_in,
    bcs_in,
    x,
    bcs,
    pieces,
    edge,
    lines,
    b_t,
    tails,
):
    del x_in, bcs_in
    g = pl.program_id(0)

    def both(side, own, taps, bias, out, tiles):
        for k in range(tiles):
            part = slice(k * 128, (k + 1) * 128)
            for slot, line in enumerate(
                [side[:LINE], own[pl.ds(0, LINE), :], own[pl.ds(LINE, LINE), :]]
                + [own[pl.ds(2 * LINE, LINE), :], own[pl.ds(3 * LINE, LINE), :], side[LINE:]]
            ):
                fill(lines, k, slot, line[:, part])
            for slot, r in ((1, 0), (4, ROWS - 1)):
                out[pl.ds(place(r), LINE), part] = convolved(lines, k, slot, lanes(taps, k), bias[:, part])

    @pl.when(g == 0)
    def _():
        for slot in range(6):
            for k in range(GROUP // 128):
                lines[k, slot, pl.ds(0, 8), :] = jnp.zeros((8, 128), F32)
                lines[k, slot, pl.ds(LINE + 8, 8), :] = jnp.zeros((8, 128), F32)
        edge[pl.ds(0, LINE), :] = rms(top[...].astype(F32), gain[...]).astype(BF16)
        edge[pl.ds(LINE, LINE), :] = rms(bottom[...].astype(F32), gain[...]).astype(BF16)
        both(
            dot(edge[...], w_bc[...]).astype(BF16),
            rim_bc,
            [taps_bc[k] for k in range(9)],
            bias_bc[...],
            bcs,
            1,
        )
        b_t[...] = bcs[...].astype(F32).T.astype(BF16)
        tails[pl.ds(place(0), LINE), :] = two_terms(band_tail[:, :LINE])
        tails[pl.ds(place(ROWS - 1), LINE), :] = two_terms(band_tail[:, LENGTH - LINE :])

    both(
        dot(edge[...], w_x[...]).astype(BF16),
        rim,
        [taps_x[k] for k in range(9)],
        bias_x[...],
        x,
        GROUP // 128,
    )
    weighted = x[...].astype(F32) * dot(tails[...], head_spread(GROUP, g * GROUP_HEADS))
    state = mid[...] + dot(b_t[pl.ds(0, STATE), :], weighted.astype(BF16))
    head = lax.broadcasted_iota(jnp.int32, (HEADS, 128), 0)
    lane = lax.broadcasted_iota(jnp.int32, (HEADS, 128), 1)
    pick = jnp.where(head == lane + g * GROUP_HEADS, 1.0, 0.0).astype(BF16)
    first = total[...].astype(BF16)
    rest = total[...] - first.astype(F32)
    second = rest.astype(BF16)
    third = (rest - second.astype(F32)).astype(BF16)
    terms = jnp.concatenate(
        [dot(jnp.broadcast_to(t, (8, HEADS)), pick)[:1] for t in (first, second, third)]
        + [jnp.zeros((13, 128), F32)],
        axis=0,
    ).astype(BF16)
    for a in range(4):
        pieces[a, 0, :, pl.ds(0, GROUP)] = state[16 * a : 16 * a + 16].astype(BF16)
        pieces[a, 0, :, pl.ds(GROUP, 128)] = terms


def edges(top, bottom, gain, w_xbc, rim, rim_bc, taps, conv_bias, band_tail, total, mid, x, bcs):
    last = INNER // 128
    return pl.pallas_call(
        edge_kernel,
        grid=(4,),
        in_specs=[
            whole(LINE, D),
            whole(LINE, D),
            whole(1, D),
            pl.BlockSpec((D, GROUP), lambda i: (0, i)),
            pl.BlockSpec((D, 128), lambda i: (0, last), pipeline_mode=pl.Buffered(1)),
            pl.BlockSpec((4 * LINE, GROUP), lambda i: (0, i)),
            whole(4 * LINE, 128),
            pl.BlockSpec((9, 1, GROUP), lambda i: (0, 0, i)),
            pl.BlockSpec((9, 1, 128), lambda i: (0, 0, last)),
            pl.BlockSpec((1, GROUP), lambda i: (0, i)),
            pl.BlockSpec((1, 128), lambda i: (0, last)),
            whole(HEADS, LENGTH),
            whole(1, HEADS),
            pl.BlockSpec((STATE, GROUP), lambda i: (0, i)),
            pl.BlockSpec(memory_space=pl.ANY),
            pl.BlockSpec(memory_space=pl.ANY),
        ],
        out_specs=[
            pl.BlockSpec((2 * LINE, GROUP), lambda i: (0, i)),
            whole(2 * LINE, 128),
            pl.BlockSpec((4, 1, 16, GROUP + 128), lambda i: (0, i, 0, 0)),
        ],
        out_shape=[
            jax.ShapeDtypeStruct((LENGTH, INNER), BF16),
            jax.ShapeDtypeStruct((LENGTH, 128), BF16),
            jax.ShapeDtypeStruct((4, 4, 16, GROUP + 128), BF16),
        ],
        input_output_aliases={14: 0, 15: 1},
        scratch_shapes=[
            pltpu.VMEM((2 * LINE, D), BF16),
            pltpu.VMEM((GROUP // 128, 6, LINE + 16, 128), F32),
            pltpu.VMEM((128, 2 * LINE), BF16),
            pltpu.VMEM((2 * LINE, 2 * HEADS), BF16),
        ],
        compiler_params=params(),
        cost_estimate=pl.CostEstimate(
            flops=2 * 256 * D * 1664 + 10 * LENGTH * 1664,
            bytes_accessed=10 << 20,
            transcendentals=256 * 1664,
        ),
        name="edges",
    )(
        top,
        bottom,
        gain,
        w_xbc,
        w_xbc,
        rim,
        rim_bc,
        taps,
        taps,
        conv_bias,
        conv_bias,
        band_tail,
        total,
        mid,
        x,
        bcs,
    )


def scan_kernel(
    half, x_even, x_odd, bcs, cum, dt, gate, skip, out, direct, state, sums, steps, weights, b_t, c
):
    lane = lax.broadcasted_iota(jnp.int32, (LINE, LINE), 1)
    left = lane < WIDTH

    @pl.when(pl.program_id(0) == 0)
    def _():
        direct[...] = dot(
            two_terms(jnp.broadcast_to(upright(skip[...]), (HEADS, 8))),
            head_spread(HALF, half * HEADS // 2),
        )
        state[...] = jnp.zeros_like(state)
        row = lax.broadcasted_iota(jnp.int32, (LINE, LINE), 0)
        for r in range(ROWS):
            part = slice(r * LINE, (r + 1) * LINE)
            sums[r] = (cum[:, part] * LOG2E).T
            steps[r] = dt[:, part].T
            both = bcs[pl.ds(place(r), LINE), :].astype(F32)
            b_t[r] = both.T.astype(BF16)[:STATE]
            c[r] = pltpu.roll(both, STATE, 1).astype(BF16)[:, :STATE]
        for r in range(ROWS):
            weights[r] = jnp.where(row >= lane, dot(c[r], b_t[r]), 0.0)

    def line(r, x, out_part):
        sums_here, steps_here, weights_here = sums[r], steps[r], weights[r]
        columns_t = pl.ds(pl.multiple_of(r * LINE, LINE), LINE)
        sums_t = cum[:, columns_t] * LOG2E
        steps_t = dt[:, columns_t]

        def mixing(h):
            along = jnp.broadcast_to(sums_here[:, h : h + 1], (LINE, LINE))
            decay = jnp.exp2(jnp.minimum(along - sums_t[h : h + 1], 0.0))
            return along, (decay * (weights_here * steps_t[h : h + 1])).astype(BF16)

        for q in range(HEADS // 8):
            quad = pl.ds(q * 256, 256)
            carried = dot(c[r], state[:, quad].astype(BF16))
            tails, decays = [], []
            for p in (2 * q, 2 * q + 1):
                part = pl.ds(p * 128, 128)
                h = half * HEADS // 2 + 2 * p
                values = x[:, part].astype(F32)
                (along_a, mixing_a), (along_b, mixing_b) = mixing(h), mixing(h + 1)
                columns = jnp.concatenate(
                    [jnp.where(left, values, 0.0), jnp.where(left, 0.0, values)], axis=0
                ).astype(BF16)
                inner = dot(jnp.concatenate([mixing_a, mixing_b], axis=1), columns)
                here = jnp.where(left, along_a, along_b)
                carry = jnp.exp2(here)
                stepped = jnp.where(left, steps_here[:, h : h + 1], steps_here[:, h + 1 : h + 2])
                tails.append((values * stepped * jnp.exp2(here[LINE - 1 :] - here)).astype(BF16))
                decays.append(carry[LINE - 1 :])
                side = slice((p % 2) * 128, (p % 2) * 128 + 128)
                y = inner + carry * carried[:, side] + direct[0:1, part] * values
                out[out_part, part] = (y * gate[out_part, part].astype(F32)).astype(BF16)
            state[:, quad] = jnp.concatenate(decays, axis=1) * state[:, quad] + dot(
                b_t[r], jnp.concatenate(tails, axis=1)
            )

    first = pl.program_id(0) * 2
    line(first, x_even, pl.ds(0, LINE))
    line(first + 1, x_odd, pl.ds(LINE, LINE))


def scan(half, x, bcs, cum, dt, gate, skip):
    return pl.pallas_call(
        functools.partial(scan_kernel, half),
        grid=(ROWS // 2,),
        in_specs=[
            pl.BlockSpec((LINE, HALF), lambda i: ((2 * i + 1) % ROWS, half)),
            pl.BlockSpec((LINE, HALF), lambda i: ((2 * i + 2) % ROWS, half)),
            whole(LENGTH, 128),
            whole(HEADS, LENGTH),
            whole(HEADS, LENGTH),
            pl.BlockSpec((2 * LINE, HALF), lambda i: (i, half)),
            whole(1, HEADS),
        ],
        out_specs=pl.BlockSpec((2 * LINE, HALF), lambda i: (i, 0)),
        out_shape=jax.ShapeDtypeStruct((LENGTH, HALF), BF16),
        scratch_shapes=[
            pltpu.VMEM((8, HALF), F32),
            pltpu.VMEM((STATE, HALF), F32),
            pltpu.VMEM((ROWS, LINE, HEADS), F32),
            pltpu.VMEM((ROWS, LINE, HEADS), F32),
            pltpu.VMEM((ROWS, LINE, LINE), F32),
            pltpu.VMEM((ROWS, STATE, LINE), BF16),
            pltpu.VMEM((ROWS, LINE, STATE), BF16),
        ],
        compiler_params=params(),
        cost_estimate=pl.CostEstimate(
            flops=2 << 30, bytes_accessed=5 << 20, transcendentals=LENGTH * LINE * HEADS // 2
        ),
        name="scan",
    )(x, x, bcs, cum, dt, gate, skip)


def relay_kernel(arrived, out):
    logs = jnp.concatenate(
        [
            jnp.sum(arrived[j, :, pl.ds(GROUP, 128)].astype(F32), axis=0, keepdims=True)
            for j in range(BANDS)
        ],
        axis=0,
    )
    decay = jnp.exp(logs)
    high = decay.astype(BF16)
    low = (decay - high.astype(F32)).astype(BF16)
    lane = lax.broadcasted_iota(jnp.int32, (128, GROUP), 0)
    channel = lax.broadcasted_iota(jnp.int32, (128, GROUP), 1)
    spread = jnp.where(lane == channel // WIDTH, 1.0, 0.0).astype(BF16)
    wide = dot(high, spread) + dot(low, spread)
    state = jnp.zeros((16, GROUP), F32)
    for j in range(BANDS):
        out[j] = state.astype(BF16)
        state = wide[j : j + 1] * state + arrived[j, :, pl.ds(0, GROUP)].astype(F32)


def relay(arrived):
    return pl.pallas_call(
        relay_kernel,
        out_shape=jax.ShapeDtypeStruct((BANDS, 16, GROUP), BF16),
        compiler_params=pltpu.CompilerParams(vmem_limit_bytes=60 * MIB),
        name="relay",
    )(arrived)


def columns_out(values, tokens, turned, out):
    values = values + tokens
    for k in range(HALF // 128):
        part = slice(k * 128, (k + 1) * 128)
        for r in range(ROWS):
            turned[k, pl.ds(r, 32, stride=ROWS), :] = values[r * 32 : (r + 1) * 32, part]
        out[:, part] = turned[k].astype(BF16)


def finish_kernel(
    local_a, local_b, gate, bcs, band_decay, entering, gain, tok, w, hidden, out, spread, state, decays, turned
):
    step = pl.program_id(0)

    @pl.when(step == 0)
    def _():
        spread[...] = head_spread(INNER, 0)
        state[pl.ds(0, STATE), :] = jnp.zeros((STATE, INNER), BF16)
        for a in range(4):
            for g in range(4):
                state[pl.ds(STATE + 16 * a, 16), pl.ds(g * GROUP, GROUP)] = entering[4 * a + g]
        for r in range(ROWS):
            decays[r] = two_terms(band_decay[:, r * LINE : (r + 1) * LINE])

    both = jnp.concatenate([bcs[1:], bcs[:1]], axis=0).reshape(256, 128)
    here = pl.ds(pl.multiple_of(step * 32, 32), 32)
    decay = dot(decays[:, here, :].reshape(256, 2 * HEADS), spread[...])
    local = jnp.concatenate([local_a[...], local_b[...]], axis=2)
    gated = local.reshape(256, INNER).astype(F32) + (
        dot(both, state[...]) * decay * gate[...].reshape(256, INNER).astype(F32)
    )
    normed = rms(gated, gain[...]).astype(BF16)
    hidden[...] = normed.reshape(ROWS, 32, INNER)
    columns_out(dot(normed, w[...]), tok[...].reshape(256, HALF).astype(F32), turned, out)


def finish(local_a, local_b, gate, bcs, band_decay, entering, gain, tok, w_out):
    cells = lambda n: pl.BlockSpec((ROWS, 32, n), lambda i: (0, i, 0))
    return pl.pallas_call(
        finish_kernel,
        grid=(LINE // 32,),
        in_specs=[
            cells(HALF),
            cells(HALF),
            cells(INNER),
            cells(128),
            whole(HEADS, LENGTH),
            whole(BANDS, 16, GROUP),
            whole(1, INNER),
            cells(HALF),
            whole(INNER, HALF),
        ],
        out_specs=[cells(INNER), pl.BlockSpec((256, HALF), lambda i: (i, 0))],
        out_shape=[
            jax.ShapeDtypeStruct((ROWS, LINE, INNER), BF16),
            jax.ShapeDtypeStruct((LENGTH, HALF), BF16),
        ],
        scratch_shapes=[
            pltpu.VMEM((2 * HEADS, INNER), BF16),
            pltpu.VMEM((2 * STATE, INNER), BF16),
            pltpu.VMEM((ROWS, LINE, 2 * HEADS), BF16),
            pltpu.VMEM((HALF // 128, 256, 128), F32),
        ],
        compiler_params=params(),
        cost_estimate=pl.CostEstimate(
            flops=2 * LENGTH * D * HALF, bytes_accessed=16 << 20, transcendentals=LENGTH
        ),
        name="finish",
    )(local_a, local_b, gate, bcs, band_decay, entering, gain, tok, w_out)


def rest_kernel(hidden, tok, w, out, turned):
    columns_out(
        dot(hidden[...].reshape(256, INNER), w[...]),
        tok[...].reshape(256, HALF).astype(F32),
        turned,
        out,
    )


def rest(hidden, tok, w_out):
    return pl.pallas_call(
        rest_kernel,
        grid=(LINE // 32,),
        in_specs=[
            pl.BlockSpec((ROWS, 32, INNER), lambda i: (0, i, 0)),
            pl.BlockSpec((ROWS, 32, HALF), lambda i: (0, i, 1)),
            pl.BlockSpec((INNER, HALF), lambda i: (0, 1), pipeline_mode=pl.Buffered(1)),
        ],
        out_specs=pl.BlockSpec((256, HALF), lambda i: (i, 0)),
        out_shape=jax.ShapeDtypeStruct((LENGTH, HALF), BF16),
        scratch_shapes=[pltpu.VMEM((HALF // 128, 256, 128), F32)],
        compiler_params=params(),
        cost_estimate=pl.CostEstimate(flops=1 << 20, bytes_accessed=1 << 20, transcendentals=0),
        name="rest",
    )(hidden, tok, w_out)


def shards(
    tokens,
    in_gain,
    w_xbc,
    w_gate,
    w_dt,
    dt_bias,
    decay_rate,
    conv_w,
    conv_bias,
    skip,
    out_gain,
    w_out,
):
    bands = lax.axis_size("band")
    segments = lax.axis_size("segment")
    cells = tokens[0]
    tok = cells.reshape(LENGTH, D)
    top = lax.ppermute(cells[ROWS - 1], "band", [(i, i + 1) for i in range(bands - 1)])
    bottom = lax.ppermute(cells[0], "band", [(i + 1, i) for i in range(bands - 1)])

    taps = conv_w.swapaxes(0, 1)
    x, gate, rim, bcs, rim_bc, cum, dt, band_tail, band_decay, total, mid = project(
        tok, in_gain, w_xbc[0], w_gate[0], w_dt[0].T, dt_bias, decay_rate, taps, conv_bias
    )
    x, bcs, pieces = edges(
        top, bottom, in_gain, w_xbc[0], rim, rim_bc, taps, conv_bias, band_tail, total, mid, x, bcs
    )
    swap = functools.partial(
        lax.all_to_all, axis_name="band", split_axis=0, concat_axis=0, tiled=True
    )
    onward = functools.partial(
        lax.ppermute, axis_name="segment", perm=[(i, (i + 1) % segments) for i in range(segments)]
    )
    arrived = swap(pieces.reshape(BANDS, 16, GROUP + 128))
    local_a = scan(0, x, bcs, cum, dt, gate, skip)
    arrived, local_a = lax.optimization_barrier((arrived, local_a))
    states = relay(arrived)
    states, x_b = lax.optimization_barrier((states, x))
    entering = swap(states)
    local_b = scan(1, x_b, bcs, cum, dt, gate, skip)

    grid = lambda a: a.reshape(ROWS, LINE, a.shape[-1])
    hidden, first = finish(
        grid(local_a), grid(local_b), grid(gate), grid(bcs), band_decay, entering, out_gain, cells, w_out[0]
    )
    first = swap(first.reshape(BANDS, LENGTH // BANDS, HALF))
    second = onward(rest(hidden, cells, w_out[0]).reshape(BANDS, LENGTH // BANDS, HALF))
    second = swap(second)
    first = onward(first)
    both = jnp.concatenate([first, second], axis=-1)
    handed = both.reshape(BANDS, LINE // BANDS, ROWS, D).swapaxes(0, 1)
    return handed.reshape(1, LINE // BANDS, BANDS * ROWS, D)


def solution(mesh):
    in_specs = (
        P("segment", "band", None, None),
        P("segment", None),
        P("segment", None, None),
        P("segment", None, None),
        P("segment", None, None),
        P("segment", None),
        P("segment", None),
        P("segment", None, None),
        P("segment", None),
        P("segment", None),
        P("segment", None),
        P("segment", None, None),
    )
    out_specs = P("segment", "band", None, None)
    return jax.shard_map(shards, mesh=mesh, in_specs=in_specs, out_specs=out_specs, check_vma=False)
```

```python
import functools

import jax
import jax.numpy as jnp
from jax import lax
from jax.experimental import pallas as pl
from jax.experimental.pallas import tpu as pltpu
from jax.sharding import PartitionSpec as P

EPSILON = 1e-05
ROWS = 8
LINE = 128
LENGTH = ROWS * LINE
HEADS = 24
WIDTH = 64
STATE = 64
INNER = HEADS * WIDTH
D = 1536
HALF = INNER // 2
FIRST = 896
GROUP = 384
GROUP_HEADS = GROUP // WIDTH
BANDS = 16
F32 = jnp.float32
BF16 = jnp.bfloat16
MIB = 1 << 20
LOG2E = 1.4426950408889634


def params(mib=24):
    return pltpu.CompilerParams(vmem_limit_bytes=mib * MIB)


kept = pl.BlockSpec(memory_space=pltpu.VMEM)
far = pl.BlockSpec(memory_space=pl.ANY)


def small(*shape):
    return pl.BlockSpec(shape, lambda *i: (0,) * len(shape))


def near(a):
    return pltpu.with_memory_space_constraint(a, pltpu.VMEM)


def hbm(a):
    return pltpu.with_memory_space_constraint(a, pltpu.HBM)


def upright(row):
    return jnp.broadcast_to(row, (LINE, HEADS)).T[:, :1]


def whole(*shape):
    return pl.BlockSpec(shape, lambda i: (0,) * len(shape), pipeline_mode=pl.Buffered(1))


def dot(a, b):
    return jnp.dot(a, b, preferred_element_type=F32)


def rms(values, gain):
    return values * lax.rsqrt(jnp.mean(values * values, -1, keepdims=True) + EPSILON) * gain


def silu(v):
    half = 0.5 * v
    return half + half * jnp.tanh(half)


def head_spread(channels, first):
    head = lax.broadcasted_iota(jnp.int32, (2 * HEADS, channels), 0)
    head = jnp.where(head < HEADS, head, head - HEADS)
    channel = lax.broadcasted_iota(jnp.int32, (2 * HEADS, channels), 1)
    return jnp.where(head - first == channel // WIDTH, 1.0, 0.0).astype(BF16)


def two_terms(values_t):
    high = values_t.astype(BF16).astype(F32)
    return jnp.concatenate([high, values_t - high], axis=0).T.astype(BF16)


def place(r):
    return (r + 1) % ROWS * LINE


def fill(padded, tile, slot, line):
    padded[tile, slot, pl.ds(8, LINE), :] = line.astype(F32)


def convolved(padded, tile, slot, taps, bias):
    total = bias
    for i in range(3):
        for j in range(3):
            total = total + padded[tile, slot - 1 + i, pl.ds(7 + j, LINE), :] * taps[3 * i + j]
    return silu(total).astype(BF16)


def lanes(refs, start):
    return [ref[:, start : start + 128] for ref in refs]


def project_kernel(
    tok,
    gain,
    w_xbc,
    w_g,
    w_dt,
    dt_bias,
    rate,
    taps_ref,
    bias,
    skip,
    out_gain,
    x,
    gate,
    rim,
    bcs,
    rim_bc,
    cum,
    dt,
    band_tail,
    band_decay,
    total,
    mid,
    w_near,
    tok_near,
    gain_near,
    taps_near,
    bias_near,
    skip_near,
    out_gain_near,
    normed,
    lines_a,
    lines_b,
    lines_bc,
    b_t,
    tails,
    w_g_near,
    tok_sem,
    w_sem,
    w_g_sem,
):
    def tokens_in(m):
        part = pl.ds(m * 256, 256)
        return pltpu.make_async_copy(tok.at[part, :], tok_near.at[part, :], tok_sem.at[m])

    def w_in(n):
        part = pl.ds(n * 512, 512 if n < 3 else 128)
        return pltpu.make_async_copy(w_xbc.at[:, part], w_near.at[:, part], w_sem.at[n])

    def gate_in(n):
        part = pl.ds(n * 512, 512)
        return pltpu.make_async_copy(w_g.at[:, part], w_g_near.at[:, part], w_g_sem.at[n])

    taps = [taps_ref[n] for n in range(9)]

    def store(m, values, padded, out, start, tiles, tile=0):
        for n in range(m * 2, m * 2 + 2):
            line = values[(n - m * 2) * LINE : (n - m * 2 + 1) * LINE]
            for k in range(tiles):
                fill(padded, tile + k, n, line[:, k * 128 : (k + 1) * 128])
            if n in (0, 1, 6, 7):
                place_n = (n if n < 2 else n - 4) * LINE
                out[pl.ds(place_n, LINE), pl.ds(start, tiles * 128)] = line

    def multiply_x(m, here, padded, chunk, side):
        start = chunk * 512 + side * 256
        values = dot(here, w_near[:, pl.ds(start, 256)]).astype(BF16)
        store(m, values, padded, rim, start, 2, side * 2)

    def multiply_gate(m, n, side):
        rows, part = pl.ds(m * 256, 256), pl.ds(n * 512 + side * 256, 256)
        gate[rows, part] = silu(dot(normed[rows, :], w_g_near[:, part])).astype(BF16)

    def inside(k, padded, chunk, rows):
        start = chunk * 512 + k * 128
        for r in rows:
            x[pl.ds(place(r), LINE), pl.ds(start, 128)] = convolved(
                padded, k, r, lanes(taps, start), bias[:, start : start + 128]
            )

    def add_state(piece):
        part = pl.ds(piece * 256, 256)
        spread = head_spread(256, piece * 4)
        own = x[pl.ds(2 * LINE, (ROWS - 2) * LINE), part].astype(F32)
        mid[:, part] = dot(b_t[pl.ds(0, STATE), :], (own * dot(tails[...], spread)).astype(BF16))

    tokens_in(0).start()
    w_in(3).start()
    w_in(0).start()
    for m in range(1, 4):
        tokens_in(m).start()
    w_in(1).start()
    w_in(2).start()
    for n in range(3):
        gate_in(n).start()
    gain_near[...] = gain[...]
    taps_near[...] = taps_ref[...]
    bias_near[...] = bias[...]
    skip_near[...] = skip[...]
    out_gain_near[...] = out_gain[...]
    for padded in (lines_a, lines_b, lines_bc):
        for n in range(ROWS):
            for k in range(padded.shape[0]):
                padded[k, n, pl.ds(0, 8), :] = jnp.zeros((8, 128), F32)
                padded[k, n, pl.ds(LINE + 8, 8), :] = jnp.zeros((8, 128), F32)
    for m in range(4):
        tokens_in(m).wait()
        if m == 0:
            w_in(3).wait()
            w_in(0).wait()
        part = pl.ds(m * 256, 256)
        here = rms(tok_near[part, :].astype(F32), gain[...]).astype(BF16)
        normed[part, :] = here
        store(m, dot(here, w_near[:, pl.ds(INNER, 128)]).astype(BF16), lines_bc, rim_bc, 0, 1)
        for side in range(2):
            multiply_x(m, here, lines_a, 0, side)

    w_in(1).wait()
    for r in range(1, ROWS - 1):
        values = convolved(
            lines_bc, 0, r, lanes(taps, INNER), bias[:, INNER : INNER + 128]
        )
        bcs[pl.ds(place(r), LINE), :] = values
        b_t[:, pl.ds((r - 1) * LINE, LINE)] = values.astype(F32).T.astype(BF16)
    raw = lax.dot_general(
        w_dt[...], normed[...], (((1,), (1,)), ((), ())), preferred_element_type=F32
    ) + upright(dt_bias[...])
    steps = jnp.maximum(raw, 0.0) + jnp.log1p(jnp.exp(-jnp.abs(raw)))
    dt[...] = steps
    for m in range(4):
        for side in range(2):
            multiply_x(m, normed[pl.ds(m * 256, 256), :], lines_b, 1, side)
            inside(m, lines_a, 0, range(1 + 3 * side, 4 + 3 * side))

    w_in(2).wait()
    log_decay = -upright(rate[...]) * steps
    i = lax.broadcasted_iota(jnp.int32, (LINE, LINE), 0)
    j = lax.broadcasted_iota(jnp.int32, (LINE, LINE), 1)
    sums = jnp.dot(
        jnp.concatenate([log_decay[:, r * LINE : (r + 1) * LINE] for r in range(ROWS)], axis=0),
        jnp.where(i <= j, 1.0, 0.0).astype(F32),
        precision=lax.Precision.HIGHEST,
        preferred_element_type=F32,
    )
    lines = [sums[r * HEADS : (r + 1) * HEADS] for r in range(ROWS)]
    ends = [line[:, LINE - 1 :] for line in lines]
    before = [jnp.zeros_like(ends[0])]
    after = [jnp.zeros_like(ends[0])]
    for r in range(ROWS - 1):
        before.append(before[-1] + ends[r])
        after.append(after[-1] + ends[ROWS - 1 - r])
    for r in range(ROWS):
        part = slice(r * LINE, (r + 1) * LINE)
        cum[:, part] = lines[r]
        band_decay[:, part] = jnp.exp(lines[r] + before[r])
        tail = steps[:, part] * jnp.exp((ends[r] - lines[r]) + after[ROWS - 1 - r])
        band_tail[:, part] = tail
        if 0 < r < ROWS - 1:
            tails[pl.ds((r - 1) * LINE, LINE), :] = two_terms(tail)
    total[...] = jnp.broadcast_to(before[-1] + ends[-1], (HEADS, LINE)).T[:1]
    for m in range(4):
        for side in range(2):
            multiply_x(m, normed[pl.ds(m * 256, 256), :], lines_a, 2, side)
            inside(m, lines_b, 1, range(1 + 3 * side, 4 + 3 * side))

    gate_in(0).wait()
    for m in range(4):
        for side in range(2):
            multiply_gate(m, 0, side)
            inside(m, lines_a, 2, range(1 + 3 * side, 4 + 3 * side))
    for n in (1, 2):
        gate_in(n).wait()
        for m in range(4):
            for side in range(2):
                multiply_gate(m, n, side)
            if m < 3:
                add_state((n - 1) * 3 + m)


def project(tok, gain, w_xbc, w_gate, w_dt_t, dt_bias, rate, taps, conv_bias, skip, out_gain):
    per_head = pltpu.VMEM((HEADS, LENGTH), F32)
    return pl.pallas_call(
        project_kernel,
        in_specs=[
            far,
            small(1, D),
            far,
            far,
            small(HEADS, D),
            small(1, HEADS),
            small(1, HEADS),
            small(9, 1, INNER + 128),
            small(1, INNER + 128),
            small(1, HEADS),
            small(1, INNER),
        ],
        out_specs=[kept] * 18,
        out_shape=[
            pltpu.VMEM((LENGTH, INNER), BF16),
            pltpu.VMEM((LENGTH, INNER), BF16),
            pltpu.VMEM((4 * LINE, INNER), BF16),
            pltpu.VMEM((LENGTH, 128), BF16),
            pltpu.VMEM((4 * LINE, 128), BF16),
            per_head,
            per_head,
            per_head,
            per_head,
            pltpu.VMEM((1, HEADS), F32),
            pltpu.VMEM((STATE, INNER), F32),
            pltpu.VMEM((D, INNER + 128), BF16),
            pltpu.VMEM((LENGTH, D), BF16),
            pltpu.VMEM((1, D), F32),
            pltpu.VMEM((9, 1, INNER + 128), F32),
            pltpu.VMEM((1, INNER + 128), F32),
            pltpu.VMEM((1, HEADS), F32),
            pltpu.VMEM((1, INNER), F32),
        ],
        scratch_shapes=[
            pltpu.VMEM((LENGTH, D), BF16),
            pltpu.VMEM((4, ROWS, LINE + 16, 128), F32),
            pltpu.VMEM((4, ROWS, LINE + 16, 128), F32),
            pltpu.VMEM((1, ROWS, LINE + 16, 128), F32),
            pltpu.VMEM((128, (ROWS - 2) * LINE), BF16),
            pltpu.VMEM(((ROWS - 2) * LINE, 2 * HEADS), BF16),
            pltpu.VMEM((D, INNER), BF16),
            pltpu.SemaphoreType.DMA((4,)),
            pltpu.SemaphoreType.DMA((4,)),
            pltpu.SemaphoreType.DMA((3,)),
        ],
        compiler_params=params(),
        cost_estimate=pl.CostEstimate(
            flops=2 * LENGTH * D * 3224, bytes_accessed=20 << 20, transcendentals=LENGTH * INNER
        ),
        name="project",
    )(hbm(tok), hbm(gain), hbm(w_xbc), hbm(w_gate), *map(hbm, (w_dt_t, dt_bias, rate, taps, conv_bias, skip, out_gain)))


def edge_kernel(
    top,
    bottom,
    gain,
    w_near,
    rim,
    rim_bc,
    taps_ref,
    bias,
    band_tail,
    total,
    mid,
    x_in,
    bcs_in,
    x,
    bcs,
    pieces,
    edge,
    lines,
    b_t,
    tails,
):
    del x_in, bcs_in
    taps = [taps_ref[n] for n in range(9)]

    def both(side, own, own_start, start, out, out_start, tiles):
        for k in range(tiles):
            part = slice(k * 128, (k + 1) * 128)
            own_part = pl.ds(own_start + k * 128, 128)
            tile = start // 128 + k
            for slot, line in enumerate(
                [side[:LINE, part], own[pl.ds(0, LINE), own_part], own[pl.ds(LINE, LINE), own_part]]
                + [own[pl.ds(2 * LINE, LINE), own_part], own[pl.ds(3 * LINE, LINE), own_part]]
                + [side[LINE:, part]]
            ):
                fill(lines, tile % 4, slot, line)
            for slot, r in ((1, 0), (4, ROWS - 1)):
                out[pl.ds(place(r), LINE), pl.ds(out_start + k * 128, 128)] = convolved(
                    lines, tile % 4, slot, lanes(taps, tile * 128), bias[:, tile * 128 : tile * 128 + 128]
                )

    for slot in range(6):
        for k in range(4):
            lines[k, slot, pl.ds(0, 8), :] = jnp.zeros((8, 128), F32)
            lines[k, slot, pl.ds(LINE + 8, 8), :] = jnp.zeros((8, 128), F32)
    tails[pl.ds(place(0), LINE), :] = two_terms(band_tail[:, :LINE])
    tails[pl.ds(place(ROWS - 1), LINE), :] = two_terms(band_tail[:, LENGTH - LINE :])
    head = lax.broadcasted_iota(jnp.int32, (HEADS, 128), 0)
    lane = lax.broadcasted_iota(jnp.int32, (HEADS, 128), 1)
    first = total[...].astype(BF16)
    rest = total[...] - first.astype(F32)
    second = rest.astype(BF16)
    third = (rest - second.astype(F32)).astype(BF16)
    for g in range(4):
        pick = jnp.where(head == lane + g * GROUP_HEADS, 1.0, 0.0).astype(BF16)
        terms = jnp.concatenate(
            [dot(jnp.broadcast_to(t, (8, HEADS)), pick)[:1] for t in (first, second, third)]
            + [jnp.zeros((13, 128), F32)],
            axis=0,
        ).astype(BF16)
        for a in range(4):
            pieces[a, g, :, pl.ds(GROUP, 128)] = terms
    for n, side in enumerate((top, bottom)):
        edge[pl.ds(n * LINE, LINE), :] = rms(side[...].astype(F32), gain[...]).astype(BF16)
    both(dot(edge[...], w_near[:, pl.ds(INNER, 128)]).astype(BF16), rim_bc, 0, INNER, bcs, 0, 1)
    b_t[...] = bcs[pl.ds(0, 2 * LINE), :].astype(F32).T.astype(BF16)
    for n in range(3):
        start = n * 512
        part = pl.ds(start, 512)
        both(dot(edge[...], w_near[:, part]).astype(BF16), rim, start, start, x, start, 4)
        weighted = x[pl.ds(0, 2 * LINE), part].astype(F32) * dot(tails[...], head_spread(512, n * 8))
        state = mid[:, part] + dot(b_t[pl.ds(0, STATE), :], weighted.astype(BF16))
        for k in range(4):
            g, within = divmod(n * 4 + k, 3)
            for a in range(4):
                pieces[a, g, :, pl.ds(within * 128, 128)] = state[
                    16 * a : 16 * a + 16, k * 128 : (k + 1) * 128
                ].astype(BF16)


def edges(top, bottom, gain, w_near, rim, rim_bc, taps, conv_bias, band_tail, total, mid, x, bcs):
    return pl.pallas_call(
        edge_kernel,
        in_specs=[kept] * 13,
        out_specs=[kept, kept, pl.BlockSpec(memory_space=pltpu.VMEM)],
        out_shape=[
            pltpu.VMEM((LENGTH, INNER), BF16),
            pltpu.VMEM((LENGTH, 128), BF16),
            jax.ShapeDtypeStruct((4, 4, 16, GROUP + 128), BF16),
        ],
        input_output_aliases={11: 0, 12: 1},
        scratch_shapes=[
            pltpu.VMEM((2 * LINE, D), BF16),
            pltpu.VMEM((4, 6, LINE + 16, 128), F32),
            pltpu.VMEM((128, 2 * LINE), BF16),
            pltpu.VMEM((2 * LINE, 2 * HEADS), BF16),
        ],
        compiler_params=params(),
        cost_estimate=pl.CostEstimate(
            flops=2 * 256 * D * 1664 + 10 * LENGTH * 1664,
            bytes_accessed=10 << 20,
            transcendentals=256 * 1664,
        ),
        name="edges",
    )(
        near(top),
        near(bottom),
        near(gain),
        near(w_near),
        near(rim),
        near(rim_bc),
        near(taps),
        near(conv_bias),
        near(band_tail),
        near(total),
        near(mid),
        near(x),
        near(bcs),
    )


def scan_kernel(half, x, bcs, cum, dt, gate, skip, *refs):
    if half:
        w, out, w_near, direct, state, sums, steps, weights, b_t, c, w_sem = refs
        fetch = pltpu.make_async_copy(w, w_near, w_sem)
        fetch.start()
    else:
        out, direct, state, sums, steps, weights, b_t, c = refs
    lane = lax.broadcasted_iota(jnp.int32, (LINE, LINE), 1)
    row = lax.broadcasted_iota(jnp.int32, (LINE, LINE), 0)
    left = lane < WIDTH
    direct[...] = dot(
        two_terms(jnp.broadcast_to(upright(skip[...]), (HEADS, 8))),
        head_spread(HALF, half * HEADS // 2),
    )
    state[...] = jnp.zeros_like(state)
    for r in range(ROWS):
        part = slice(r * LINE, (r + 1) * LINE)
        sums[r] = (cum[:, part] * LOG2E).T
        steps[r] = dt[:, part].T
        both = bcs[pl.ds(place(r), LINE), :].astype(F32)
        b_t[r] = both.T.astype(BF16)[:STATE]
        c[r] = pltpu.roll(both, STATE, 1).astype(BF16)[:, :STATE]
    for r in range(ROWS):
        weights[r] = jnp.where(row >= lane, dot(c[r], b_t[r]), 0.0)

    def line(r, placed):
        rows = pl.ds(pl.multiple_of(r * LINE, LINE), LINE)
        placed_rows = pl.ds(pl.multiple_of(placed * LINE, LINE), LINE)
        sums_here, steps_here, weights_here = sums[r], steps[r], weights[r]
        sums_t = cum[:, rows] * LOG2E
        steps_t = dt[:, rows]

        def mixing(h):
            along = jnp.broadcast_to(sums_here[:, h : h + 1], (LINE, LINE))
            decay = jnp.exp2(jnp.minimum(along - sums_t[h : h + 1], 0.0))
            return along, (decay * (weights_here * steps_t[h : h + 1])).astype(BF16)

        for q in range(HEADS // 8):
            quad = pl.ds(q * 256, 256)
            carried = dot(c[r], state[:, quad].astype(BF16))
            tails, decays = [], []
            for p in (2 * q, 2 * q + 1):
                part = pl.ds(p * 128, 128)
                whole_part = pl.ds(half * HALF + p * 128, 128)
                h = half * HEADS // 2 + 2 * p
                values = x[placed_rows, whole_part].astype(F32)
                (along_a, mixing_a), (along_b, mixing_b) = mixing(h), mixing(h + 1)
                columns = jnp.concatenate(
                    [jnp.where(left, values, 0.0), jnp.where(left, 0.0, values)], axis=0
                ).astype(BF16)
                inner = dot(jnp.concatenate([mixing_a, mixing_b], axis=1), columns)
                here = jnp.where(left, along_a, along_b)
                carry = jnp.exp2(here)
                stepped = jnp.where(left, steps_here[:, h : h + 1], steps_here[:, h + 1 : h + 2])
                tails.append((values * stepped * jnp.exp2(here[LINE - 1 :] - here)).astype(BF16))
                decays.append(carry[LINE - 1 :])
                side = slice((p % 2) * 128, (p % 2) * 128 + 128)
                y = inner + carry * carried[:, side] + direct[0:1, part] * values
                out[rows, part] = (y * gate[rows, whole_part].astype(F32)).astype(BF16)
            state[:, quad] = jnp.concatenate(decays, axis=1) * state[:, quad] + dot(
                b_t[r], jnp.concatenate(tails, axis=1)
            )

    @pl.loop(0, ROWS // 2)
    def _(pair):
        line(2 * pair, 2 * pair + 1)
        line(2 * pair + 1, lax.rem(2 * pair + 2, ROWS))

    if half:
        fetch.wait()


def scan(half, x, bcs, cum, dt, gate, skip, *w):
    weights = [pltpu.VMEM((INNER, D), BF16)] * half
    return pl.pallas_call(
        functools.partial(scan_kernel, half),
        in_specs=[kept] * 6 + [far] * half,
        out_specs=[kept] * (1 + half),
        out_shape=[pltpu.VMEM((LENGTH, HALF), BF16)] + weights,
        scratch_shapes=[
            pltpu.VMEM((8, HALF), F32),
            pltpu.VMEM((STATE, HALF), F32),
            pltpu.VMEM((ROWS, LINE, HEADS), F32),
            pltpu.VMEM((ROWS, LINE, HEADS), F32),
            pltpu.VMEM((ROWS, LINE, LINE), F32),
            pltpu.VMEM((ROWS, STATE, LINE), BF16),
            pltpu.VMEM((ROWS, LINE, STATE), BF16),
        ]
        + [pltpu.SemaphoreType.DMA(())] * half,
        compiler_params=params(),
        cost_estimate=pl.CostEstimate(
            flops=2 << 30, bytes_accessed=5 << 20, transcendentals=LENGTH * LINE * HEADS // 2
        ),
        name="scan",
    )(near(x), near(bcs), near(cum), near(dt), near(gate), near(skip), *map(hbm, w))


def relay_kernel(arrived, out):
    logs = jnp.concatenate(
        [
            jnp.sum(arrived[j, :, pl.ds(GROUP, 128)].astype(F32), axis=0, keepdims=True)
            for j in range(BANDS)
        ],
        axis=0,
    )
    decay = jnp.exp(logs)
    high = decay.astype(BF16)
    low = (decay - high.astype(F32)).astype(BF16)
    lane = lax.broadcasted_iota(jnp.int32, (128, GROUP), 0)
    channel = lax.broadcasted_iota(jnp.int32, (128, GROUP), 1)
    spread = jnp.where(lane == channel // WIDTH, 1.0, 0.0).astype(BF16)
    wide = dot(high, spread) + dot(low, spread)
    state = jnp.zeros((16, GROUP), F32)
    for j in range(BANDS):
        out[j] = state.astype(BF16)
        state = wide[j : j + 1] * state + arrived[j, :, pl.ds(0, GROUP)].astype(F32)


def relay(arrived):
    return pl.pallas_call(
        relay_kernel,
        out_shape=jax.ShapeDtypeStruct((BANDS, 16, GROUP), BF16),
        compiler_params=params(16),
        name="relay",
    )(arrived)


def columns_out(values, tokens, turned, out, step):
    values = values + tokens.astype(F32)
    rows = pl.ds(pl.multiple_of(step * 256, 256), 256)
    for k in range(values.shape[1] // 128):
        part = slice(k * 128, (k + 1) * 128)
        for r in range(ROWS):
            turned[k, pl.ds(r, 32, stride=ROWS), :] = values[r * 32 : (r + 1) * 32, part]
        out[rows, part] = turned[k].astype(BF16)


def finish_kernel(
    local_a, local_b, gate, bcs, band_decay, entering, gain, tok, w, out, hidden, spread, state, decays, turned
):
    step = pl.program_id(0)

    @pl.when(step == 0)
    def _():
        spread[...] = head_spread(INNER, 0)
        state[pl.ds(0, STATE), :] = jnp.zeros((STATE, INNER), BF16)
        for a in range(4):
            for g in range(4):
                state[pl.ds(STATE + 16 * a, 16), pl.ds(g * GROUP, GROUP)] = entering[4 * a + g]
        for r in range(ROWS):
            decays[r] = two_terms(band_decay[:, r * LINE : (r + 1) * LINE])

    here = pl.ds(pl.multiple_of(step * 32, 32), 32)
    cells = lambda ref: ref[:, here, :].reshape(256, ref.shape[2])
    both = jnp.concatenate([bcs[1:, here, :], bcs[:1, here, :]], axis=0).reshape(256, 128)
    decay = dot(cells(decays), spread[...])
    local = jnp.concatenate([cells(local_a), cells(local_b)], axis=1)
    gated = local.astype(F32) + dot(both, state[...]) * decay * cells(gate).astype(F32)
    normed = rms(gated, gain[...]).astype(BF16)
    hidden[:, here, :] = normed.reshape(ROWS, 32, INNER)
    columns_out(
        dot(normed, w[:, pl.ds(0, FIRST)]),
        tok[:, here, pl.ds(0, FIRST)].reshape(256, FIRST),
        turned,
        out,
        step,
    )


def finish(local_a, local_b, gate, bcs, band_decay, entering, gain, tok, w_near):
    return pl.pallas_call(
        finish_kernel,
        grid=(LINE // 32,),
        in_specs=[kept] * 5 + [whole(BANDS, 16, GROUP), kept, kept, kept],
        out_specs=[kept, kept],
        out_shape=[
            pltpu.VMEM((LENGTH, FIRST), BF16),
            pltpu.VMEM((ROWS, LINE, INNER), BF16),
        ],
        scratch_shapes=[
            pltpu.VMEM((2 * HEADS, INNER), BF16),
            pltpu.VMEM((2 * STATE, INNER), BF16),
            pltpu.VMEM((ROWS, LINE, 2 * HEADS), BF16),
            pltpu.VMEM((FIRST // 128, 256, 128), F32),
        ],
        compiler_params=params(),
        cost_estimate=pl.CostEstimate(
            flops=2 * LENGTH * D * FIRST, bytes_accessed=16 << 20, transcendentals=LENGTH
        ),
        name="finish",
    )(
        near(local_a),
        near(local_b),
        near(gate),
        near(bcs),
        near(band_decay),
        entering,
        near(gain),
        near(tok),
        near(w_near),
    )


def rest_kernel(hidden, tok, w, out, turned):
    step = pl.program_id(0)
    here = pl.ds(pl.multiple_of(step * 32, 32), 32)
    part = pl.ds(FIRST, D - FIRST)
    columns_out(
        dot(hidden[:, here, :].reshape(256, INNER), w[:, part]),
        tok[:, here, part].reshape(256, D - FIRST),
        turned,
        out,
        step,
    )


def rest(hidden, tok, w_near):
    return pl.pallas_call(
        rest_kernel,
        grid=(LINE // 32,),
        in_specs=[kept] * 3,
        out_specs=kept,
        out_shape=pltpu.VMEM((LENGTH, D - FIRST), BF16),
        scratch_shapes=[pltpu.VMEM(((D - FIRST) // 128, 256, 128), F32)],
        compiler_params=params(),
        cost_estimate=pl.CostEstimate(
            flops=2 * LENGTH * D * (D - FIRST), bytes_accessed=8 << 20, transcendentals=0
        ),
        name="rest",
    )(near(hidden), near(tok), near(w_near))


def shards(
    tokens,
    in_gain,
    w_xbc,
    w_gate,
    w_dt,
    dt_bias,
    decay_rate,
    conv_w,
    conv_bias,
    skip,
    out_gain,
    w_out,
):
    bands = lax.axis_size("band")
    segments = lax.axis_size("segment")
    cells = tokens[0]
    tok = cells.reshape(LENGTH, D)
    top = lax.ppermute(cells[ROWS - 1], "band", [(i, i + 1) for i in range(bands - 1)])
    bottom = lax.ppermute(cells[0], "band", [(i + 1, i) for i in range(bands - 1)])

    (
        x,
        gate,
        rim,
        bcs,
        rim_bc,
        cum,
        dt,
        band_tail,
        band_decay,
        total,
        mid,
        w_xbc_near,
        tok_near,
        in_gain_near,
        taps_near,
        bias_near,
        skip_near,
        out_gain_near,
    ) = project(
        tok,
        in_gain,
        w_xbc[0],
        w_gate[0],
        w_dt[0].T,
        dt_bias,
        decay_rate,
        conv_w.swapaxes(0, 1),
        conv_bias,
        skip,
        out_gain,
    )
    x, bcs, pieces = edges(
        top,
        bottom,
        in_gain_near,
        w_xbc_near,
        rim,
        rim_bc,
        taps_near,
        bias_near,
        band_tail,
        total,
        mid,
        x,
        bcs,
    )
    swap = functools.partial(
        lax.all_to_all, axis_name="band", split_axis=0, concat_axis=0, tiled=True
    )
    onward = functools.partial(
        lax.ppermute, axis_name="segment", perm=[(i, (i + 1) % segments) for i in range(segments)]
    )
    arrived = swap(pieces.reshape(BANDS, 16, GROUP + 128))
    (local_a,) = scan(0, x, bcs, cum, dt, gate, skip_near)
    arrived, local_a = lax.optimization_barrier((arrived, local_a))
    states = relay(arrived)
    states, skip_b = lax.optimization_barrier((states, skip_near))
    entering = swap(states)
    local_b, w_out_near = scan(1, x, bcs, cum, dt, gate, skip_b, w_out[0])

    grid = lambda a: a.reshape(ROWS, LINE, a.shape[-1])
    parted = lambda a: a.reshape(BANDS, LENGTH // BANDS, a.shape[-1])
    first, hidden = finish(
        grid(local_a),
        grid(local_b),
        grid(gate),
        grid(bcs),
        band_decay,
        entering,
        out_gain_near,
        grid(tok_near),
        w_out_near,
    )
    first = swap(parted(first))
    second = onward(parted(rest(hidden, grid(tok_near), w_out_near)))
    second = swap(second)
    first = onward(first)
    both = jnp.concatenate([first, second], axis=-1)
    handed = both.reshape(BANDS, LINE // BANDS, ROWS, D).swapaxes(0, 1)
    return handed.reshape(1, LINE // BANDS, BANDS * ROWS, D)


def solution(mesh):
    in_specs = (
        P("segment", "band", None, None),
        P("segment", None),
        P("segment", None, None),
        P("segment", None, None),
        P("segment", None, None),
        P("segment", None),
        P("segment", None),
        P("segment", None, None),
        P("segment", None),
        P("segment", None),
        P("segment", None),
        P("segment", None, None),
    )
    out_specs = P("segment", "band", None, None)
    return jax.shard_map(shards, mesh=mesh, in_specs=in_specs, out_specs=out_specs, check_vma=False)
```

```python
import functools

import jax
import jax.numpy as jnp
from jax import lax
from jax.experimental import pallas as pl
from jax.experimental.pallas import tpu as pltpu
from jax.sharding import PartitionSpec as P

EPSILON = 1e-05
ROWS = 8
LINE = 128
LENGTH = ROWS * LINE
HEADS = 24
WIDTH = 64
STATE = 64
INNER = HEADS * WIDTH
D = 1536
HALF = INNER // 2
FIRST = 896
GROUP = 384
GROUP_HEADS = GROUP // WIDTH
BANDS = 16
F32 = jnp.float32
BF16 = jnp.bfloat16
MIB = 1 << 20
LOG2E = 1.4426950408889634


def params(mib=24):
    return pltpu.CompilerParams(vmem_limit_bytes=mib * MIB)


kept = pl.BlockSpec(memory_space=pltpu.VMEM)
far = pl.BlockSpec(memory_space=pl.ANY)


def small(*shape):
    return pl.BlockSpec(shape, lambda *i: (0,) * len(shape))


def near(a):
    return pltpu.with_memory_space_constraint(a, pltpu.VMEM)


def hbm(a):
    return pltpu.with_memory_space_constraint(a, pltpu.HBM)


def upright(row):
    return jnp.broadcast_to(row, (LINE, HEADS)).T[:, :1]


def whole(*shape):
    return pl.BlockSpec(shape, lambda i: (0,) * len(shape), pipeline_mode=pl.Buffered(1))


def dot(a, b):
    return jnp.dot(a, b, preferred_element_type=F32)


def rms(values, gain):
    return values * lax.rsqrt(jnp.mean(values * values, -1, keepdims=True) + EPSILON) * gain


def silu(v):
    half = 0.5 * v
    return half + half * jnp.tanh(half)


def head_spread(channels, first):
    head = lax.broadcasted_iota(jnp.int32, (2 * HEADS, channels), 0)
    head = jnp.where(head < HEADS, head, head - HEADS)
    channel = lax.broadcasted_iota(jnp.int32, (2 * HEADS, channels), 1)
    return jnp.where(head - first == channel // WIDTH, 1.0, 0.0).astype(BF16)


def two_terms(values_t):
    high = values_t.astype(BF16).astype(F32)
    return jnp.concatenate([high, values_t - high], axis=0).T.astype(BF16)


def place(r):
    return (r + 1) % ROWS * LINE


def fill(padded, tile, slot, line):
    padded[tile, slot, pl.ds(8, LINE), :] = line.astype(F32)


def convolved(padded, tile, slot, taps, bias):
    total = bias
    for i in range(3):
        for j in range(3):
            total = total + padded[tile, slot - 1 + i, pl.ds(7 + j, LINE), :] * taps[3 * i + j]
    return silu(total).astype(BF16)


def lanes(refs, start):
    return [ref[:, start : start + 128] for ref in refs]


def project_kernel(
    tok,
    gain,
    w_xbc,
    w_g,
    w_dt,
    dt_bias,
    rate,
    taps_ref,
    bias,
    x,
    gate_out,
    rim,
    bcs,
    rim_bc,
    cum,
    dt,
    band_tail,
    band_decay,
    total,
    mid,
    w_near,
    gain_near,
    taps_near,
    bias_near,
    tok_near,
    gate,
    normed,
    lines_a,
    lines_b,
    lines_bc,
    b_t,
    tails,
    w_g_near,
    tok_sem,
    w_sem,
    w_g_sem,
    gate_sem,
):
    def tokens_in(m):
        part = pl.ds(m * 256, 256)
        return pltpu.make_async_copy(tok.at[part, :], tok_near.at[part, :], tok_sem.at[m])

    def w_in(n):
        part = pl.ds(n * 512, 512 if n < 3 else 128)
        return pltpu.make_async_copy(w_xbc.at[:, part], w_near.at[:, part], w_sem.at[n])

    def gate_in(n):
        part = pl.ds(n * 512, 512)
        return pltpu.make_async_copy(w_g.at[:, part], w_g_near.at[:, part], w_g_sem.at[n])

    def send_gate(n):
        part = pl.ds(n * 512, 512)
        return pltpu.make_async_copy(gate.at[:, part], gate_out.at[:, part], gate_sem.at[n])

    taps = [taps_ref[n] for n in range(9)]

    def store(m, values, padded, out, start, tiles, tile=0):
        for n in range(m * 2, m * 2 + 2):
            line = values[(n - m * 2) * LINE : (n - m * 2 + 1) * LINE]
            for k in range(tiles):
                fill(padded, tile + k, n, line[:, k * 128 : (k + 1) * 128])
            if n in (0, 1, 6, 7):
                place_n = (n if n < 2 else n - 4) * LINE
                out[pl.ds(place_n, LINE), pl.ds(start, tiles * 128)] = line

    def multiply_x(m, here, padded, chunk, side):
        start = chunk * 512 + side * 256
        values = dot(here, w_near[:, pl.ds(start, 256)]).astype(BF16)
        store(m, values, padded, rim, start, 2, side * 2)

    def multiply_gate(m, n, side):
        rows, part = pl.ds(m * 256, 256), pl.ds(n * 512 + side * 256, 256)
        gate[rows, part] = silu(dot(normed[rows, :], w_g_near[:, part])).astype(BF16)

    def inside(k, padded, chunk, rows):
        start = chunk * 512 + k * 128
        for r in rows:
            x[pl.ds(place(r), LINE), pl.ds(start, 128)] = convolved(
                padded, k, r, lanes(taps, start), bias[:, start : start + 128]
            )

    def add_state(piece):
        part = pl.ds(piece * 256, 256)
        spread = head_spread(256, piece * 4)
        own = x[pl.ds(2 * LINE, (ROWS - 2) * LINE), part].astype(F32)
        mid[:, part] = dot(b_t[pl.ds(0, STATE), :], (own * dot(tails[...], spread)).astype(BF16))

    tokens_in(0).start()
    w_in(3).start()
    w_in(0).start()
    for m in range(1, 4):
        tokens_in(m).start()
    w_in(1).start()
    w_in(2).start()
    for n in range(3):
        gate_in(n).start()
    gain_near[...] = gain[...]
    taps_near[...] = taps_ref[...]
    bias_near[...] = bias[...]
    for padded in (lines_a, lines_b, lines_bc):
        for n in range(ROWS):
            for k in range(padded.shape[0]):
                padded[k, n, pl.ds(0, 8), :] = jnp.zeros((8, 128), F32)
                padded[k, n, pl.ds(LINE + 8, 8), :] = jnp.zeros((8, 128), F32)
    for m in range(4):
        tokens_in(m).wait()
        if m == 0:
            w_in(3).wait()
            w_in(0).wait()
        part = pl.ds(m * 256, 256)
        here = rms(tok_near[part, :].astype(F32), gain[...]).astype(BF16)
        normed[part, :] = here
        store(m, dot(here, w_near[:, pl.ds(INNER, 128)]).astype(BF16), lines_bc, rim_bc, 0, 1)
        for side in range(2):
            multiply_x(m, here, lines_a, 0, side)

    w_in(1).wait()
    for r in range(1, ROWS - 1):
        values = convolved(
            lines_bc, 0, r, lanes(taps, INNER), bias[:, INNER : INNER + 128]
        )
        bcs[pl.ds(place(r), LINE), :] = values
        b_t[:, pl.ds((r - 1) * LINE, LINE)] = values.astype(F32).T.astype(BF16)
    raw = lax.dot_general(
        w_dt[...], normed[...], (((1,), (1,)), ((), ())), preferred_element_type=F32
    ) + upright(dt_bias[...])
    steps = jnp.maximum(raw, 0.0) + jnp.log1p(jnp.exp(-jnp.abs(raw)))
    dt[...] = steps
    for m in range(4):
        for side in range(2):
            multiply_x(m, normed[pl.ds(m * 256, 256), :], lines_b, 1, side)
            inside(m, lines_a, 0, range(1 + 3 * side, 4 + 3 * side))

    w_in(2).wait()
    log_decay = -upright(rate[...]) * steps
    i = lax.broadcasted_iota(jnp.int32, (LINE, LINE), 0)
    j = lax.broadcasted_iota(jnp.int32, (LINE, LINE), 1)
    sums = jnp.dot(
        jnp.concatenate([log_decay[:, r * LINE : (r + 1) * LINE] for r in range(ROWS)], axis=0),
        jnp.where(i <= j, 1.0, 0.0).astype(F32),
        precision=lax.Precision.HIGHEST,
        preferred_element_type=F32,
    )
    lines = [sums[r * HEADS : (r + 1) * HEADS] for r in range(ROWS)]
    ends = [line[:, LINE - 1 :] for line in lines]
    before = [jnp.zeros_like(ends[0])]
    after = [jnp.zeros_like(ends[0])]
    for r in range(ROWS - 1):
        before.append(before[-1] + ends[r])
        after.append(after[-1] + ends[ROWS - 1 - r])
    for r in range(ROWS):
        part = slice(r * LINE, (r + 1) * LINE)
        cum[:, part] = lines[r]
        band_decay[:, part] = jnp.exp(lines[r] + before[r])
        tail = steps[:, part] * jnp.exp((ends[r] - lines[r]) + after[ROWS - 1 - r])
        band_tail[:, part] = tail
        if 0 < r < ROWS - 1:
            tails[pl.ds((r - 1) * LINE, LINE), :] = two_terms(tail)
    total[...] = jnp.broadcast_to(before[-1] + ends[-1], (HEADS, LINE)).T[:1]
    for m in range(4):
        for side in range(2):
            multiply_x(m, normed[pl.ds(m * 256, 256), :], lines_a, 2, side)
            inside(m, lines_b, 1, range(1 + 3 * side, 4 + 3 * side))

    gate_in(0).wait()
    for m in range(4):
        for side in range(2):
            multiply_gate(m, 0, side)
            inside(m, lines_a, 2, range(1 + 3 * side, 4 + 3 * side))
    send_gate(0).start()
    for n in (1, 2):
        gate_in(n).wait()
        for m in range(4):
            for side in range(2):
                multiply_gate(m, n, side)
            if m < 3:
                add_state((n - 1) * 3 + m)
        send_gate(n).start()
    for n in range(3):
        send_gate(n).wait()


def project(tok, gain, w_xbc, w_gate, w_dt_t, dt_bias, rate, taps, conv_bias):
    per_head = pltpu.HBM((HEADS, LENGTH), F32)
    return pl.pallas_call(
        project_kernel,
        in_specs=[
            far,
            small(1, D),
            far,
            far,
            small(HEADS, D),
            small(1, HEADS),
            small(1, HEADS),
            small(9, 1, INNER + 128),
            small(1, INNER + 128),
        ],
        out_specs=[kept, far, kept, kept, kept]
        + [small(HEADS, LENGTH)] * 2
        + [kept]
        + [small(HEADS, LENGTH)]
        + [kept] * 6,
        out_shape=[
            pltpu.VMEM((LENGTH, INNER), BF16),
            pltpu.HBM((LENGTH, INNER), BF16),
            pltpu.VMEM((4 * LINE, INNER), BF16),
            pltpu.VMEM((LENGTH, 128), BF16),
            pltpu.VMEM((4 * LINE, 128), BF16),
            per_head,
            per_head,
            pltpu.VMEM((HEADS, LENGTH), F32),
            per_head,
            pltpu.VMEM((1, HEADS), F32),
            pltpu.VMEM((STATE, INNER), F32),
            pltpu.VMEM((D, INNER + 128), BF16),
            pltpu.VMEM((1, D), F32),
            pltpu.VMEM((9, 1, INNER + 128), F32),
            pltpu.VMEM((1, INNER + 128), F32),
        ],
        scratch_shapes=[
            pltpu.VMEM((LENGTH, D), BF16),
            pltpu.VMEM((LENGTH, INNER), BF16),
            pltpu.VMEM((LENGTH, D), BF16),
            pltpu.VMEM((4, ROWS, LINE + 16, 128), F32),
            pltpu.VMEM((4, ROWS, LINE + 16, 128), F32),
            pltpu.VMEM((1, ROWS, LINE + 16, 128), F32),
            pltpu.VMEM((128, (ROWS - 2) * LINE), BF16),
            pltpu.VMEM(((ROWS - 2) * LINE, 2 * HEADS), BF16),
            pltpu.VMEM((D, INNER), BF16),
            pltpu.SemaphoreType.DMA((4,)),
            pltpu.SemaphoreType.DMA((4,)),
            pltpu.SemaphoreType.DMA((3,)),
            pltpu.SemaphoreType.DMA((3,)),
        ],
        compiler_params=params(),
        cost_estimate=pl.CostEstimate(
            flops=2 * LENGTH * D * 3224, bytes_accessed=20 << 20, transcendentals=LENGTH * INNER
        ),
        name="project",
    )(hbm(tok), hbm(gain), hbm(w_xbc), hbm(w_gate), *map(hbm, (w_dt_t, dt_bias, rate, taps, conv_bias)))


def edge_kernel(
    top,
    bottom,
    gain,
    w_near,
    rim,
    rim_bc,
    taps_ref,
    bias,
    band_tail,
    total,
    mid,
    x_near,
    bcs_near,
    x_out,
    bcs,
    pieces,
    x,
    edge,
    lines,
    b_t,
    tails,
    mid_sem,
    edge_sem,
):
    inner_part = pl.ds(2 * LINE, (ROWS - 2) * LINE)
    send_mid = pltpu.make_async_copy(x_near.at[inner_part, :], x_out.at[inner_part, :], mid_sem)
    send_mid.start()

    def send_edge(n):
        rows, part = pl.ds(0, 2 * LINE), pl.ds(n * 512, 512)
        return pltpu.make_async_copy(x.at[:, part], x_out.at[rows, part], edge_sem.at[n])

    bcs[inner_part, :] = bcs_near[inner_part, :]
    taps = [taps_ref[n] for n in range(9)]

    def both(side, own, own_start, start, out, out_start, tiles):
        for k in range(tiles):
            part = slice(k * 128, (k + 1) * 128)
            own_part = pl.ds(own_start + k * 128, 128)
            tile = start // 128 + k
            for slot, line in enumerate(
                [side[:LINE, part], own[pl.ds(0, LINE), own_part], own[pl.ds(LINE, LINE), own_part]]
                + [own[pl.ds(2 * LINE, LINE), own_part], own[pl.ds(3 * LINE, LINE), own_part]]
                + [side[LINE:, part]]
            ):
                fill(lines, tile % 4, slot, line)
            for slot, r in ((1, 0), (4, ROWS - 1)):
                out[pl.ds(place(r), LINE), pl.ds(out_start + k * 128, 128)] = convolved(
                    lines, tile % 4, slot, lanes(taps, tile * 128), bias[:, tile * 128 : tile * 128 + 128]
                )

    for slot in range(6):
        for k in range(4):
            lines[k, slot, pl.ds(0, 8), :] = jnp.zeros((8, 128), F32)
            lines[k, slot, pl.ds(LINE + 8, 8), :] = jnp.zeros((8, 128), F32)
    tails[pl.ds(place(0), LINE), :] = two_terms(band_tail[:, :LINE])
    tails[pl.ds(place(ROWS - 1), LINE), :] = two_terms(band_tail[:, LENGTH - LINE :])
    head = lax.broadcasted_iota(jnp.int32, (HEADS, 128), 0)
    lane = lax.broadcasted_iota(jnp.int32, (HEADS, 128), 1)
    first = total[...].astype(BF16)
    rest = total[...] - first.astype(F32)
    second = rest.astype(BF16)
    third = (rest - second.astype(F32)).astype(BF16)
    for g in range(4):
        pick = jnp.where(head == lane + g * GROUP_HEADS, 1.0, 0.0).astype(BF16)
        terms = jnp.concatenate(
            [dot(jnp.broadcast_to(t, (8, HEADS)), pick)[:1] for t in (first, second, third)]
            + [jnp.zeros((13, 128), F32)],
            axis=0,
        ).astype(BF16)
        for a in range(4):
            pieces[a, g, :, pl.ds(GROUP, 128)] = terms
    for n, side in enumerate((top, bottom)):
        edge[pl.ds(n * LINE, LINE), :] = rms(side[...].astype(F32), gain[...]).astype(BF16)
    both(dot(edge[...], w_near[:, pl.ds(INNER, 128)]).astype(BF16), rim_bc, 0, INNER, bcs, 0, 1)
    b_t[...] = bcs[pl.ds(0, 2 * LINE), :].astype(F32).T.astype(BF16)
    for n in range(3):
        start = n * 512
        part = pl.ds(start, 512)
        both(dot(edge[...], w_near[:, part]).astype(BF16), rim, start, start, x, start, 4)
        send_edge(n).start()
        weighted = x[:, part].astype(F32) * dot(tails[...], head_spread(512, n * 8))
        state = mid[:, part] + dot(b_t[pl.ds(0, STATE), :], weighted.astype(BF16))
        for k in range(4):
            g, within = divmod(n * 4 + k, 3)
            for a in range(4):
                pieces[a, g, :, pl.ds(within * 128, 128)] = state[
                    16 * a : 16 * a + 16, k * 128 : (k + 1) * 128
                ].astype(BF16)
    send_mid.wait()
    for n in range(3):
        send_edge(n).wait()


def edges(top, bottom, gain, w_near, rim, rim_bc, taps, conv_bias, band_tail, total, mid, x, bcs):
    return pl.pallas_call(
        edge_kernel,
        in_specs=[kept] * 13,
        out_specs=[far, small(LENGTH, 128), small(4, 4, 16, GROUP + 128)],
        out_shape=[
            pltpu.HBM((LENGTH, INNER), BF16),
            pltpu.HBM((LENGTH, 128), BF16),
            pltpu.HBM((4, 4, 16, GROUP + 128), BF16),
        ],
        scratch_shapes=[
            pltpu.VMEM((2 * LINE, INNER), BF16),
            pltpu.VMEM((2 * LINE, D), BF16),
            pltpu.VMEM((4, 6, LINE + 16, 128), F32),
            pltpu.VMEM((128, 2 * LINE), BF16),
            pltpu.VMEM((2 * LINE, 2 * HEADS), BF16),
            pltpu.SemaphoreType.DMA(()),
            pltpu.SemaphoreType.DMA((3,)),
        ],
        compiler_params=params(),
        cost_estimate=pl.CostEstimate(
            flops=2 * 256 * D * 1664 + 10 * LENGTH * 1664,
            bytes_accessed=10 << 20,
            transcendentals=256 * 1664,
        ),
        name="edges",
    )(
        near(top),
        near(bottom),
        near(gain),
        near(w_near),
        near(rim),
        near(rim_bc),
        near(taps),
        near(conv_bias),
        near(band_tail),
        near(total),
        near(mid),
        near(x),
        near(bcs),
    )


def scan_kernel(
    x_far,
    bcs,
    cum,
    dt,
    gate_far,
    skip,
    band_decay,
    out_gain,
    w_far,
    tok_far,
    out,
    gate,
    w_near,
    tok_near,
    bcs_near,
    decay_near,
    gain_near,
    x,
    direct,
    state,
    sums,
    steps,
    weights,
    b_t,
    c,
    sem,
    late_sem,
):
    def rows_of(place):
        return pl.ds(pl.multiple_of(place * LINE, LINE), LINE)

    def x_in(r):
        rows = rows_of(lax.rem(r + 1, ROWS))
        return pltpu.make_async_copy(x_far.at[rows, :], x.at[rows, :], sem.at[0, r])

    def gate_in(r):
        rows = rows_of(r)
        return pltpu.make_async_copy(gate_far.at[rows, :], gate.at[rows, :], sem.at[1, r])

    late = [
        pltpu.make_async_copy(w_far, w_near, late_sem.at[0]),
        pltpu.make_async_copy(tok_far, tok_near, late_sem.at[1]),
    ]
    for r in range(ROWS):
        x_in(r).start()
        gate_in(r).start()
    for copy in late:
        copy.start()
    bcs_near[...] = bcs[...]
    decay_near[...] = band_decay[...]
    gain_near[...] = out_gain[...]
    lane = lax.broadcasted_iota(jnp.int32, (LINE, LINE), 1)
    row = lax.broadcasted_iota(jnp.int32, (LINE, LINE), 0)
    left = lane < WIDTH
    direct[...] = dot(
        two_terms(jnp.broadcast_to(upright(skip[...]), (HEADS, 8))),
        head_spread(INNER, 0),
    )
    state[...] = jnp.zeros_like(state)
    for r in range(ROWS):
        part = slice(r * LINE, (r + 1) * LINE)
        sums[r] = (cum[:, part] * LOG2E).T
        steps[r] = dt[:, part].T
        both = bcs[pl.ds(place(r), LINE), :].astype(F32)
        b_t[r] = both.T.astype(BF16)[:STATE]
        c[r] = pltpu.roll(both, STATE, 1).astype(BF16)[:, :STATE]
    for r in range(ROWS):
        weights[r] = jnp.where(row >= lane, dot(c[r], b_t[r]), 0.0)

    def line(r):
        rows, placed_rows = rows_of(r), rows_of(lax.rem(r + 1, ROWS))
        sums_here, steps_here, weights_here = sums[r], steps[r], weights[r]
        sums_t = cum[:, rows] * LOG2E
        steps_t = dt[:, rows]

        def mixing(h):
            along = jnp.broadcast_to(sums_here[:, h : h + 1], (LINE, LINE))
            decay = jnp.exp2(jnp.minimum(along - sums_t[h : h + 1], 0.0))
            return along, (decay * (weights_here * steps_t[h : h + 1])).astype(BF16)

        for q in range(HEADS // 4):
            quad = pl.ds(q * 256, 256)
            carried = dot(c[r], state[:, quad].astype(BF16))
            tails, decays = [], []
            for p in (2 * q, 2 * q + 1):
                part = pl.ds(p * 128, 128)
                h = 2 * p
                values = x[placed_rows, part].astype(F32)
                (along_a, mixing_a), (along_b, mixing_b) = mixing(h), mixing(h + 1)
                columns = jnp.concatenate(
                    [jnp.where(left, values, 0.0), jnp.where(left, 0.0, values)], axis=0
                ).astype(BF16)
                inner = dot(jnp.concatenate([mixing_a, mixing_b], axis=1), columns)
                here = jnp.where(left, along_a, along_b)
                carry = jnp.exp2(here)
                stepped = jnp.where(left, steps_here[:, h : h + 1], steps_here[:, h + 1 : h + 2])
                tails.append((values * stepped * jnp.exp2(here[LINE - 1 :] - here)).astype(BF16))
                decays.append(carry[LINE - 1 :])
                side = slice((p % 2) * 128, (p % 2) * 128 + 128)
                y = inner + carry * carried[:, side] + direct[0:1, part] * values
                out[rows, part] = (y * gate[rows, part].astype(F32)).astype(BF16)
            state[:, quad] = jnp.concatenate(decays, axis=1) * state[:, quad] + dot(
                b_t[r], jnp.concatenate(tails, axis=1)
            )

    @pl.loop(0, ROWS // 2)
    def _(pair):
        for r in (2 * pair, 2 * pair + 1):
            x_in(r).wait()
            gate_in(r).wait()
        line(2 * pair)
        line(2 * pair + 1)

    for copy in late:
        copy.wait()


def scan(x, bcs, cum, dt, gate, skip, band_decay, out_gain, w_out, tok):
    return pl.pallas_call(
        scan_kernel,
        in_specs=[
            far,
            small(LENGTH, 128),
            small(HEADS, LENGTH),
            small(HEADS, LENGTH),
            far,
            small(1, HEADS),
            small(HEADS, LENGTH),
            small(1, INNER),
            far,
            far,
        ],
        out_specs=[kept] * 7,
        out_shape=[
            pltpu.VMEM((LENGTH, INNER), BF16),
            pltpu.VMEM((LENGTH, INNER), BF16),
            pltpu.VMEM((INNER, D), BF16),
            pltpu.VMEM((ROWS, LINE, D), BF16),
            pltpu.VMEM((LENGTH, 128), BF16),
            pltpu.VMEM((HEADS, LENGTH), F32),
            pltpu.VMEM((1, INNER), F32),
        ],
        scratch_shapes=[
            pltpu.VMEM((LENGTH, INNER), BF16),
            pltpu.VMEM((8, INNER), F32),
            pltpu.VMEM((STATE, INNER), F32),
            pltpu.VMEM((ROWS, LINE, HEADS), F32),
            pltpu.VMEM((ROWS, LINE, HEADS), F32),
            pltpu.VMEM((ROWS, LINE, LINE), F32),
            pltpu.VMEM((ROWS, STATE, LINE), BF16),
            pltpu.VMEM((ROWS, LINE, STATE), BF16),
            pltpu.SemaphoreType.DMA((2, ROWS)),
            pltpu.SemaphoreType.DMA((2,)),
        ],
        compiler_params=params(),
        cost_estimate=pl.CostEstimate(
            flops=4 << 30, bytes_accessed=20 << 20, transcendentals=LENGTH * LINE * HEADS
        ),
        name="scan",
    )(
        hbm(x),
        hbm(bcs),
        hbm(cum),
        hbm(dt),
        hbm(gate),
        hbm(skip),
        hbm(band_decay),
        hbm(out_gain),
        hbm(w_out),
        hbm(tok),
    )


def relay_kernel(arrived, out):
    logs = jnp.concatenate(
        [
            jnp.sum(arrived[j, :, pl.ds(GROUP, 128)].astype(F32), axis=0, keepdims=True)
            for j in range(BANDS)
        ],
        axis=0,
    )
    decay = jnp.exp(logs)
    high = decay.astype(BF16)
    low = (decay - high.astype(F32)).astype(BF16)
    lane = lax.broadcasted_iota(jnp.int32, (128, GROUP), 0)
    channel = lax.broadcasted_iota(jnp.int32, (128, GROUP), 1)
    spread = jnp.where(lane == channel // WIDTH, 1.0, 0.0).astype(BF16)
    wide = dot(high, spread) + dot(low, spread)
    state = jnp.zeros((16, GROUP), F32)
    for j in range(BANDS):
        out[j] = state.astype(BF16)
        state = wide[j : j + 1] * state + arrived[j, :, pl.ds(0, GROUP)].astype(F32)


def relay(arrived):
    return pl.pallas_call(
        relay_kernel,
        out_specs=kept,
        out_shape=pltpu.VMEM((BANDS, 16, GROUP), BF16),
        compiler_params=params(16),
        name="relay",
    )(arrived)


def columns_out(values, tokens, turned, out):
    values = values + tokens.astype(F32)
    for k in range(values.shape[1] // 128):
        part = slice(k * 128, (k + 1) * 128)
        for r in range(ROWS):
            turned[k, pl.ds(r, 32, stride=ROWS), :] = values[r * 32 : (r + 1) * 32, part]
        out[:, part] = turned[k].astype(BF16)


def finish_kernel(
    local, gate, bcs, band_decay, entering, gain, tok, w, out, hidden, spread, state, decays, turned
):
    step = pl.program_id(0)

    @pl.when(step == 0)
    def _():
        spread[...] = head_spread(INNER, 0)
        state[pl.ds(0, STATE), :] = jnp.zeros((STATE, INNER), BF16)
        for a in range(4):
            for g in range(4):
                state[pl.ds(STATE + 16 * a, 16), pl.ds(g * GROUP, GROUP)] = entering[4 * a + g]
        for r in range(ROWS):
            decays[r] = two_terms(band_decay[:, r * LINE : (r + 1) * LINE])

    here = pl.ds(pl.multiple_of(step * 32, 32), 32)
    cells = lambda ref: ref[:, here, :].reshape(256, ref.shape[2])
    both = jnp.concatenate([bcs[1:, here, :], bcs[:1, here, :]], axis=0).reshape(256, 128)
    decay = dot(cells(decays), spread[...])
    gated = cells(local).astype(F32) + dot(both, state[...]) * decay * cells(gate).astype(F32)
    normed = rms(gated, gain[...]).astype(BF16)
    hidden[...] = normed.reshape(ROWS, 32, INNER)
    columns_out(
        dot(normed, w[:, pl.ds(0, FIRST)]),
        tok[:, here, pl.ds(0, FIRST)].reshape(256, FIRST),
        turned,
        out,
    )


def finish(local, gate, bcs, band_decay, entering, gain, tok, w_out):
    return pl.pallas_call(
        finish_kernel,
        grid=(LINE // 32,),
        in_specs=[kept] * 8,
        out_specs=[
            pl.BlockSpec((256, FIRST), lambda i: (i, 0)),
            pl.BlockSpec((ROWS, 32, INNER), lambda i: (0, i, 0)),
        ],
        out_shape=[
            pltpu.HBM((LENGTH, FIRST), BF16),
            pltpu.HBM((ROWS, LINE, INNER), BF16),
        ],
        scratch_shapes=[
            pltpu.VMEM((2 * HEADS, INNER), BF16),
            pltpu.VMEM((2 * STATE, INNER), BF16),
            pltpu.VMEM((ROWS, LINE, 2 * HEADS), BF16),
            pltpu.VMEM((FIRST // 128, 256, 128), F32),
        ],
        compiler_params=params(),
        cost_estimate=pl.CostEstimate(
            flops=2 * LENGTH * D * FIRST, bytes_accessed=16 << 20, transcendentals=LENGTH
        ),
        name="finish",
    )(*map(near, (local, gate, bcs, band_decay, entering, gain, tok, w_out)))


def rest_kernel(hidden, w_far, tok_far, out, turned, w, tok_all, sem):
    step = pl.program_id(0)
    part = pl.ds(FIRST, D - FIRST)
    fetch = [
        pltpu.make_async_copy(w_far.at[:, part], w, sem.at[0]),
        pltpu.make_async_copy(tok_far.at[:, :, part], tok_all, sem.at[1]),
    ]

    @pl.when(step == 0)
    def _():
        for copy in fetch:
            copy.start()
        for copy in fetch:
            copy.wait()

    here = pl.ds(pl.multiple_of(step * 32, 32), 32)
    columns_out(
        dot(hidden[...].reshape(256, INNER), w[...]),
        tok_all[:, here, :].reshape(256, D - FIRST),
        turned,
        out,
    )


def rest(hidden, tok, w_out):
    return pl.pallas_call(
        rest_kernel,
        grid=(LINE // 32,),
        in_specs=[pl.BlockSpec((ROWS, 32, INNER), lambda i: (0, i, 0)), far, far],
        out_specs=pl.BlockSpec((256, D - FIRST), lambda i: (i, 0)),
        out_shape=pltpu.HBM((LENGTH, D - FIRST), BF16),
        scratch_shapes=[
            pltpu.VMEM(((D - FIRST) // 128, 256, 128), F32),
            pltpu.VMEM((INNER, D - FIRST), BF16),
            pltpu.VMEM((ROWS, LINE, D - FIRST), BF16),
            pltpu.SemaphoreType.DMA((2,)),
        ],
        compiler_params=params(60),
        cost_estimate=pl.CostEstimate(
            flops=2 * LENGTH * D * (D - FIRST), bytes_accessed=8 << 20, transcendentals=0
        ),
        name="rest",
    )(hidden, hbm(w_out), hbm(tok))


def shards(
    tokens,
    in_gain,
    w_xbc,
    w_gate,
    w_dt,
    dt_bias,
    decay_rate,
    conv_w,
    conv_bias,
    skip,
    out_gain,
    w_out,
):
    bands = lax.axis_size("band")
    segments = lax.axis_size("segment")
    cells = tokens[0]
    tok = cells.reshape(LENGTH, D)
    top = lax.ppermute(cells[ROWS - 1], "band", [(i, i + 1) for i in range(bands - 1)])
    bottom = lax.ppermute(cells[0], "band", [(i + 1, i) for i in range(bands - 1)])

    (
        x,
        gate,
        rim,
        bcs,
        rim_bc,
        cum,
        dt,
        band_tail,
        band_decay,
        total,
        mid,
        w_xbc_near,
        in_gain_near,
        taps_near,
        bias_near,
    ) = project(
        tok,
        in_gain,
        w_xbc[0],
        w_gate[0],
        w_dt[0].T,
        dt_bias,
        decay_rate,
        conv_w.swapaxes(0, 1),
        conv_bias,
    )
    x, bcs, pieces = edges(
        top,
        bottom,
        in_gain_near,
        w_xbc_near,
        rim,
        rim_bc,
        taps_near,
        bias_near,
        band_tail,
        total,
        mid,
        x,
        bcs,
    )
    swap = functools.partial(
        lax.all_to_all, axis_name="band", split_axis=0, concat_axis=0, tiled=True
    )
    onward = functools.partial(
        lax.ppermute, axis_name="segment", perm=[(i, (i + 1) % segments) for i in range(segments)]
    )
    arrived = swap(pieces.reshape(BANDS, 16, GROUP + 128))
    local, gate, w_out_near, tok_near, bcs, band_decay, gain_near = scan(
        x, bcs, cum, dt, gate, skip, band_decay, out_gain, w_out[0], cells
    )
    arrived, local = lax.optimization_barrier((arrived, local))
    entering = swap(relay(arrived))

    grid = lambda a: a.reshape(ROWS, LINE, a.shape[-1])
    parted = lambda a: a.reshape(BANDS, LENGTH // BANDS, a.shape[-1])
    first, hidden = finish(
        grid(local), grid(gate), grid(bcs), band_decay, entering, gain_near, tok_near, w_out_near
    )
    first = swap(parted(first))
    second = onward(parted(rest(hidden, cells, w_out[0])))
    second = swap(second)
    first = onward(first)
    both = jnp.concatenate([first, second], axis=-1)
    handed = both.reshape(BANDS, LINE // BANDS, ROWS, D).swapaxes(0, 1)
    return handed.reshape(1, LINE // BANDS, BANDS * ROWS, D)


def solution(mesh):
    in_specs = (
        P("segment", "band", None, None),
        P("segment", None),
        P("segment", None, None),
        P("segment", None, None),
        P("segment", None, None),
        P("segment", None),
        P("segment", None),
        P("segment", None, None),
        P("segment", None),
        P("segment", None),
        P("segment", None),
        P("segment", None, None),
    )
    out_specs = P("segment", "band", None, None)
    return jax.shard_map(shards, mesh=mesh, in_specs=in_specs, out_specs=out_specs, check_vma=False)
```

```python
import functools

import jax
import jax.numpy as jnp
from jax import lax
from jax.experimental import pallas as pl
from jax.experimental.pallas import tpu as pltpu
from jax.sharding import PartitionSpec as P

EPSILON = 1e-05
ROWS = 8
LINE = 128
LENGTH = ROWS * LINE
HEADS = 24
WIDTH = 64
STATE = 64
INNER = HEADS * WIDTH
D = 1536
HALF = INNER // 2
FIRST = 896
GROUP = 384
GROUP_HEADS = GROUP // WIDTH
BANDS = 16
F32 = jnp.float32
BF16 = jnp.bfloat16
MIB = 1 << 20
LOG2E = 1.4426950408889634


def params(mib=24):
    return pltpu.CompilerParams(vmem_limit_bytes=mib * MIB)


kept = pl.BlockSpec(memory_space=pltpu.VMEM)
far = pl.BlockSpec(memory_space=pl.ANY)


def small(*shape):
    return pl.BlockSpec(shape, lambda *i: (0,) * len(shape))


def near(a):
    return pltpu.with_memory_space_constraint(a, pltpu.VMEM)


def hbm(a):
    return pltpu.with_memory_space_constraint(a, pltpu.HBM)


def upright(row):
    return jnp.broadcast_to(row, (LINE, HEADS)).T[:, :1]


def whole(*shape):
    return pl.BlockSpec(shape, lambda i: (0,) * len(shape), pipeline_mode=pl.Buffered(1))


def dot(a, b):
    return jnp.dot(a, b, preferred_element_type=F32)


def rms(values, gain):
    return values * lax.rsqrt(jnp.mean(values * values, -1, keepdims=True) + EPSILON) * gain


def silu(v):
    half = 0.5 * v
    return half + half * jnp.tanh(half)


def head_spread(channels, first):
    head = lax.broadcasted_iota(jnp.int32, (2 * HEADS, channels), 0)
    head = jnp.where(head < HEADS, head, head - HEADS)
    channel = lax.broadcasted_iota(jnp.int32, (2 * HEADS, channels), 1)
    return jnp.where(head - first == channel // WIDTH, 1.0, 0.0).astype(BF16)


def two_terms(values_t):
    high = values_t.astype(BF16).astype(F32)
    return jnp.concatenate([high, values_t - high], axis=0).T.astype(BF16)


def place(r):
    return (r + 1) % ROWS * LINE


def fill(padded, tile, slot, line):
    padded[tile, slot, pl.ds(8, LINE), :] = line.astype(F32)


def convolved(padded, tile, slot, taps, bias):
    total = bias
    for i in range(3):
        for j in range(3):
            total = total + padded[tile, slot - 1 + i, pl.ds(7 + j, LINE), :] * taps[3 * i + j]
    return silu(total).astype(BF16)


def lanes(refs, start):
    return [ref[:, start : start + 128] for ref in refs]


def project_kernel(
    tok,
    gain,
    w_xbc,
    w_g,
    w_dt,
    dt_bias,
    rate,
    taps_ref,
    bias,
    x,
    gate_out,
    rim,
    bcs,
    rim_bc,
    cum,
    dt,
    band_tail,
    band_decay,
    total,
    mid,
    w_near,
    gain_near,
    taps_near,
    bias_near,
    tok_near,
    gate,
    normed,
    lines_a,
    lines_b,
    lines_bc,
    b_t,
    tails,
    w_g_near,
    tok_sem,
    w_sem,
    w_g_sem,
    gate_sem,
):
    def tokens_in(m):
        part = pl.ds(m * 256, 256)
        return pltpu.make_async_copy(tok.at[part, :], tok_near.at[part, :], tok_sem.at[m])

    def w_in(n):
        part = pl.ds(n * 512, 512 if n < 3 else 128)
        return pltpu.make_async_copy(w_xbc.at[:, part], w_near.at[:, part], w_sem.at[n])

    def gate_in(n):
        part = pl.ds(n * 512, 512)
        return pltpu.make_async_copy(w_g.at[:, part], w_g_near.at[:, part], w_g_sem.at[n])

    def send_gate(n):
        part = pl.ds(n * 512, 512)
        return pltpu.make_async_copy(gate.at[:, part], gate_out.at[:, part], gate_sem.at[n])

    taps = [taps_ref[n] for n in range(9)]

    def store(m, values, padded, out, start, tiles, tile=0):
        for n in range(m * 2, m * 2 + 2):
            line = values[(n - m * 2) * LINE : (n - m * 2 + 1) * LINE]
            for k in range(tiles):
                fill(padded, tile + k, n, line[:, k * 128 : (k + 1) * 128])
            if n in (0, 1, 6, 7):
                place_n = (n if n < 2 else n - 4) * LINE
                out[pl.ds(place_n, LINE), pl.ds(start, tiles * 128)] = line

    def multiply_x(m, here, padded, chunk, side):
        start = chunk * 512 + side * 256
        values = dot(here, w_near[:, pl.ds(start, 256)]).astype(BF16)
        store(m, values, padded, rim, start, 2, side * 2)

    def multiply_gate(m, n, side):
        rows, part = pl.ds(m * 256, 256), pl.ds(n * 512 + side * 256, 256)
        gate[rows, part] = silu(dot(normed[rows, :], w_g_near[:, part])).astype(BF16)

    def inside(k, padded, chunk, rows):
        start = chunk * 512 + k * 128
        for r in rows:
            x[pl.ds(place(r), LINE), pl.ds(start, 128)] = convolved(
                padded, k, r, lanes(taps, start), bias[:, start : start + 128]
            )

    def add_state(piece):
        part = pl.ds(piece * 256, 256)
        spread = head_spread(256, piece * 4)
        own = x[pl.ds(2 * LINE, (ROWS - 2) * LINE), part].astype(F32)
        mid[:, part] = dot(b_t[pl.ds(0, STATE), :], (own * dot(tails[...], spread)).astype(BF16))

    tokens_in(0).start()
    w_in(3).start()
    w_in(0).start()
    for m in range(1, 4):
        tokens_in(m).start()
    w_in(1).start()
    w_in(2).start()
    for n in range(3):
        gate_in(n).start()
    gain_near[...] = gain[...]
    taps_near[...] = taps_ref[...]
    bias_near[...] = bias[...]
    for padded in (lines_a, lines_b, lines_bc):
        for n in range(ROWS):
            for k in range(padded.shape[0]):
                padded[k, n, pl.ds(0, 8), :] = jnp.zeros((8, 128), F32)
                padded[k, n, pl.ds(LINE + 8, 8), :] = jnp.zeros((8, 128), F32)
    for m in range(4):
        tokens_in(m).wait()
        if m == 0:
            w_in(3).wait()
            w_in(0).wait()
        part = pl.ds(m * 256, 256)
        here = rms(tok_near[part, :].astype(F32), gain[...]).astype(BF16)
        normed[part, :] = here
        store(m, dot(here, w_near[:, pl.ds(INNER, 128)]).astype(BF16), lines_bc, rim_bc, 0, 1)
        for side in range(2):
            multiply_x(m, here, lines_a, 0, side)

    w_in(1).wait()
    for r in range(1, ROWS - 1):
        values = convolved(
            lines_bc, 0, r, lanes(taps, INNER), bias[:, INNER : INNER + 128]
        )
        bcs[pl.ds(place(r), LINE), :] = values
        b_t[:, pl.ds((r - 1) * LINE, LINE)] = values.astype(F32).T.astype(BF16)
    raw = lax.dot_general(
        w_dt[...], normed[...], (((1,), (1,)), ((), ())), preferred_element_type=F32
    ) + upright(dt_bias[...])
    steps = jnp.maximum(raw, 0.0) + jnp.log1p(jnp.exp(-jnp.abs(raw)))
    dt[...] = steps
    for m in range(4):
        for side in range(2):
            multiply_x(m, normed[pl.ds(m * 256, 256), :], lines_b, 1, side)
            inside(m, lines_a, 0, range(1 + 3 * side, 4 + 3 * side))

    w_in(2).wait()
    log_decay = -upright(rate[...]) * steps
    i = lax.broadcasted_iota(jnp.int32, (LINE, LINE), 0)
    j = lax.broadcasted_iota(jnp.int32, (LINE, LINE), 1)
    sums = jnp.dot(
        jnp.concatenate([log_decay[:, r * LINE : (r + 1) * LINE] for r in range(ROWS)], axis=0),
        jnp.where(i <= j, 1.0, 0.0).astype(F32),
        precision=lax.Precision.HIGHEST,
        preferred_element_type=F32,
    )
    lines = [sums[r * HEADS : (r + 1) * HEADS] for r in range(ROWS)]
    ends = [line[:, LINE - 1 :] for line in lines]
    before = [jnp.zeros_like(ends[0])]
    after = [jnp.zeros_like(ends[0])]
    for r in range(ROWS - 1):
        before.append(before[-1] + ends[r])
        after.append(after[-1] + ends[ROWS - 1 - r])
    for r in range(ROWS):
        part = slice(r * LINE, (r + 1) * LINE)
        cum[:, part] = lines[r]
        band_decay[:, part] = jnp.exp(lines[r] + before[r])
        tail = steps[:, part] * jnp.exp((ends[r] - lines[r]) + after[ROWS - 1 - r])
        band_tail[:, part] = tail
        if 0 < r < ROWS - 1:
            tails[pl.ds((r - 1) * LINE, LINE), :] = two_terms(tail)
    total[...] = jnp.broadcast_to(before[-1] + ends[-1], (HEADS, LINE)).T[:1]
    for m in range(4):
        for side in range(2):
            multiply_x(m, normed[pl.ds(m * 256, 256), :], lines_a, 2, side)
            inside(m, lines_b, 1, range(1 + 3 * side, 4 + 3 * side))

    gate_in(0).wait()
    for m in range(4):
        for side in range(2):
            multiply_gate(m, 0, side)
            inside(m, lines_a, 2, range(1 + 3 * side, 4 + 3 * side))
    send_gate(0).start()
    for n in (1, 2):
        gate_in(n).wait()
        for m in range(4):
            for side in range(2):
                multiply_gate(m, n, side)
            if m < 3:
                add_state((n - 1) * 3 + m)
        send_gate(n).start()
    for n in range(3):
        send_gate(n).wait()


def project(tok, gain, w_xbc, w_gate, w_dt_t, dt_bias, rate, taps, conv_bias):
    per_head = pltpu.HBM((HEADS, LENGTH), F32)
    return pl.pallas_call(
        project_kernel,
        in_specs=[
            far,
            small(1, D),
            far,
            far,
            small(HEADS, D),
            small(1, HEADS),
            small(1, HEADS),
            small(9, 1, INNER + 128),
            small(1, INNER + 128),
        ],
        out_specs=[kept, far, kept, kept, kept]
        + [small(HEADS, LENGTH)] * 2
        + [kept]
        + [small(HEADS, LENGTH)]
        + [kept] * 6,
        out_shape=[
            pltpu.VMEM((LENGTH, INNER), BF16),
            pltpu.HBM((LENGTH, INNER), BF16),
            pltpu.VMEM((4 * LINE, INNER), BF16),
            pltpu.VMEM((LENGTH, 128), BF16),
            pltpu.VMEM((4 * LINE, 128), BF16),
            per_head,
            per_head,
            pltpu.VMEM((HEADS, LENGTH), F32),
            per_head,
            pltpu.VMEM((1, HEADS), F32),
            pltpu.VMEM((STATE, INNER), F32),
            pltpu.VMEM((D, INNER + 128), BF16),
            pltpu.VMEM((1, D), F32),
            pltpu.VMEM((9, 1, INNER + 128), F32),
            pltpu.VMEM((1, INNER + 128), F32),
        ],
        scratch_shapes=[
            pltpu.VMEM((LENGTH, D), BF16),
            pltpu.VMEM((LENGTH, INNER), BF16),
            pltpu.VMEM((LENGTH, D), BF16),
            pltpu.VMEM((4, ROWS, LINE + 16, 128), F32),
            pltpu.VMEM((4, ROWS, LINE + 16, 128), F32),
            pltpu.VMEM((1, ROWS, LINE + 16, 128), F32),
            pltpu.VMEM((128, (ROWS - 2) * LINE), BF16),
            pltpu.VMEM(((ROWS - 2) * LINE, 2 * HEADS), BF16),
            pltpu.VMEM((D, INNER), BF16),
            pltpu.SemaphoreType.DMA((4,)),
            pltpu.SemaphoreType.DMA((4,)),
            pltpu.SemaphoreType.DMA((3,)),
            pltpu.SemaphoreType.DMA((3,)),
        ],
        compiler_params=params(),
        cost_estimate=pl.CostEstimate(
            flops=2 * LENGTH * D * 3224, bytes_accessed=20 << 20, transcendentals=LENGTH * INNER
        ),
        name="project",
    )(hbm(tok), hbm(gain), hbm(w_xbc), hbm(w_gate), *map(hbm, (w_dt_t, dt_bias, rate, taps, conv_bias)))


def edge_kernel(
    top,
    bottom,
    gain,
    w_near,
    rim,
    rim_bc,
    taps_ref,
    bias,
    band_tail,
    total,
    mid,
    x_near,
    bcs_near,
    x_out,
    bcs,
    pieces,
    x,
    edge,
    lines,
    b_t,
    tails,
    mid_sem,
    edge_sem,
):
    inner_part = pl.ds(2 * LINE, (ROWS - 2) * LINE)
    send_mid = pltpu.make_async_copy(x_near.at[inner_part, :], x_out.at[inner_part, :], mid_sem)
    send_mid.start()

    def send_edge(n):
        rows, part = pl.ds(0, 2 * LINE), pl.ds(n * 512, 512)
        return pltpu.make_async_copy(x.at[:, part], x_out.at[rows, part], edge_sem.at[n])

    bcs[inner_part, :] = bcs_near[inner_part, :]
    taps = [taps_ref[n] for n in range(9)]

    def both(side, own, own_start, start, out, out_start, tiles):
        for k in range(tiles):
            part = slice(k * 128, (k + 1) * 128)
            own_part = pl.ds(own_start + k * 128, 128)
            tile = start // 128 + k
            for slot, line in enumerate(
                [side[:LINE, part], own[pl.ds(0, LINE), own_part], own[pl.ds(LINE, LINE), own_part]]
                + [own[pl.ds(2 * LINE, LINE), own_part], own[pl.ds(3 * LINE, LINE), own_part]]
                + [side[LINE:, part]]
            ):
                fill(lines, tile % 4, slot, line)
            for slot, r in ((1, 0), (4, ROWS - 1)):
                out[pl.ds(place(r), LINE), pl.ds(out_start + k * 128, 128)] = convolved(
                    lines, tile % 4, slot, lanes(taps, tile * 128), bias[:, tile * 128 : tile * 128 + 128]
                )

    for slot in range(6):
        for k in range(4):
            lines[k, slot, pl.ds(0, 8), :] = jnp.zeros((8, 128), F32)
            lines[k, slot, pl.ds(LINE + 8, 8), :] = jnp.zeros((8, 128), F32)
    tails[pl.ds(place(0), LINE), :] = two_terms(band_tail[:, :LINE])
    tails[pl.ds(place(ROWS - 1), LINE), :] = two_terms(band_tail[:, LENGTH - LINE :])
    head = lax.broadcasted_iota(jnp.int32, (HEADS, 128), 0)
    lane = lax.broadcasted_iota(jnp.int32, (HEADS, 128), 1)
    first = total[...].astype(BF16)
    rest = total[...] - first.astype(F32)
    second = rest.astype(BF16)
    third = (rest - second.astype(F32)).astype(BF16)
    for g in range(4):
        pick = jnp.where(head == lane + g * GROUP_HEADS, 1.0, 0.0).astype(BF16)
        terms = jnp.concatenate(
            [dot(jnp.broadcast_to(t, (8, HEADS)), pick)[:1] for t in (first, second, third)]
            + [jnp.zeros((13, 128), F32)],
            axis=0,
        ).astype(BF16)
        for a in range(4):
            pieces[a, g, :, pl.ds(GROUP, 128)] = terms
    for n, side in enumerate((top, bottom)):
        edge[pl.ds(n * LINE, LINE), :] = rms(side[...].astype(F32), gain[...]).astype(BF16)
    both(dot(edge[...], w_near[:, pl.ds(INNER, 128)]).astype(BF16), rim_bc, 0, INNER, bcs, 0, 1)
    b_t[...] = bcs[pl.ds(0, 2 * LINE), :].astype(F32).T.astype(BF16)
    for n in range(3):
        start = n * 512
        part = pl.ds(start, 512)
        both(dot(edge[...], w_near[:, part]).astype(BF16), rim, start, start, x, start, 4)
        send_edge(n).start()
        weighted = x[:, part].astype(F32) * dot(tails[...], head_spread(512, n * 8))
        state = mid[:, part] + dot(b_t[pl.ds(0, STATE), :], weighted.astype(BF16))
        for k in range(4):
            g, within = divmod(n * 4 + k, 3)
            for a in range(4):
                pieces[a, g, :, pl.ds(within * 128, 128)] = state[
                    16 * a : 16 * a + 16, k * 128 : (k + 1) * 128
                ].astype(BF16)
    send_mid.wait()
    for n in range(3):
        send_edge(n).wait()


def edges(top, bottom, gain, w_near, rim, rim_bc, taps, conv_bias, band_tail, total, mid, x, bcs):
    return pl.pallas_call(
        edge_kernel,
        in_specs=[kept] * 13,
        out_specs=[far, small(LENGTH, 128), small(4, 4, 16, GROUP + 128)],
        out_shape=[
            pltpu.HBM((LENGTH, INNER), BF16),
            pltpu.HBM((LENGTH, 128), BF16),
            pltpu.HBM((4, 4, 16, GROUP + 128), BF16),
        ],
        scratch_shapes=[
            pltpu.VMEM((2 * LINE, INNER), BF16),
            pltpu.VMEM((2 * LINE, D), BF16),
            pltpu.VMEM((4, 6, LINE + 16, 128), F32),
            pltpu.VMEM((128, 2 * LINE), BF16),
            pltpu.VMEM((2 * LINE, 2 * HEADS), BF16),
            pltpu.SemaphoreType.DMA(()),
            pltpu.SemaphoreType.DMA((3,)),
        ],
        compiler_params=params(),
        cost_estimate=pl.CostEstimate(
            flops=2 * 256 * D * 1664 + 10 * LENGTH * 1664,
            bytes_accessed=10 << 20,
            transcendentals=256 * 1664,
        ),
        name="edges",
    )(
        near(top),
        near(bottom),
        near(gain),
        near(w_near),
        near(rim),
        near(rim_bc),
        near(taps),
        near(conv_bias),
        near(band_tail),
        near(total),
        near(mid),
        near(x),
        near(bcs),
    )


def scan_kernel(
    x_far,
    bcs,
    cum,
    dt,
    gate_far,
    skip,
    out_far,
    out,
    gate,
    x,
    direct,
    state,
    sums,
    steps,
    weights,
    b_t,
    c,
    sem,
):
    def rows_of(place):
        return pl.ds(pl.multiple_of(place * LINE, LINE), LINE)

    def x_in(r):
        rows = rows_of(lax.rem(r + 1, ROWS))
        return pltpu.make_async_copy(x_far.at[rows, :], x.at[rows, :], sem.at[0, r])

    def gate_in(r):
        rows = rows_of(r)
        return pltpu.make_async_copy(gate_far.at[rows, :], gate.at[rows, :], sem.at[1, r])

    def send(r):
        rows = rows_of(r)
        return pltpu.make_async_copy(out.at[rows, :], out_far.at[rows, :], sem.at[2, r])

    for r in range(ROWS):
        x_in(r).start()
        gate_in(r).start()
    lane = lax.broadcasted_iota(jnp.int32, (LINE, LINE), 1)
    row = lax.broadcasted_iota(jnp.int32, (LINE, LINE), 0)
    left = lane < WIDTH
    direct[...] = dot(
        two_terms(jnp.broadcast_to(upright(skip[...]), (HEADS, 8))),
        head_spread(INNER, 0),
    )
    state[...] = jnp.zeros_like(state)
    for r in range(ROWS):
        part = slice(r * LINE, (r + 1) * LINE)
        sums[r] = (cum[:, part] * LOG2E).T
        steps[r] = dt[:, part].T
        both = bcs[pl.ds(place(r), LINE), :].astype(F32)
        b_t[r] = both.T.astype(BF16)[:STATE]
        c[r] = pltpu.roll(both, STATE, 1).astype(BF16)[:, :STATE]
    for r in range(ROWS):
        weights[r] = jnp.where(row >= lane, dot(c[r], b_t[r]), 0.0)

    def line(r):
        rows, placed_rows = rows_of(r), rows_of(lax.rem(r + 1, ROWS))
        sums_here, steps_here, weights_here = sums[r], steps[r], weights[r]
        sums_t = cum[:, rows] * LOG2E
        steps_t = dt[:, rows]

        def mixing(h):
            along = jnp.broadcast_to(sums_here[:, h : h + 1], (LINE, LINE))
            decay = jnp.exp2(jnp.minimum(along - sums_t[h : h + 1], 0.0))
            return along, (decay * (weights_here * steps_t[h : h + 1])).astype(BF16)

        for q in range(HEADS // 4):
            quad = pl.ds(q * 256, 256)
            carried = dot(c[r], state[:, quad].astype(BF16))
            tails, decays = [], []
            for p in (2 * q, 2 * q + 1):
                part = pl.ds(p * 128, 128)
                h = 2 * p
                values = x[placed_rows, part].astype(F32)
                (along_a, mixing_a), (along_b, mixing_b) = mixing(h), mixing(h + 1)
                columns = jnp.concatenate(
                    [jnp.where(left, values, 0.0), jnp.where(left, 0.0, values)], axis=0
                ).astype(BF16)
                inner = dot(jnp.concatenate([mixing_a, mixing_b], axis=1), columns)
                here = jnp.where(left, along_a, along_b)
                carry = jnp.exp2(here)
                stepped = jnp.where(left, steps_here[:, h : h + 1], steps_here[:, h + 1 : h + 2])
                tails.append((values * stepped * jnp.exp2(here[LINE - 1 :] - here)).astype(BF16))
                decays.append(carry[LINE - 1 :])
                side = slice((p % 2) * 128, (p % 2) * 128 + 128)
                y = inner + carry * carried[:, side] + direct[0:1, part] * values
                out[rows, part] = (y * gate[rows, part].astype(F32)).astype(BF16)
            state[:, quad] = jnp.concatenate(decays, axis=1) * state[:, quad] + dot(
                b_t[r], jnp.concatenate(tails, axis=1)
            )

    @pl.loop(0, ROWS // 2)
    def _(pair):
        for r in (2 * pair, 2 * pair + 1):
            x_in(r).wait()
            gate_in(r).wait()
        for r in (2 * pair, 2 * pair + 1):
            line(r)
            send(r).start()

    for r in range(ROWS):
        send(r).wait()


def scan(x, bcs, cum, dt, gate, skip):
    return pl.pallas_call(
        scan_kernel,
        in_specs=[
            far,
            small(LENGTH, 128),
            small(HEADS, LENGTH),
            small(HEADS, LENGTH),
            far,
            small(1, HEADS),
        ],
        out_specs=far,
        out_shape=pltpu.HBM((LENGTH, INNER), BF16),
        scratch_shapes=[
            pltpu.VMEM((LENGTH, INNER), BF16),
            pltpu.VMEM((LENGTH, INNER), BF16),
            pltpu.VMEM((LENGTH, INNER), BF16),
            pltpu.VMEM((8, INNER), F32),
            pltpu.VMEM((STATE, INNER), F32),
            pltpu.VMEM((ROWS, LINE, HEADS), F32),
            pltpu.VMEM((ROWS, LINE, HEADS), F32),
            pltpu.VMEM((ROWS, LINE, LINE), F32),
            pltpu.VMEM((ROWS, STATE, LINE), BF16),
            pltpu.VMEM((ROWS, LINE, STATE), BF16),
            pltpu.SemaphoreType.DMA((3, ROWS)),
        ],
        compiler_params=params(48),
        cost_estimate=pl.CostEstimate(
            flops=4 << 30, bytes_accessed=20 << 20, transcendentals=LENGTH * LINE * HEADS
        ),
        name="scan",
    )(*map(hbm, (x, bcs, cum, dt, gate, skip)))


def relay_kernel(arrived, out):
    logs = jnp.concatenate(
        [
            jnp.sum(arrived[j, :, pl.ds(GROUP, 128)].astype(F32), axis=0, keepdims=True)
            for j in range(BANDS)
        ],
        axis=0,
    )
    decay = jnp.exp(logs)
    high = decay.astype(BF16)
    low = (decay - high.astype(F32)).astype(BF16)
    lane = lax.broadcasted_iota(jnp.int32, (128, GROUP), 0)
    channel = lax.broadcasted_iota(jnp.int32, (128, GROUP), 1)
    spread = jnp.where(lane == channel // WIDTH, 1.0, 0.0).astype(BF16)
    wide = dot(high, spread) + dot(low, spread)
    state = jnp.zeros((16, GROUP), F32)
    for j in range(BANDS):
        out[j] = state.astype(BF16)
        state = wide[j : j + 1] * state + arrived[j, :, pl.ds(0, GROUP)].astype(F32)


def relay(arrived):
    return pl.pallas_call(
        relay_kernel,
        out_specs=kept,
        out_shape=pltpu.VMEM((BANDS, 16, GROUP), BF16),
        compiler_params=params(16),
        name="relay",
    )(arrived)


def columns_out(values, tokens, turned, out, rows=slice(None)):
    values = values + tokens.astype(F32)
    for k in range(values.shape[1] // 128):
        part = slice(k * 128, (k + 1) * 128)
        for r in range(ROWS):
            turned[k, pl.ds(r, 32, stride=ROWS), :] = values[r * 32 : (r + 1) * 32, part]
        out[rows, part] = turned[k].astype(BF16)


def finish_kernel(
    local_far,
    gate_far,
    bcs,
    band_decay,
    entering,
    gain,
    tok_far,
    w_far,
    out_far,
    hidden_far,
    local,
    gate,
    tok,
    w,
    out,
    hidden,
    spread,
    state,
    decays,
    turned,
    sem,
    w_sem,
):
    def columns_of(step):
        return pl.ds(pl.multiple_of(step * 32, 32), 32)

    def rows_of(step):
        return pl.ds(pl.multiple_of(step * 256, 256), 256)

    def local_in(step):
        here = columns_of(step)
        return pltpu.make_async_copy(local_far.at[:, here, :], local.at[:, here, :], sem.at[0, step])

    def gate_in(step):
        here = columns_of(step)
        return pltpu.make_async_copy(gate_far.at[:, here, :], gate.at[:, here, :], sem.at[1, step])

    def tok_in(step):
        here = columns_of(step)
        return pltpu.make_async_copy(
            tok_far.at[:, here, pl.ds(0, FIRST)], tok.at[:, here, :], sem.at[2, step]
        )

    def send_hidden(step):
        here = columns_of(step)
        return pltpu.make_async_copy(hidden.at[:, here, :], hidden_far.at[:, here, :], sem.at[3, step])

    def send_out(step):
        rows = rows_of(step)
        return pltpu.make_async_copy(out.at[rows, :], out_far.at[rows, :], sem.at[4, step])

    fetch = pltpu.make_async_copy(w_far.at[:, pl.ds(0, FIRST)], w, w_sem)
    for step in range(4):
        local_in(step).start()
        gate_in(step).start()
        if step == 0:
            fetch.start()
        tok_in(step).start()
    spread[...] = head_spread(INNER, 0)
    state[pl.ds(0, STATE), :] = jnp.zeros((STATE, INNER), BF16)
    for a in range(4):
        for g in range(4):
            state[pl.ds(STATE + 16 * a, 16), pl.ds(g * GROUP, GROUP)] = entering[4 * a + g]
    for r in range(ROWS):
        decays[r] = two_terms(band_decay[:, r * LINE : (r + 1) * LINE])

    @pl.loop(0, 4)
    def _(step):
        here = columns_of(step)
        cells = lambda ref: ref[:, here, :].reshape(256, ref.shape[2])
        both = jnp.concatenate([bcs[1:, here, :], bcs[:1, here, :]], axis=0).reshape(256, 128)
        entered = dot(both, state[...]) * dot(cells(decays), spread[...])
        local_in(step).wait()
        gate_in(step).wait()
        gated = cells(local).astype(F32) + entered * cells(gate).astype(F32)
        normed = rms(gated, gain[...]).astype(BF16)
        hidden[:, here, :] = normed.reshape(ROWS, 32, INNER)
        send_hidden(step).start()

        @pl.when(step == 0)
        def _():
            fetch.wait()

        tok_in(step).wait()
        columns_out(dot(normed, w[...]), cells(tok), turned, out, rows_of(step))
        send_out(step).start()

    for step in range(4):
        send_hidden(step).wait()
        send_out(step).wait()


def finish(local, gate, bcs, band_decay, entering, gain, tok, w_out):
    return pl.pallas_call(
        finish_kernel,
        in_specs=[
            far,
            far,
            small(ROWS, LINE, 128),
            small(HEADS, LENGTH),
            kept,
            small(1, INNER),
            far,
            far,
        ],
        out_specs=[far, far],
        out_shape=[
            pltpu.HBM((LENGTH, FIRST), BF16),
            pltpu.HBM((ROWS, LINE, INNER), BF16),
        ],
        scratch_shapes=[
            pltpu.VMEM((ROWS, LINE, INNER), BF16),
            pltpu.VMEM((ROWS, LINE, INNER), BF16),
            pltpu.VMEM((ROWS, LINE, FIRST), BF16),
            pltpu.VMEM((INNER, FIRST), BF16),
            pltpu.VMEM((LENGTH, FIRST), BF16),
            pltpu.VMEM((ROWS, LINE, INNER), BF16),
            pltpu.VMEM((2 * HEADS, INNER), BF16),
            pltpu.VMEM((2 * STATE, INNER), BF16),
            pltpu.VMEM((ROWS, LINE, 2 * HEADS), BF16),
            pltpu.VMEM((FIRST // 128, 256, 128), F32),
            pltpu.SemaphoreType.DMA((5, 4)),
            pltpu.SemaphoreType.DMA(()),
        ],
        compiler_params=params(48),
        cost_estimate=pl.CostEstimate(
            flops=2 * LENGTH * D * FIRST, bytes_accessed=16 << 20, transcendentals=LENGTH
        ),
        name="finish",
    )(
        hbm(local),
        hbm(gate),
        hbm(bcs),
        hbm(band_decay),
        near(entering),
        hbm(gain),
        hbm(tok),
        hbm(w_out),
    )


def rest_kernel(hidden, w_far, tok_far, out, turned, w, tok_all, sem):
    step = pl.program_id(0)
    part = pl.ds(FIRST, D - FIRST)
    fetch = [
        pltpu.make_async_copy(w_far.at[:, part], w, sem.at[0]),
        pltpu.make_async_copy(tok_far.at[:, :, part], tok_all, sem.at[1]),
    ]

    @pl.when(step == 0)
    def _():
        for copy in fetch:
            copy.start()
        for copy in fetch:
            copy.wait()

    here = pl.ds(pl.multiple_of(step * 32, 32), 32)
    columns_out(
        dot(hidden[...].reshape(256, INNER), w[...]),
        tok_all[:, here, :].reshape(256, D - FIRST),
        turned,
        out,
    )


def rest(hidden, tok, w_out):
    return pl.pallas_call(
        rest_kernel,
        grid=(LINE // 32,),
        in_specs=[pl.BlockSpec((ROWS, 32, INNER), lambda i: (0, i, 0)), far, far],
        out_specs=pl.BlockSpec((256, D - FIRST), lambda i: (i, 0)),
        out_shape=pltpu.HBM((LENGTH, D - FIRST), BF16),
        scratch_shapes=[
            pltpu.VMEM(((D - FIRST) // 128, 256, 128), F32),
            pltpu.VMEM((INNER, D - FIRST), BF16),
            pltpu.VMEM((ROWS, LINE, D - FIRST), BF16),
            pltpu.SemaphoreType.DMA((2,)),
        ],
        compiler_params=params(60),
        cost_estimate=pl.CostEstimate(
            flops=2 * LENGTH * D * (D - FIRST), bytes_accessed=8 << 20, transcendentals=0
        ),
        name="rest",
    )(hidden, hbm(w_out), hbm(tok))


def shards(
    tokens,
    in_gain,
    w_xbc,
    w_gate,
    w_dt,
    dt_bias,
    decay_rate,
    conv_w,
    conv_bias,
    skip,
    out_gain,
    w_out,
):
    bands = lax.axis_size("band")
    segments = lax.axis_size("segment")
    cells = tokens[0]
    tok = cells.reshape(LENGTH, D)
    top = lax.ppermute(cells[ROWS - 1], "band", [(i, i + 1) for i in range(bands - 1)])
    bottom = lax.ppermute(cells[0], "band", [(i + 1, i) for i in range(bands - 1)])

    (
        x,
        gate,
        rim,
        bcs,
        rim_bc,
        cum,
        dt,
        band_tail,
        band_decay,
        total,
        mid,
        w_xbc_near,
        in_gain_near,
        taps_near,
        bias_near,
    ) = project(
        tok,
        in_gain,
        w_xbc[0],
        w_gate[0],
        w_dt[0].T,
        dt_bias,
        decay_rate,
        conv_w.swapaxes(0, 1),
        conv_bias,
    )
    x, bcs, pieces = edges(
        top,
        bottom,
        in_gain_near,
        w_xbc_near,
        rim,
        rim_bc,
        taps_near,
        bias_near,
        band_tail,
        total,
        mid,
        x,
        bcs,
    )
    swap = functools.partial(
        lax.all_to_all, axis_name="band", split_axis=0, concat_axis=0, tiled=True
    )
    onward = functools.partial(
        lax.ppermute, axis_name="segment", perm=[(i, (i + 1) % segments) for i in range(segments)]
    )
    arrived = swap(pieces.reshape(BANDS, 16, GROUP + 128))
    local = scan(x, bcs, cum, dt, gate, skip)
    arrived, local = lax.optimization_barrier((arrived, local))
    entering = swap(relay(arrived))

    grid = lambda a: a.reshape(ROWS, LINE, a.shape[-1])
    parted = lambda a: a.reshape(BANDS, LENGTH // BANDS, a.shape[-1])
    first, hidden = finish(
        grid(local), grid(gate), grid(bcs), band_decay, entering, out_gain, cells, w_out[0]
    )
    first = swap(parted(first))
    second = onward(parted(rest(hidden, cells, w_out[0])))
    second = swap(second)
    first = onward(first)
    both = jnp.concatenate([first, second], axis=-1)
    handed = both.reshape(BANDS, LINE // BANDS, ROWS, D).swapaxes(0, 1)
    return handed.reshape(1, LINE // BANDS, BANDS * ROWS, D)


def solution(mesh):
    in_specs = (
        P("segment", "band", None, None),
        P("segment", None),
        P("segment", None, None),
        P("segment", None, None),
        P("segment", None, None),
        P("segment", None),
        P("segment", None),
        P("segment", None, None),
        P("segment", None),
        P("segment", None),
        P("segment", None),
        P("segment", None, None),
    )
    out_specs = P("segment", "band", None, None)
    return jax.shard_map(shards, mesh=mesh, in_specs=in_specs, out_specs=out_specs, check_vma=False)
```

```python
import functools

import jax
import jax.numpy as jnp
from jax import lax
from jax.experimental import pallas as pl
from jax.experimental.pallas import tpu as pltpu
from jax.sharding import PartitionSpec as P

EPSILON = 1e-05
ROWS = 8
LINE = 128
LENGTH = ROWS * LINE
HEADS = 24
WIDTH = 64
STATE = 64
INNER = HEADS * WIDTH
D = 1536
HALF = INNER // 2
FIRST = 896
GROUP = 384
GROUP_HEADS = GROUP // WIDTH
BANDS = 16
F32 = jnp.float32
BF16 = jnp.bfloat16
MIB = 1 << 20
LOG2E = 1.4426950408889634


def params(mib=24):
    return pltpu.CompilerParams(vmem_limit_bytes=mib * MIB)


kept = pl.BlockSpec(memory_space=pltpu.VMEM)
far = pl.BlockSpec(memory_space=pl.ANY)


def small(*shape):
    return pl.BlockSpec(shape, lambda *i: (0,) * len(shape))


def near(a):
    return pltpu.with_memory_space_constraint(a, pltpu.VMEM)


def hbm(a):
    return pltpu.with_memory_space_constraint(a, pltpu.HBM)


def upright(row):
    return jnp.broadcast_to(row, (LINE, HEADS)).T[:, :1]


def whole(*shape):
    return pl.BlockSpec(shape, lambda i: (0,) * len(shape), pipeline_mode=pl.Buffered(1))


def dot(a, b):
    return jnp.dot(a, b, preferred_element_type=F32)


def rms(values, gain):
    return values * lax.rsqrt(jnp.mean(values * values, -1, keepdims=True) + EPSILON) * gain


def silu(v):
    half = 0.5 * v
    return half + half * jnp.tanh(half)


def head_spread(channels, first):
    head = lax.broadcasted_iota(jnp.int32, (2 * HEADS, channels), 0)
    head = jnp.where(head < HEADS, head, head - HEADS)
    channel = lax.broadcasted_iota(jnp.int32, (2 * HEADS, channels), 1)
    return jnp.where(head - first == channel // WIDTH, 1.0, 0.0).astype(BF16)


def two_terms(values_t):
    high = values_t.astype(BF16).astype(F32)
    return jnp.concatenate([high, values_t - high], axis=0).T.astype(BF16)


def place(r):
    return (r + 1) % ROWS * LINE


def fill(padded, tile, slot, line):
    padded[tile, slot, pl.ds(8, LINE), :] = line.astype(F32)


def convolved(padded, tile, slot, taps, bias):
    total = bias
    for i in range(3):
        for j in range(3):
            total = total + padded[tile, slot - 1 + i, pl.ds(7 + j, LINE), :] * taps[3 * i + j]
    return silu(total).astype(BF16)


def lanes(refs, start):
    return [ref[:, start : start + 128] for ref in refs]


def project_kernel(
    tok,
    gain,
    w_xbc,
    w_g,
    w_dt,
    dt_bias,
    rate,
    taps_ref,
    bias,
    skip,
    out_gain,
    x,
    gate,
    rim,
    bcs,
    rim_bc,
    cum,
    dt,
    band_tail,
    band_decay,
    total,
    mid,
    w_near,
    tok_near,
    gain_near,
    taps_near,
    bias_near,
    skip_near,
    out_gain_near,
    normed,
    lines_a,
    lines_b,
    lines_bc,
    b_t,
    tails,
    w_g_near,
    tok_sem,
    w_sem,
    w_g_sem,
):
    def tokens_in(m):
        part = pl.ds(m * 256, 256)
        return pltpu.make_async_copy(tok.at[part, :], tok_near.at[part, :], tok_sem.at[m])

    def w_in(n):
        part = pl.ds(n * 512, 512 if n < 3 else 128)
        return pltpu.make_async_copy(w_xbc.at[:, part], w_near.at[:, part], w_sem.at[n])

    def gate_in(n):
        part = pl.ds(n * 512, 512)
        return pltpu.make_async_copy(w_g.at[:, part], w_g_near.at[:, part], w_g_sem.at[n])

    taps = [taps_ref[n] for n in range(9)]

    def store(m, values, padded, out, start, tiles, tile=0):
        for n in range(m * 2, m * 2 + 2):
            line = values[(n - m * 2) * LINE : (n - m * 2 + 1) * LINE]
            for k in range(tiles):
                fill(padded, tile + k, n, line[:, k * 128 : (k + 1) * 128])
            if n in (0, 1, 6, 7):
                place_n = (n if n < 2 else n - 4) * LINE
                out[pl.ds(place_n, LINE), pl.ds(start, tiles * 128)] = line

    def multiply_x(m, here, padded, chunk, side):
        start = chunk * 512 + side * 256
        values = dot(here, w_near[:, pl.ds(start, 256)]).astype(BF16)
        store(m, values, padded, rim, start, 2, side * 2)

    def multiply_gate(m, n, side):
        rows, part = pl.ds(m * 256, 256), pl.ds(n * 512 + side * 256, 256)
        gate[rows, part] = silu(dot(normed[rows, :], w_g_near[:, part])).astype(BF16)

    def inside(k, padded, chunk, rows):
        start = chunk * 512 + k * 128
        for r in rows:
            x[pl.ds(place(r), LINE), pl.ds(start, 128)] = convolved(
                padded, k, r, lanes(taps, start), bias[:, start : start + 128]
            )

    def add_state(piece):
        part = pl.ds(piece * 256, 256)
        spread = head_spread(256, piece * 4)
        own = x[pl.ds(2 * LINE, (ROWS - 2) * LINE), part].astype(F32)
        mid[:, part] = dot(b_t[pl.ds(0, STATE), :], (own * dot(tails[...], spread)).astype(BF16))

    tokens_in(0).start()
    w_in(3).start()
    w_in(0).start()
    for m in range(1, 4):
        tokens_in(m).start()
    w_in(1).start()
    w_in(2).start()
    for n in range(3):
        gate_in(n).start()
    gain_near[...] = gain[...]
    taps_near[...] = taps_ref[...]
    bias_near[...] = bias[...]
    skip_near[...] = skip[...]
    out_gain_near[...] = out_gain[...]
    for padded in (lines_a, lines_b, lines_bc):
        for n in range(ROWS):
            for k in range(padded.shape[0]):
                padded[k, n, pl.ds(0, 8), :] = jnp.zeros((8, 128), F32)
                padded[k, n, pl.ds(LINE + 8, 8), :] = jnp.zeros((8, 128), F32)
    for m in range(4):
        tokens_in(m).wait()
        if m == 0:
            w_in(3).wait()
            w_in(0).wait()
        part = pl.ds(m * 256, 256)
        here = rms(tok_near[part, :].astype(F32), gain[...]).astype(BF16)
        normed[part, :] = here
        store(m, dot(here, w_near[:, pl.ds(INNER, 128)]).astype(BF16), lines_bc, rim_bc, 0, 1)
        for side in range(2):
            multiply_x(m, here, lines_a, 0, side)

    w_in(1).wait()
    for r in range(1, ROWS - 1):
        values = convolved(
            lines_bc, 0, r, lanes(taps, INNER), bias[:, INNER : INNER + 128]
        )
        bcs[pl.ds(place(r), LINE), :] = values
        b_t[:, pl.ds((r - 1) * LINE, LINE)] = values.astype(F32).T.astype(BF16)
    raw = lax.dot_general(
        w_dt[...], normed[...], (((1,), (1,)), ((), ())), preferred_element_type=F32
    ) + upright(dt_bias[...])
    steps = jnp.maximum(raw, 0.0) + jnp.log1p(jnp.exp(-jnp.abs(raw)))
    dt[...] = steps
    for m in range(4):
        for side in range(2):
            multiply_x(m, normed[pl.ds(m * 256, 256), :], lines_b, 1, side)
            inside(m, lines_a, 0, range(1 + 3 * side, 4 + 3 * side))

    w_in(2).wait()
    log_decay = -upright(rate[...]) * steps
    i = lax.broadcasted_iota(jnp.int32, (LINE, LINE), 0)
    j = lax.broadcasted_iota(jnp.int32, (LINE, LINE), 1)
    sums = jnp.dot(
        jnp.concatenate([log_decay[:, r * LINE : (r + 1) * LINE] for r in range(ROWS)], axis=0),
        jnp.where(i <= j, 1.0, 0.0).astype(F32),
        precision=lax.Precision.HIGHEST,
        preferred_element_type=F32,
    )
    lines = [sums[r * HEADS : (r + 1) * HEADS] for r in range(ROWS)]
    ends = [line[:, LINE - 1 :] for line in lines]
    before = [jnp.zeros_like(ends[0])]
    after = [jnp.zeros_like(ends[0])]
    for r in range(ROWS - 1):
        before.append(before[-1] + ends[r])
        after.append(after[-1] + ends[ROWS - 1 - r])
    for r in range(ROWS):
        part = slice(r * LINE, (r + 1) * LINE)
        cum[:, part] = lines[r]
        band_decay[:, part] = jnp.exp(lines[r] + before[r])
        tail = steps[:, part] * jnp.exp((ends[r] - lines[r]) + after[ROWS - 1 - r])
        band_tail[:, part] = tail
        if 0 < r < ROWS - 1:
            tails[pl.ds((r - 1) * LINE, LINE), :] = two_terms(tail)
    total[...] = jnp.broadcast_to(before[-1] + ends[-1], (HEADS, LINE)).T[:1]
    for m in range(4):
        for side in range(2):
            multiply_x(m, normed[pl.ds(m * 256, 256), :], lines_a, 2, side)
            inside(m, lines_b, 1, range(1 + 3 * side, 4 + 3 * side))

    gate_in(0).wait()
    for m in range(4):
        for side in range(2):
            multiply_gate(m, 0, side)
            inside(m, lines_a, 2, range(1 + 3 * side, 4 + 3 * side))
    for n in (1, 2):
        gate_in(n).wait()
        for m in range(4):
            for side in range(2):
                multiply_gate(m, n, side)
            if m < 3:
                add_state((n - 1) * 3 + m)


def project(tok, gain, w_xbc, w_gate, w_dt_t, dt_bias, rate, taps, conv_bias, skip, out_gain):
    per_head = pltpu.VMEM((HEADS, LENGTH), F32)
    return pl.pallas_call(
        project_kernel,
        in_specs=[
            far,
            small(1, D),
            far,
            far,
            small(HEADS, D),
            small(1, HEADS),
            small(1, HEADS),
            small(9, 1, INNER + 128),
            small(1, INNER + 128),
            small(1, HEADS),
            small(1, INNER),
        ],
        out_specs=[kept] * 18,
        out_shape=[
            pltpu.VMEM((LENGTH, INNER), BF16),
            pltpu.VMEM((LENGTH, INNER), BF16),
            pltpu.VMEM((4 * LINE, INNER), BF16),
            pltpu.VMEM((LENGTH, 128), BF16),
            pltpu.VMEM((4 * LINE, 128), BF16),
            per_head,
            per_head,
            per_head,
            per_head,
            pltpu.VMEM((1, HEADS), F32),
            pltpu.VMEM((STATE, INNER), F32),
            pltpu.VMEM((D, INNER + 128), BF16),
            pltpu.VMEM((LENGTH, D), BF16),
            pltpu.VMEM((1, D), F32),
            pltpu.VMEM((9, 1, INNER + 128), F32),
            pltpu.VMEM((1, INNER + 128), F32),
            pltpu.VMEM((1, HEADS), F32),
            pltpu.VMEM((1, INNER), F32),
        ],
        scratch_shapes=[
            pltpu.VMEM((LENGTH, D), BF16),
            pltpu.VMEM((4, ROWS, LINE + 16, 128), F32),
            pltpu.VMEM((4, ROWS, LINE + 16, 128), F32),
            pltpu.VMEM((1, ROWS, LINE + 16, 128), F32),
            pltpu.VMEM((128, (ROWS - 2) * LINE), BF16),
            pltpu.VMEM(((ROWS - 2) * LINE, 2 * HEADS), BF16),
            pltpu.VMEM((D, INNER), BF16),
            pltpu.SemaphoreType.DMA((4,)),
            pltpu.SemaphoreType.DMA((4,)),
            pltpu.SemaphoreType.DMA((3,)),
        ],
        compiler_params=params(),
        cost_estimate=pl.CostEstimate(
            flops=2 * LENGTH * D * 3224, bytes_accessed=20 << 20, transcendentals=LENGTH * INNER
        ),
        name="project",
    )(hbm(tok), hbm(gain), hbm(w_xbc), hbm(w_gate), *map(hbm, (w_dt_t, dt_bias, rate, taps, conv_bias, skip, out_gain)))


def edge_kernel(
    top,
    bottom,
    gain,
    w_near,
    rim,
    rim_bc,
    taps_ref,
    bias,
    band_tail,
    total,
    mid,
    x_in,
    bcs_in,
    x,
    bcs,
    pieces,
    edge,
    lines,
    b_t,
    tails,
):
    del x_in, bcs_in
    taps = [taps_ref[n] for n in range(9)]

    def both(side, own, own_start, start, out, out_start, tiles):
        for k in range(tiles):
            part = slice(k * 128, (k + 1) * 128)
            own_part = pl.ds(own_start + k * 128, 128)
            tile = start // 128 + k
            for slot, line in enumerate(
                [side[:LINE, part], own[pl.ds(0, LINE), own_part], own[pl.ds(LINE, LINE), own_part]]
                + [own[pl.ds(2 * LINE, LINE), own_part], own[pl.ds(3 * LINE, LINE), own_part]]
                + [side[LINE:, part]]
            ):
                fill(lines, tile % 4, slot, line)
            for slot, r in ((1, 0), (4, ROWS - 1)):
                out[pl.ds(place(r), LINE), pl.ds(out_start + k * 128, 128)] = convolved(
                    lines, tile % 4, slot, lanes(taps, tile * 128), bias[:, tile * 128 : tile * 128 + 128]
                )

    for slot in range(6):
        for k in range(4):
            lines[k, slot, pl.ds(0, 8), :] = jnp.zeros((8, 128), F32)
            lines[k, slot, pl.ds(LINE + 8, 8), :] = jnp.zeros((8, 128), F32)
    tails[pl.ds(place(0), LINE), :] = two_terms(band_tail[:, :LINE])
    tails[pl.ds(place(ROWS - 1), LINE), :] = two_terms(band_tail[:, LENGTH - LINE :])
    head = lax.broadcasted_iota(jnp.int32, (HEADS, 128), 0)
    lane = lax.broadcasted_iota(jnp.int32, (HEADS, 128), 1)
    first = total[...].astype(BF16)
    rest = total[...] - first.astype(F32)
    second = rest.astype(BF16)
    third = (rest - second.astype(F32)).astype(BF16)
    for g in range(4):
        pick = jnp.where(head == lane + g * GROUP_HEADS, 1.0, 0.0).astype(BF16)
        terms = jnp.concatenate(
            [dot(jnp.broadcast_to(t, (8, HEADS)), pick)[:1] for t in (first, second, third)]
            + [jnp.zeros((13, 128), F32)],
            axis=0,
        ).astype(BF16)
        for a in range(4):
            pieces[a, g, :, pl.ds(GROUP, 128)] = terms
    for n, side in enumerate((top, bottom)):
        edge[pl.ds(n * LINE, LINE), :] = rms(side[...].astype(F32), gain[...]).astype(BF16)
    both(dot(edge[...], w_near[:, pl.ds(INNER, 128)]).astype(BF16), rim_bc, 0, INNER, bcs, 0, 1)
    b_t[...] = bcs[pl.ds(0, 2 * LINE), :].astype(F32).T.astype(BF16)
    for n in range(3):
        start = n * 512
        part = pl.ds(start, 512)
        both(dot(edge[...], w_near[:, part]).astype(BF16), rim, start, start, x, start, 4)
        weighted = x[pl.ds(0, 2 * LINE), part].astype(F32) * dot(tails[...], head_spread(512, n * 8))
        state = mid[:, part] + dot(b_t[pl.ds(0, STATE), :], weighted.astype(BF16))
        for k in range(4):
            g, within = divmod(n * 4 + k, 3)
            for a in range(4):
                pieces[a, g, :, pl.ds(within * 128, 128)] = state[
                    16 * a : 16 * a + 16, k * 128 : (k + 1) * 128
                ].astype(BF16)


def edges(top, bottom, gain, w_near, rim, rim_bc, taps, conv_bias, band_tail, total, mid, x, bcs):
    return pl.pallas_call(
        edge_kernel,
        in_specs=[kept] * 13,
        out_specs=[kept, kept, pl.BlockSpec(memory_space=pltpu.VMEM)],
        out_shape=[
            pltpu.VMEM((LENGTH, INNER), BF16),
            pltpu.VMEM((LENGTH, 128), BF16),
            jax.ShapeDtypeStruct((4, 4, 16, GROUP + 128), BF16),
        ],
        input_output_aliases={11: 0, 12: 1},
        scratch_shapes=[
            pltpu.VMEM((2 * LINE, D), BF16),
            pltpu.VMEM((4, 6, LINE + 16, 128), F32),
            pltpu.VMEM((128, 2 * LINE), BF16),
            pltpu.VMEM((2 * LINE, 2 * HEADS), BF16),
        ],
        compiler_params=params(),
        cost_estimate=pl.CostEstimate(
            flops=2 * 256 * D * 1664 + 10 * LENGTH * 1664,
            bytes_accessed=10 << 20,
            transcendentals=256 * 1664,
        ),
        name="edges",
    )(
        near(top),
        near(bottom),
        near(gain),
        near(w_near),
        near(rim),
        near(rim_bc),
        near(taps),
        near(conv_bias),
        near(band_tail),
        near(total),
        near(mid),
        near(x),
        near(bcs),
    )


def scan_kernel(
    x, bcs, cum, dt, gate, skip, w_far, out, w_near, direct, state, sums, steps, weights, b_t, c, w_sem
):
    def rows_of(place):
        return pl.ds(pl.multiple_of(place * LINE, LINE), LINE)

    fetch = pltpu.make_async_copy(w_far, w_near, w_sem)
    fetch.start()
    lane = lax.broadcasted_iota(jnp.int32, (LINE, LINE), 1)
    row = lax.broadcasted_iota(jnp.int32, (LINE, LINE), 0)
    left = lane < WIDTH
    direct[...] = dot(
        two_terms(jnp.broadcast_to(upright(skip[...]), (HEADS, 8))),
        head_spread(INNER, 0),
    )
    state[...] = jnp.zeros_like(state)
    for r in range(ROWS):
        part = slice(r * LINE, (r + 1) * LINE)
        sums[r] = (cum[:, part] * LOG2E).T
        steps[r] = dt[:, part].T
        both = bcs[pl.ds(place(r), LINE), :].astype(F32)
        b_t[r] = both.T.astype(BF16)[:STATE]
        c[r] = pltpu.roll(both, STATE, 1).astype(BF16)[:, :STATE]
    for r in range(ROWS):
        weights[r] = jnp.where(row >= lane, dot(c[r], b_t[r]), 0.0)

    def line(r):
        rows, placed_rows = rows_of(r), rows_of(lax.rem(r + 1, ROWS))
        sums_here, steps_here, weights_here = sums[r], steps[r], weights[r]
        sums_t = cum[:, rows] * LOG2E
        steps_t = dt[:, rows]

        def mixing(h):
            along = jnp.broadcast_to(sums_here[:, h : h + 1], (LINE, LINE))
            decay = jnp.exp2(jnp.minimum(along - sums_t[h : h + 1], 0.0))
            return along, (decay * (weights_here * steps_t[h : h + 1])).astype(BF16)

        for q in range(HEADS // 4):
            quad = pl.ds(q * 256, 256)
            carried = dot(c[r], state[:, quad].astype(BF16))
            tails, decays = [], []
            for p in (2 * q, 2 * q + 1):
                part = pl.ds(p * 128, 128)
                h = 2 * p
                values = x[placed_rows, part].astype(F32)
                (along_a, mixing_a), (along_b, mixing_b) = mixing(h), mixing(h + 1)
                columns = jnp.concatenate(
                    [jnp.where(left, values, 0.0), jnp.where(left, 0.0, values)], axis=0
                ).astype(BF16)
                inner = dot(jnp.concatenate([mixing_a, mixing_b], axis=1), columns)
                here = jnp.where(left, along_a, along_b)
                carry = jnp.exp2(here)
                stepped = jnp.where(left, steps_here[:, h : h + 1], steps_here[:, h + 1 : h + 2])
                tails.append((values * stepped * jnp.exp2(here[LINE - 1 :] - here)).astype(BF16))
                decays.append(carry[LINE - 1 :])
                side = slice((p % 2) * 128, (p % 2) * 128 + 128)
                y = inner + carry * carried[:, side] + direct[0:1, part] * values
                out[rows, part] = (y * gate[rows, part].astype(F32)).astype(BF16)
            state[:, quad] = jnp.concatenate(decays, axis=1) * state[:, quad] + dot(
                b_t[r], jnp.concatenate(tails, axis=1)
            )

    @pl.loop(0, ROWS // 2)
    def _(pair):
        line(2 * pair)
        line(2 * pair + 1)

    fetch.wait()


def scan(x, bcs, cum, dt, gate, skip, w_out):
    return pl.pallas_call(
        scan_kernel,
        in_specs=[kept] * 6 + [far],
        out_specs=[kept] * 2,
        out_shape=[pltpu.VMEM((LENGTH, INNER), BF16), pltpu.VMEM((INNER, D), BF16)],
        scratch_shapes=[
            pltpu.VMEM((8, INNER), F32),
            pltpu.VMEM((STATE, INNER), F32),
            pltpu.VMEM((ROWS, LINE, HEADS), F32),
            pltpu.VMEM((ROWS, LINE, HEADS), F32),
            pltpu.VMEM((ROWS, LINE, LINE), F32),
            pltpu.VMEM((ROWS, STATE, LINE), BF16),
            pltpu.VMEM((ROWS, LINE, STATE), BF16),
            pltpu.SemaphoreType.DMA(()),
        ],
        compiler_params=params(),
        cost_estimate=pl.CostEstimate(
            flops=4 << 30, bytes_accessed=20 << 20, transcendentals=LENGTH * LINE * HEADS
        ),
        name="scan",
    )(*map(near, (x, bcs, cum, dt, gate, skip)), hbm(w_out))


def relay_kernel(arrived, out):
    logs = jnp.concatenate(
        [
            jnp.sum(arrived[j, :, pl.ds(GROUP, 128)].astype(F32), axis=0, keepdims=True)
            for j in range(BANDS)
        ],
        axis=0,
    )
    decay = jnp.exp(logs)
    high = decay.astype(BF16)
    low = (decay - high.astype(F32)).astype(BF16)
    lane = lax.broadcasted_iota(jnp.int32, (128, GROUP), 0)
    channel = lax.broadcasted_iota(jnp.int32, (128, GROUP), 1)
    spread = jnp.where(lane == channel // WIDTH, 1.0, 0.0).astype(BF16)
    wide = dot(high, spread) + dot(low, spread)
    state = jnp.zeros((16, GROUP), F32)
    for j in range(BANDS):
        out[j] = state.astype(BF16)
        state = wide[j : j + 1] * state + arrived[j, :, pl.ds(0, GROUP)].astype(F32)


def relay(arrived):
    return pl.pallas_call(
        relay_kernel,
        out_specs=kept,
        out_shape=pltpu.VMEM((BANDS, 16, GROUP), BF16),
        compiler_params=params(16),
        name="relay",
    )(arrived)


def columns_out(values, tokens, turned, out, rows=slice(None)):
    values = values + tokens.astype(F32)
    for k in range(values.shape[1] // 128):
        part = slice(k * 128, (k + 1) * 128)
        for r in range(ROWS):
            turned[k, pl.ds(r, 32, stride=ROWS), :] = values[r * 32 : (r + 1) * 32, part]
        out[rows, part] = turned[k].astype(BF16)


def finish_kernel(
    local, gate, bcs, band_decay, entering, gain, tok, w, out, hidden, spread, state, decays, turned
):
    step = pl.program_id(0)

    @pl.when(step == 0)
    def _():
        spread[...] = head_spread(INNER, 0)
        state[pl.ds(0, STATE), :] = jnp.zeros((STATE, INNER), BF16)
        for a in range(4):
            for g in range(4):
                state[pl.ds(STATE + 16 * a, 16), pl.ds(g * GROUP, GROUP)] = entering[4 * a + g]
        for r in range(ROWS):
            decays[r] = two_terms(band_decay[:, r * LINE : (r + 1) * LINE])

    here = pl.ds(pl.multiple_of(step * 32, 32), 32)
    cells = lambda ref: ref[:, here, :].reshape(256, ref.shape[2])
    both = jnp.concatenate([bcs[1:, here, :], bcs[:1, here, :]], axis=0).reshape(256, 128)
    decay = dot(cells(decays), spread[...])
    gated = cells(local).astype(F32) + dot(both, state[...]) * decay * cells(gate).astype(F32)
    normed = rms(gated, gain[...]).astype(BF16)
    hidden[...] = normed.reshape(ROWS, 32, INNER)
    columns_out(
        dot(normed, w[:, pl.ds(0, FIRST)]),
        tok[:, here, pl.ds(0, FIRST)].reshape(256, FIRST),
        turned,
        out,
    )


def finish(local, gate, bcs, band_decay, entering, gain, tok, w_out):
    return pl.pallas_call(
        finish_kernel,
        grid=(LINE // 32,),
        in_specs=[kept] * 8,
        out_specs=[
            pl.BlockSpec((256, FIRST), lambda i: (i, 0)),
            pl.BlockSpec((ROWS, 32, INNER), lambda i: (0, i, 0)),
        ],
        out_shape=[
            pltpu.HBM((LENGTH, FIRST), BF16),
            pltpu.HBM((ROWS, LINE, INNER), BF16),
        ],
        scratch_shapes=[
            pltpu.VMEM((2 * HEADS, INNER), BF16),
            pltpu.VMEM((2 * STATE, INNER), BF16),
            pltpu.VMEM((ROWS, LINE, 2 * HEADS), BF16),
            pltpu.VMEM((FIRST // 128, 256, 128), F32),
        ],
        compiler_params=params(),
        cost_estimate=pl.CostEstimate(
            flops=2 * LENGTH * D * FIRST, bytes_accessed=16 << 20, transcendentals=LENGTH
        ),
        name="finish",
    )(*map(near, (local, gate, bcs, band_decay, entering, gain, tok, w_out)))


def rest_kernel(hidden, w_far, tok_far, out, turned, w, tok_all, sem):
    step = pl.program_id(0)
    part = pl.ds(FIRST, D - FIRST)
    fetch = [
        pltpu.make_async_copy(w_far.at[:, part], w, sem.at[0]),
        pltpu.make_async_copy(tok_far.at[:, :, part], tok_all, sem.at[1]),
    ]

    @pl.when(step == 0)
    def _():
        for copy in fetch:
            copy.start()
        for copy in fetch:
            copy.wait()

    here = pl.ds(pl.multiple_of(step * 32, 32), 32)
    columns_out(
        dot(hidden[...].reshape(256, INNER), w[...]),
        tok_all[:, here, :].reshape(256, D - FIRST),
        turned,
        out,
    )


def rest(hidden, tok, w_out):
    return pl.pallas_call(
        rest_kernel,
        grid=(LINE // 32,),
        in_specs=[pl.BlockSpec((ROWS, 32, INNER), lambda i: (0, i, 0)), far, far],
        out_specs=pl.BlockSpec((256, D - FIRST), lambda i: (i, 0)),
        out_shape=pltpu.HBM((LENGTH, D - FIRST), BF16),
        scratch_shapes=[
            pltpu.VMEM(((D - FIRST) // 128, 256, 128), F32),
            pltpu.VMEM((INNER, D - FIRST), BF16),
            pltpu.VMEM((ROWS, LINE, D - FIRST), BF16),
            pltpu.SemaphoreType.DMA((2,)),
        ],
        compiler_params=params(60),
        cost_estimate=pl.CostEstimate(
            flops=2 * LENGTH * D * (D - FIRST), bytes_accessed=8 << 20, transcendentals=0
        ),
        name="rest",
    )(hidden, hbm(w_out), hbm(tok))


def shards(
    tokens,
    in_gain,
    w_xbc,
    w_gate,
    w_dt,
    dt_bias,
    decay_rate,
    conv_w,
    conv_bias,
    skip,
    out_gain,
    w_out,
):
    bands = lax.axis_size("band")
    segments = lax.axis_size("segment")
    cells = tokens[0]
    tok = cells.reshape(LENGTH, D)
    top = lax.ppermute(cells[ROWS - 1], "band", [(i, i + 1) for i in range(bands - 1)])
    bottom = lax.ppermute(cells[0], "band", [(i + 1, i) for i in range(bands - 1)])

    (
        x,
        gate,
        rim,
        bcs,
        rim_bc,
        cum,
        dt,
        band_tail,
        band_decay,
        total,
        mid,
        w_xbc_near,
        tok_near,
        in_gain_near,
        taps_near,
        bias_near,
        skip_near,
        out_gain_near,
    ) = project(
        tok,
        in_gain,
        w_xbc[0],
        w_gate[0],
        w_dt[0].T,
        dt_bias,
        decay_rate,
        conv_w.swapaxes(0, 1),
        conv_bias,
        skip,
        out_gain,
    )
    x, bcs, pieces = edges(
        top,
        bottom,
        in_gain_near,
        w_xbc_near,
        rim,
        rim_bc,
        taps_near,
        bias_near,
        band_tail,
        total,
        mid,
        x,
        bcs,
    )
    swap = functools.partial(
        lax.all_to_all, axis_name="band", split_axis=0, concat_axis=0, tiled=True
    )
    onward = functools.partial(
        lax.ppermute, axis_name="segment", perm=[(i, (i + 1) % segments) for i in range(segments)]
    )
    local, w_out_near = scan(x, bcs, cum, dt, gate, skip_near, w_out[0])
    pieces, local = lax.optimization_barrier((pieces, local))
    arrived = swap(pieces.reshape(BANDS, 16, GROUP + 128))
    entering = swap(relay(arrived))

    grid = lambda a: a.reshape(ROWS, LINE, a.shape[-1])
    parted = lambda a: a.reshape(BANDS, LENGTH // BANDS, a.shape[-1])
    first, hidden = finish(
        grid(local),
        grid(gate),
        grid(bcs),
        band_decay,
        entering,
        out_gain_near,
        grid(tok_near),
        w_out_near,
    )
    first = swap(parted(first))
    second = onward(parted(rest(hidden, cells, w_out[0])))
    second = swap(second)
    first = onward(first)
    both = jnp.concatenate([first, second], axis=-1)
    handed = both.reshape(BANDS, LINE // BANDS, ROWS, D).swapaxes(0, 1)
    return handed.reshape(1, LINE // BANDS, BANDS * ROWS, D)


def solution(mesh):
    in_specs = (
        P("segment", "band", None, None),
        P("segment", None),
        P("segment", None, None),
        P("segment", None, None),
        P("segment", None, None),
        P("segment", None),
        P("segment", None),
        P("segment", None, None),
        P("segment", None),
        P("segment", None),
        P("segment", None),
        P("segment", None, None),
    )
    out_specs = P("segment", "band", None, None)
    return jax.shard_map(shards, mesh=mesh, in_specs=in_specs, out_specs=out_specs, check_vma=False)
```

```python
import functools

import jax
import jax.numpy as jnp
from jax import lax
from jax.experimental import pallas as pl
from jax.experimental.pallas import tpu as pltpu
from jax.sharding import PartitionSpec as P

EPSILON = 1e-05
ROWS = 8
LINE = 128
LENGTH = ROWS * LINE
HEADS = 24
WIDTH = 64
STATE = 64
INNER = HEADS * WIDTH
D = 1536
HALF = INNER // 2
FIRST = 1024
GROUP = 384
GROUP_HEADS = GROUP // WIDTH
BANDS = 16
F32 = jnp.float32
BF16 = jnp.bfloat16
MIB = 1 << 20
LOG2E = 1.4426950408889634


def params(mib=24):
    return pltpu.CompilerParams(vmem_limit_bytes=mib * MIB)


kept = pl.BlockSpec(memory_space=pltpu.VMEM)
far = pl.BlockSpec(memory_space=pl.ANY)


def small(*shape):
    return pl.BlockSpec(shape, lambda *i: (0,) * len(shape))


def near(a):
    return pltpu.with_memory_space_constraint(a, pltpu.VMEM)


def hbm(a):
    return pltpu.with_memory_space_constraint(a, pltpu.HBM)


def upright(row):
    return jnp.broadcast_to(row, (LINE, HEADS)).T[:, :1]


def whole(*shape):
    return pl.BlockSpec(shape, lambda i: (0,) * len(shape), pipeline_mode=pl.Buffered(1))


def dot(a, b):
    return jnp.dot(a, b, preferred_element_type=F32)


def rms(values, gain):
    return values * lax.rsqrt(jnp.mean(values * values, -1, keepdims=True) + EPSILON) * gain


def silu(v):
    half = 0.5 * v
    return half + half * jnp.tanh(half)


def head_spread(channels, first):
    head = lax.broadcasted_iota(jnp.int32, (2 * HEADS, channels), 0)
    head = jnp.where(head < HEADS, head, head - HEADS)
    channel = lax.broadcasted_iota(jnp.int32, (2 * HEADS, channels), 1)
    return jnp.where(head - first == channel // WIDTH, 1.0, 0.0).astype(BF16)


def two_terms(values_t):
    high = values_t.astype(BF16).astype(F32)
    return jnp.concatenate([high, values_t - high], axis=0).T.astype(BF16)


def place(r):
    return (r + 1) % ROWS * LINE


def fill(padded, tile, slot, line):
    padded[tile, slot, pl.ds(8, LINE), :] = line.astype(F32)


def convolved(padded, tile, slot, taps, bias):
    total = bias
    for i in range(3):
        for j in range(3):
            total = total + padded[tile, slot - 1 + i, pl.ds(7 + j, LINE), :] * taps[3 * i + j]
    return silu(total).astype(BF16)


def lanes(refs, start):
    return [ref[:, start : start + 128] for ref in refs]


def project_kernel(
    tok,
    gain,
    w_xbc,
    w_g,
    w_dt,
    dt_bias,
    rate,
    taps_ref,
    bias,
    skip,
    out_gain,
    x,
    gate,
    rim,
    bcs,
    rim_bc,
    cum,
    dt,
    band_tail,
    band_decay,
    total,
    mid,
    w_near,
    tok_near,
    gain_near,
    taps_near,
    bias_near,
    skip_near,
    out_gain_near,
    normed,
    lines_a,
    lines_b,
    lines_bc,
    b_t,
    tails,
    w_g_near,
    tok_sem,
    w_sem,
    w_g_sem,
):
    def tokens_in(m):
        part = pl.ds(m * 256, 256)
        return pltpu.make_async_copy(tok.at[part, :], tok_near.at[part, :], tok_sem.at[m])

    def w_in(n):
        part = pl.ds(n * 512, 512 if n < 3 else 128)
        return pltpu.make_async_copy(w_xbc.at[:, part], w_near.at[:, part], w_sem.at[n])

    def gate_in(n):
        part = pl.ds(n * 512, 512)
        return pltpu.make_async_copy(w_g.at[:, part], w_g_near.at[:, part], w_g_sem.at[n])

    taps = [taps_ref[n] for n in range(9)]

    def store(m, values, padded, out, start, tiles, tile=0):
        for n in range(m * 2, m * 2 + 2):
            line = values[(n - m * 2) * LINE : (n - m * 2 + 1) * LINE]
            for k in range(tiles):
                fill(padded, tile + k, n, line[:, k * 128 : (k + 1) * 128])
            if n in (0, 1, 6, 7):
                place_n = (n if n < 2 else n - 4) * LINE
                out[pl.ds(place_n, LINE), pl.ds(start, tiles * 128)] = line

    def multiply_x(m, here, padded, chunk, side):
        start = chunk * 512 + side * 256
        values = dot(here, w_near[:, pl.ds(start, 256)]).astype(BF16)
        store(m, values, padded, rim, start, 2, side * 2)

    def multiply_gate(m, n, side):
        rows, part = pl.ds(m * 256, 256), pl.ds(n * 512 + side * 256, 256)
        gate[rows, part] = silu(dot(normed[rows, :], w_g_near[:, part])).astype(BF16)

    def inside(k, padded, chunk, rows):
        start = chunk * 512 + k * 128
        for r in rows:
            x[pl.ds(place(r), LINE), pl.ds(start, 128)] = convolved(
                padded, k, r, lanes(taps, start), bias[:, start : start + 128]
            )

    def add_state(piece):
        part = pl.ds(piece * 256, 256)
        spread = head_spread(256, piece * 4)
        own = x[pl.ds(2 * LINE, (ROWS - 2) * LINE), part].astype(F32)
        mid[:, part] = dot(b_t[pl.ds(0, STATE), :], (own * dot(tails[...], spread)).astype(BF16))

    tokens_in(0).start()
    w_in(3).start()
    w_in(0).start()
    for m in range(1, 4):
        tokens_in(m).start()
    w_in(1).start()
    w_in(2).start()
    for n in range(3):
        gate_in(n).start()
    gain_near[...] = gain[...]
    taps_near[...] = taps_ref[...]
    bias_near[...] = bias[...]
    skip_near[...] = skip[...]
    out_gain_near[...] = out_gain[...]
    for padded in (lines_a, lines_b, lines_bc):
        for n in range(ROWS):
            for k in range(padded.shape[0]):
                padded[k, n, pl.ds(0, 8), :] = jnp.zeros((8, 128), F32)
                padded[k, n, pl.ds(LINE + 8, 8), :] = jnp.zeros((8, 128), F32)
    for m in range(4):
        tokens_in(m).wait()
        if m == 0:
            w_in(3).wait()
            w_in(0).wait()
        part = pl.ds(m * 256, 256)
        here = rms(tok_near[part, :].astype(F32), gain[...]).astype(BF16)
        normed[part, :] = here
        store(m, dot(here, w_near[:, pl.ds(INNER, 128)]).astype(BF16), lines_bc, rim_bc, 0, 1)
        for side in range(2):
            multiply_x(m, here, lines_a, 0, side)

    w_in(1).wait()
    for r in range(1, ROWS - 1):
        values = convolved(
            lines_bc, 0, r, lanes(taps, INNER), bias[:, INNER : INNER + 128]
        )
        bcs[pl.ds(place(r), LINE), :] = values
        b_t[:, pl.ds((r - 1) * LINE, LINE)] = values.astype(F32).T.astype(BF16)
    raw = lax.dot_general(
        w_dt[...], normed[...], (((1,), (1,)), ((), ())), preferred_element_type=F32
    ) + upright(dt_bias[...])
    steps = jnp.maximum(raw, 0.0) + jnp.log1p(jnp.exp(-jnp.abs(raw)))
    dt[...] = steps
    for m in range(4):
        for side in range(2):
            multiply_x(m, normed[pl.ds(m * 256, 256), :], lines_b, 1, side)
            inside(m, lines_a, 0, range(1 + 3 * side, 4 + 3 * side))

    w_in(2).wait()
    log_decay = -upright(rate[...]) * steps
    i = lax.broadcasted_iota(jnp.int32, (LINE, LINE), 0)
    j = lax.broadcasted_iota(jnp.int32, (LINE, LINE), 1)
    sums = jnp.dot(
        jnp.concatenate([log_decay[:, r * LINE : (r + 1) * LINE] for r in range(ROWS)], axis=0),
        jnp.where(i <= j, 1.0, 0.0).astype(F32),
        precision=lax.Precision.HIGHEST,
        preferred_element_type=F32,
    )
    lines = [sums[r * HEADS : (r + 1) * HEADS] for r in range(ROWS)]
    ends = [line[:, LINE - 1 :] for line in lines]
    before = [jnp.zeros_like(ends[0])]
    after = [jnp.zeros_like(ends[0])]
    for r in range(ROWS - 1):
        before.append(before[-1] + ends[r])
        after.append(after[-1] + ends[ROWS - 1 - r])
    for r in range(ROWS):
        part = slice(r * LINE, (r + 1) * LINE)
        cum[:, part] = lines[r]
        band_decay[:, part] = jnp.exp(lines[r] + before[r])
        tail = steps[:, part] * jnp.exp((ends[r] - lines[r]) + after[ROWS - 1 - r])
        band_tail[:, part] = tail
        if 0 < r < ROWS - 1:
            tails[pl.ds((r - 1) * LINE, LINE), :] = two_terms(tail)
    total[...] = jnp.broadcast_to(before[-1] + ends[-1], (HEADS, LINE)).T[:1]
    for m in range(4):
        for side in range(2):
            multiply_x(m, normed[pl.ds(m * 256, 256), :], lines_a, 2, side)
            inside(m, lines_b, 1, range(1 + 3 * side, 4 + 3 * side))

    gate_in(0).wait()
    for m in range(4):
        for side in range(2):
            multiply_gate(m, 0, side)
            inside(m, lines_a, 2, range(1 + 3 * side, 4 + 3 * side))
    for n in (1, 2):
        gate_in(n).wait()
        for m in range(4):
            for side in range(2):
                multiply_gate(m, n, side)
            if m < 3:
                add_state((n - 1) * 3 + m)


def project(tok, gain, w_xbc, w_gate, w_dt_t, dt_bias, rate, taps, conv_bias, skip, out_gain):
    per_head = pltpu.VMEM((HEADS, LENGTH), F32)
    return pl.pallas_call(
        project_kernel,
        in_specs=[
            far,
            small(1, D),
            far,
            far,
            small(HEADS, D),
            small(1, HEADS),
            small(1, HEADS),
            small(9, 1, INNER + 128),
            small(1, INNER + 128),
            small(1, HEADS),
            small(1, INNER),
        ],
        out_specs=[kept] * 18,
        out_shape=[
            pltpu.VMEM((LENGTH, INNER), BF16),
            pltpu.VMEM((LENGTH, INNER), BF16),
            pltpu.VMEM((4 * LINE, INNER), BF16),
            pltpu.VMEM((LENGTH, 128), BF16),
            pltpu.VMEM((4 * LINE, 128), BF16),
            per_head,
            per_head,
            per_head,
            per_head,
            pltpu.VMEM((1, HEADS), F32),
            pltpu.VMEM((STATE, INNER), F32),
            pltpu.VMEM((D, INNER + 128), BF16),
            pltpu.VMEM((LENGTH, D), BF16),
            pltpu.VMEM((1, D), F32),
            pltpu.VMEM((9, 1, INNER + 128), F32),
            pltpu.VMEM((1, INNER + 128), F32),
            pltpu.VMEM((1, HEADS), F32),
            pltpu.VMEM((1, INNER), F32),
        ],
        scratch_shapes=[
            pltpu.VMEM((LENGTH, D), BF16),
            pltpu.VMEM((4, ROWS, LINE + 16, 128), F32),
            pltpu.VMEM((4, ROWS, LINE + 16, 128), F32),
            pltpu.VMEM((1, ROWS, LINE + 16, 128), F32),
            pltpu.VMEM((128, (ROWS - 2) * LINE), BF16),
            pltpu.VMEM(((ROWS - 2) * LINE, 2 * HEADS), BF16),
            pltpu.VMEM((D, INNER), BF16),
            pltpu.SemaphoreType.DMA((4,)),
            pltpu.SemaphoreType.DMA((4,)),
            pltpu.SemaphoreType.DMA((3,)),
        ],
        compiler_params=params(),
        cost_estimate=pl.CostEstimate(
            flops=2 * LENGTH * D * 3224, bytes_accessed=20 << 20, transcendentals=LENGTH * INNER
        ),
        name="project",
    )(hbm(tok), hbm(gain), hbm(w_xbc), hbm(w_gate), *map(hbm, (w_dt_t, dt_bias, rate, taps, conv_bias, skip, out_gain)))


def edge_kernel(
    top,
    bottom,
    gain,
    w_near,
    rim,
    rim_bc,
    taps_ref,
    bias,
    band_tail,
    total,
    mid,
    x_in,
    bcs_in,
    x,
    bcs,
    pieces,
    edge,
    lines,
    b_t,
    tails,
):
    del x_in, bcs_in
    taps = [taps_ref[n] for n in range(9)]

    def both(side, own, own_start, start, out, out_start, tiles):
        for k in range(tiles):
            part = slice(k * 128, (k + 1) * 128)
            own_part = pl.ds(own_start + k * 128, 128)
            tile = start // 128 + k
            for slot, line in enumerate(
                [side[:LINE, part], own[pl.ds(0, LINE), own_part], own[pl.ds(LINE, LINE), own_part]]
                + [own[pl.ds(2 * LINE, LINE), own_part], own[pl.ds(3 * LINE, LINE), own_part]]
                + [side[LINE:, part]]
            ):
                fill(lines, tile % 4, slot, line)
            for slot, r in ((1, 0), (4, ROWS - 1)):
                out[pl.ds(place(r), LINE), pl.ds(out_start + k * 128, 128)] = convolved(
                    lines, tile % 4, slot, lanes(taps, tile * 128), bias[:, tile * 128 : tile * 128 + 128]
                )

    for slot in range(6):
        for k in range(4):
            lines[k, slot, pl.ds(0, 8), :] = jnp.zeros((8, 128), F32)
            lines[k, slot, pl.ds(LINE + 8, 8), :] = jnp.zeros((8, 128), F32)
    tails[pl.ds(place(0), LINE), :] = two_terms(band_tail[:, :LINE])
    tails[pl.ds(place(ROWS - 1), LINE), :] = two_terms(band_tail[:, LENGTH - LINE :])
    head = lax.broadcasted_iota(jnp.int32, (HEADS, 128), 0)
    lane = lax.broadcasted_iota(jnp.int32, (HEADS, 128), 1)
    first = total[...].astype(BF16)
    rest = total[...] - first.astype(F32)
    second = rest.astype(BF16)
    third = (rest - second.astype(F32)).astype(BF16)
    for g in range(4):
        pick = jnp.where(head == lane + g * GROUP_HEADS, 1.0, 0.0).astype(BF16)
        terms = jnp.concatenate(
            [dot(jnp.broadcast_to(t, (8, HEADS)), pick)[:1] for t in (first, second, third)]
            + [jnp.zeros((13, 128), F32)],
            axis=0,
        ).astype(BF16)
        for a in range(4):
            pieces[a, g, :, pl.ds(GROUP, 128)] = terms
    for n, side in enumerate((top, bottom)):
        edge[pl.ds(n * LINE, LINE), :] = rms(side[...].astype(F32), gain[...]).astype(BF16)
    both(dot(edge[...], w_near[:, pl.ds(INNER, 128)]).astype(BF16), rim_bc, 0, INNER, bcs, 0, 1)
    b_t[...] = bcs[pl.ds(0, 2 * LINE), :].astype(F32).T.astype(BF16)
    for n in range(3):
        start = n * 512
        part = pl.ds(start, 512)
        both(dot(edge[...], w_near[:, part]).astype(BF16), rim, start, start, x, start, 4)
        weighted = x[pl.ds(0, 2 * LINE), part].astype(F32) * dot(tails[...], head_spread(512, n * 8))
        state = mid[:, part] + dot(b_t[pl.ds(0, STATE), :], weighted.astype(BF16))
        for k in range(4):
            g, within = divmod(n * 4 + k, 3)
            for a in range(4):
                pieces[a, g, :, pl.ds(within * 128, 128)] = state[
                    16 * a : 16 * a + 16, k * 128 : (k + 1) * 128
                ].astype(BF16)


def edges(top, bottom, gain, w_near, rim, rim_bc, taps, conv_bias, band_tail, total, mid, x, bcs):
    return pl.pallas_call(
        edge_kernel,
        in_specs=[kept] * 13,
        out_specs=[kept, kept, pl.BlockSpec(memory_space=pltpu.VMEM)],
        out_shape=[
            pltpu.VMEM((LENGTH, INNER), BF16),
            pltpu.VMEM((LENGTH, 128), BF16),
            jax.ShapeDtypeStruct((4, 4, 16, GROUP + 128), BF16),
        ],
        input_output_aliases={11: 0, 12: 1},
        scratch_shapes=[
            pltpu.VMEM((2 * LINE, D), BF16),
            pltpu.VMEM((4, 6, LINE + 16, 128), F32),
            pltpu.VMEM((128, 2 * LINE), BF16),
            pltpu.VMEM((2 * LINE, 2 * HEADS), BF16),
        ],
        compiler_params=params(),
        cost_estimate=pl.CostEstimate(
            flops=2 * 256 * D * 1664 + 10 * LENGTH * 1664,
            bytes_accessed=10 << 20,
            transcendentals=256 * 1664,
        ),
        name="edges",
    )(
        near(top),
        near(bottom),
        near(gain),
        near(w_near),
        near(rim),
        near(rim_bc),
        near(taps),
        near(conv_bias),
        near(band_tail),
        near(total),
        near(mid),
        near(x),
        near(bcs),
    )


def scan_kernel(
    x, bcs, cum, dt, gate, skip, w_far, out, w_near, direct, state, sums, steps, weights, b_t, c, w_sem
):
    def rows_of(place):
        return pl.ds(pl.multiple_of(place * LINE, LINE), LINE)

    fetch = pltpu.make_async_copy(w_far, w_near, w_sem)
    fetch.start()
    lane = lax.broadcasted_iota(jnp.int32, (LINE, LINE), 1)
    row = lax.broadcasted_iota(jnp.int32, (LINE, LINE), 0)
    left = lane < WIDTH
    direct[...] = dot(
        two_terms(jnp.broadcast_to(upright(skip[...]), (HEADS, 8))),
        head_spread(INNER, 0),
    )
    state[...] = jnp.zeros_like(state)
    for r in range(ROWS):
        part = slice(r * LINE, (r + 1) * LINE)
        sums[r] = (cum[:, part] * LOG2E).T
        steps[r] = dt[:, part].T
        both = bcs[pl.ds(place(r), LINE), :].astype(F32)
        b_t[r] = both.T.astype(BF16)[:STATE]
        c[r] = pltpu.roll(both, STATE, 1).astype(BF16)[:, :STATE]
    for r in range(ROWS):
        weights[r] = jnp.where(row >= lane, dot(c[r], b_t[r]), 0.0)

    def line(r):
        rows, placed_rows = rows_of(r), rows_of(lax.rem(r + 1, ROWS))
        sums_here, steps_here, weights_here = sums[r], steps[r], weights[r]
        sums_t = cum[:, rows] * LOG2E
        steps_t = dt[:, rows]

        def mixing(h):
            along = jnp.broadcast_to(sums_here[:, h : h + 1], (LINE, LINE))
            decay = jnp.exp2(jnp.minimum(along - sums_t[h : h + 1], 0.0))
            return along, (decay * (weights_here * steps_t[h : h + 1])).astype(BF16)

        for q in range(HEADS // 4):
            quad = pl.ds(q * 256, 256)
            carried = dot(c[r], state[:, quad].astype(BF16))
            tails, decays = [], []
            for p in (2 * q, 2 * q + 1):
                part = pl.ds(p * 128, 128)
                h = 2 * p
                values = x[placed_rows, part].astype(F32)
                (along_a, mixing_a), (along_b, mixing_b) = mixing(h), mixing(h + 1)
                columns = jnp.concatenate(
                    [jnp.where(left, values, 0.0), jnp.where(left, 0.0, values)], axis=0
                ).astype(BF16)
                inner = dot(jnp.concatenate([mixing_a, mixing_b], axis=1), columns)
                here = jnp.where(left, along_a, along_b)
                carry = jnp.exp2(here)
                stepped = jnp.where(left, steps_here[:, h : h + 1], steps_here[:, h + 1 : h + 2])
                tails.append((values * stepped * jnp.exp2(here[LINE - 1 :] - here)).astype(BF16))
                decays.append(carry[LINE - 1 :])
                side = slice((p % 2) * 128, (p % 2) * 128 + 128)
                y = inner + carry * carried[:, side] + direct[0:1, part] * values
                out[rows, part] = (y * gate[rows, part].astype(F32)).astype(BF16)
            state[:, quad] = jnp.concatenate(decays, axis=1) * state[:, quad] + dot(
                b_t[r], jnp.concatenate(tails, axis=1)
            )

    @pl.loop(0, ROWS)
    def _(r):
        line(r)

    fetch.wait()


def scan(x, bcs, cum, dt, gate, skip, w_out):
    return pl.pallas_call(
        scan_kernel,
        in_specs=[kept] * 6 + [far],
        out_specs=[kept] * 2,
        out_shape=[pltpu.VMEM((LENGTH, INNER), BF16), pltpu.VMEM((INNER, D), BF16)],
        scratch_shapes=[
            pltpu.VMEM((8, INNER), F32),
            pltpu.VMEM((STATE, INNER), F32),
            pltpu.VMEM((ROWS, LINE, HEADS), F32),
            pltpu.VMEM((ROWS, LINE, HEADS), F32),
            pltpu.VMEM((ROWS, LINE, LINE), F32),
            pltpu.VMEM((ROWS, STATE, LINE), BF16),
            pltpu.VMEM((ROWS, LINE, STATE), BF16),
            pltpu.SemaphoreType.DMA(()),
        ],
        compiler_params=params(),
        cost_estimate=pl.CostEstimate(
            flops=4 << 30, bytes_accessed=20 << 20, transcendentals=LENGTH * LINE * HEADS
        ),
        name="scan",
    )(*map(near, (x, bcs, cum, dt, gate, skip)), hbm(w_out))


def relay_kernel(arrived, out):
    logs = jnp.concatenate(
        [
            jnp.sum(arrived[j, :, pl.ds(GROUP, 128)].astype(F32), axis=0, keepdims=True)
            for j in range(BANDS)
        ],
        axis=0,
    )
    decay = jnp.exp(logs)
    high = decay.astype(BF16)
    low = (decay - high.astype(F32)).astype(BF16)
    lane = lax.broadcasted_iota(jnp.int32, (128, GROUP), 0)
    channel = lax.broadcasted_iota(jnp.int32, (128, GROUP), 1)
    spread = jnp.where(lane == channel // WIDTH, 1.0, 0.0).astype(BF16)
    wide = dot(high, spread) + dot(low, spread)
    state = jnp.zeros((16, GROUP), F32)
    for j in range(BANDS):
        out[j] = state.astype(BF16)
        state = wide[j : j + 1] * state + arrived[j, :, pl.ds(0, GROUP)].astype(F32)


def relay(arrived):
    return pl.pallas_call(
        relay_kernel,
        out_specs=kept,
        out_shape=pltpu.VMEM((BANDS, 16, GROUP), BF16),
        compiler_params=params(16),
        name="relay",
    )(arrived)


def columns_out(values, tokens, turned, out, rows=slice(None)):
    values = values + tokens.astype(F32)
    for k in range(values.shape[1] // 128):
        part = slice(k * 128, (k + 1) * 128)
        for r in range(ROWS):
            turned[k, pl.ds(r, 32, stride=ROWS), :] = values[r * 32 : (r + 1) * 32, part]
        out[rows, part] = turned[k].astype(BF16)


def finish_kernel(
    local, gate, bcs, band_decay, entering, gain, tok, w, out, hidden, spread, state, decays, turned
):
    step = pl.program_id(0)

    @pl.when(step == 0)
    def _():
        spread[...] = head_spread(INNER, 0)
        state[pl.ds(0, STATE), :] = jnp.zeros((STATE, INNER), BF16)
        for a in range(4):
            for g in range(4):
                state[pl.ds(STATE + 16 * a, 16), pl.ds(g * GROUP, GROUP)] = entering[4 * a + g]
        for r in range(ROWS):
            decays[r] = two_terms(band_decay[:, r * LINE : (r + 1) * LINE])

    here = pl.ds(pl.multiple_of(step * 32, 32), 32)
    cells = lambda ref: ref[:, here, :].reshape(256, ref.shape[2])
    both = jnp.concatenate([bcs[1:, here, :], bcs[:1, here, :]], axis=0).reshape(256, 128)
    decay = dot(cells(decays), spread[...])
    gated = cells(local).astype(F32) + dot(both, state[...]) * decay * cells(gate).astype(F32)
    normed = rms(gated, gain[...]).astype(BF16)
    hidden[...] = normed.reshape(ROWS, 32, INNER)
    columns_out(
        dot(normed, w[:, pl.ds(0, FIRST)]),
        tok[:, here, pl.ds(0, FIRST)].reshape(256, FIRST),
        turned,
        out,
    )


def finish(local, gate, bcs, band_decay, entering, gain, tok, w_out):
    return pl.pallas_call(
        finish_kernel,
        grid=(LINE // 32,),
        in_specs=[kept] * 8,
        out_specs=[
            pl.BlockSpec((256, FIRST), lambda i: (i, 0)),
            pl.BlockSpec((ROWS, 32, INNER), lambda i: (0, i, 0)),
        ],
        out_shape=[
            pltpu.HBM((LENGTH, FIRST), BF16),
            pltpu.HBM((ROWS, LINE, INNER), BF16),
        ],
        scratch_shapes=[
            pltpu.VMEM((2 * HEADS, INNER), BF16),
            pltpu.VMEM((2 * STATE, INNER), BF16),
            pltpu.VMEM((ROWS, LINE, 2 * HEADS), BF16),
            pltpu.VMEM((FIRST // 128, 256, 128), F32),
        ],
        compiler_params=params(),
        cost_estimate=pl.CostEstimate(
            flops=2 * LENGTH * D * FIRST, bytes_accessed=16 << 20, transcendentals=LENGTH
        ),
        name="finish",
    )(*map(near, (local, gate, bcs, band_decay, entering, gain, tok, w_out)))


def rest_kernel(hidden, w_far, tok_far, out, turned, w, tok_all, sem):
    step = pl.program_id(0)
    part = pl.ds(FIRST, D - FIRST)
    fetch = [
        pltpu.make_async_copy(w_far.at[:, part], w, sem.at[0]),
        pltpu.make_async_copy(tok_far.at[:, :, part], tok_all, sem.at[1]),
    ]

    @pl.when(step == 0)
    def _():
        for copy in fetch:
            copy.start()
        for copy in fetch:
            copy.wait()

    here = pl.ds(pl.multiple_of(step * 32, 32), 32)
    columns_out(
        dot(hidden[...].reshape(256, INNER), w[...]),
        tok_all[:, here, :].reshape(256, D - FIRST),
        turned,
        out,
    )


def rest(hidden, tok, w_out):
    return pl.pallas_call(
        rest_kernel,
        grid=(LINE // 32,),
        in_specs=[pl.BlockSpec((ROWS, 32, INNER), lambda i: (0, i, 0)), far, far],
        out_specs=pl.BlockSpec((256, D - FIRST), lambda i: (i, 0)),
        out_shape=pltpu.HBM((LENGTH, D - FIRST), BF16),
        scratch_shapes=[
            pltpu.VMEM(((D - FIRST) // 128, 256, 128), F32),
            pltpu.VMEM((INNER, D - FIRST), BF16),
            pltpu.VMEM((ROWS, LINE, D - FIRST), BF16),
            pltpu.SemaphoreType.DMA((2,)),
        ],
        compiler_params=params(60),
        cost_estimate=pl.CostEstimate(
            flops=2 * LENGTH * D * (D - FIRST), bytes_accessed=8 << 20, transcendentals=0
        ),
        name="rest",
    )(hidden, hbm(w_out), hbm(tok))


def shards(
    tokens,
    in_gain,
    w_xbc,
    w_gate,
    w_dt,
    dt_bias,
    decay_rate,
    conv_w,
    conv_bias,
    skip,
    out_gain,
    w_out,
):
    bands = lax.axis_size("band")
    segments = lax.axis_size("segment")
    cells = tokens[0]
    tok = cells.reshape(LENGTH, D)
    top = lax.ppermute(cells[ROWS - 1], "band", [(i, i + 1) for i in range(bands - 1)])
    bottom = lax.ppermute(cells[0], "band", [(i + 1, i) for i in range(bands - 1)])

    (
        x,
        gate,
        rim,
        bcs,
        rim_bc,
        cum,
        dt,
        band_tail,
        band_decay,
        total,
        mid,
        w_xbc_near,
        tok_near,
        in_gain_near,
        taps_near,
        bias_near,
        skip_near,
        out_gain_near,
    ) = project(
        tok,
        in_gain,
        w_xbc[0],
        w_gate[0],
        w_dt[0].T,
        dt_bias,
        decay_rate,
        conv_w.swapaxes(0, 1),
        conv_bias,
        skip,
        out_gain,
    )
    x, bcs, pieces = edges(
        top,
        bottom,
        in_gain_near,
        w_xbc_near,
        rim,
        rim_bc,
        taps_near,
        bias_near,
        band_tail,
        total,
        mid,
        x,
        bcs,
    )
    swap = functools.partial(
        lax.all_to_all, axis_name="band", split_axis=0, concat_axis=0, tiled=True
    )
    onward = functools.partial(
        lax.ppermute, axis_name="segment", perm=[(i, (i + 1) % segments) for i in range(segments)]
    )
    local, w_out_near = scan(x, bcs, cum, dt, gate, skip_near, w_out[0])
    pieces, local = lax.optimization_barrier((pieces, local))
    arrived = swap(pieces.reshape(BANDS, 16, GROUP + 128))
    entering = swap(relay(arrived))

    grid = lambda a: a.reshape(ROWS, LINE, a.shape[-1])
    parted = lambda a: a.reshape(BANDS, LENGTH // BANDS, a.shape[-1])
    first, hidden = finish(
        grid(local),
        grid(gate),
        grid(bcs),
        band_decay,
        entering,
        out_gain_near,
        grid(tok_near),
        w_out_near,
    )
    first = swap(parted(first))
    second = onward(parted(rest(hidden, cells, w_out[0])))
    second = swap(second)
    first = onward(first)
    both = jnp.concatenate([first, second], axis=-1)
    handed = both.reshape(BANDS, LINE // BANDS, ROWS, D).swapaxes(0, 1)
    return handed.reshape(1, LINE // BANDS, BANDS * ROWS, D)


def solution(mesh):
    in_specs = (
        P("segment", "band", None, None),
        P("segment", None),
        P("segment", None, None),
        P("segment", None, None),
        P("segment", None, None),
        P("segment", None),
        P("segment", None),
        P("segment", None, None),
        P("segment", None),
        P("segment", None),
        P("segment", None),
        P("segment", None, None),
    )
    out_specs = P("segment", "band", None, None)
    return jax.shard_map(shards, mesh=mesh, in_specs=in_specs, out_specs=out_specs, check_vma=False)
```
